256 devices in a mesh: tile: 16 (over z, core), lev: 4 (over x), tag: 4 (over y).
Axes of the slice: x: 4, y: 4, z: 8, core: 2. Of those that a mesh axis runs over, the one named last changes fastest.
Arguments:
- parent_field: float32 [8, 32, 256, 1024], P('tag', 'lev', 'tile'), may hold values from -6 to 6
- nest_field: float32 [8, 32, 256, 1024], P('tag', 'lev', 'tile'), may hold values from -6 to 6
- parent_mixing: float32 [32, 256, 1024], P('lev', 'tile'), may hold values from 0.05 to 5
- parent_eastward: float32 [256, 1024], P('tile'), may hold values from 0.02 to 0.12
- parent_northward: float32 [256, 1024], P('tile'), may hold values from 0.02 to 0.12
- nest_eastward: float32 [256, 1024], P('tile'), may hold values from 0.02 to 0.12
- nest_northward: float32 [256, 1024], P('tile'), may hold values from 0.02 to 0.12
- strip_tile: int32 [16, 256], replicated, may hold values from 0 to 15, as said below
- strip_block: int32 [16, 256], replicated, may hold values from 0 to 127
- strip_target: int32 [16, 256], replicated, may hold values from 0 to 127
- strip_count: int32 [16], replicated, may hold values from 1 to 256, as said below
Outputs:
- parent_adjoint: float32 [8, 32, 256, 1024], P('tag', 'lev', 'tile')
- nest_adjoint: float32 [8, 32, 256, 1024], P('tag', 'lev', 'tile')
- bulk_adjoint: float32 [32, 256, 1024], P('lev', 'tile', 'tag')
The draws below stay inside these ranges and needn't reach their ends.
Inputs may be any that keep to these rules, and one draw needn't show every extreme that they name: `strip_tile`: among the first strip_count[j] entries of row j, every parent tile appears at most 16 times; in the row whose count is 256 every parent tile appears exactly 16 times. `strip_count`: exactly one nest tile lists 256 strips; every other lists at most 128.
All inputs are finite; a program needn't handle non-finite values.
Results may differ from the reference program's by a relative error of at most 0.0003.
Values sent between devices are 32-bit elements; how exact they have to be, the bound alone decides.
A program may use at most 64 MiB of HBM per device.

```python
import math
import jax
import jax.numpy as jnp
from jax import lax

TAGS = 8
LEVELS = 32
PW = 1024
PROWS = 256
BLOCKS = 128
CAP = 16
NTILES = 16
SMAX = 256
NSUB = 3


def permute(subkey):
    return jax.random.permutation(subkey, SMAX)


def strip_plan(key):
    base_key = jax.random.fold_in(key, 17)
    count_key, busy_key, order_key = jax.random.split(base_key, 3)
    counts = jax.random.randint(count_key, (NTILES,), 1, SMAX // 2 + 1)
    busiest = jax.random.randint(busy_key, (), 0, NTILES)
    counts = jnp.where(jnp.arange(NTILES) == busiest, SMAX, counts).astype(jnp.int32)
    subkeys = jax.random.split(order_key, NTILES)
    orders = jax.vmap(permute)(subkeys)
    tiles = (orders // CAP).astype(jnp.int32)
    return (tiles, counts)


def draw_strip_tile(key, part):
    return strip_plan(key)[0]


def draw_strip_count(key, part):
    return strip_plan(key)[1]


def place_ends(result, stream_key, smallest, top_value):
    shape = result.shape
    place = [jax.random.randint(jax.random.fold_in(stream_key, axis), (), 0, shape[axis]) for axis in range(len(shape))]
    result = result.at[tuple(place)].set(smallest)
    longest = shape.index(max(shape))
    place[longest] = (place[longest] + 1) % shape[longest]
    return result.at[tuple(place)].set(top_value)


def block_scale(stream_key, shape, shards, low, top_value):
    gain = 1.0
    for axis_at, parts in shards:
        heights = jax.random.uniform(jax.random.fold_in(jax.random.fold_in(stream_key, 6), axis_at), (parts,), jnp.float32, low / len(shards), top_value / len(shards))
        gain = gain * jnp.repeat(jnp.exp(heights), shape[axis_at] // parts).reshape((-1,) + (1,) * (len(shape) - 1 - axis_at))
    return gain


def gaussian(rng, extent, scale, bound, cuts=(), kind=jnp.bfloat16):
    result = scale * jax.random.normal(rng, extent, jnp.float32)
    if cuts:
        result = result * block_scale(rng, extent, cuts, -0.22, 0.18)
    return jnp.clip(result, -bound, bound).astype(kind)


def setup_inputs(seed: int = 0) -> dict:
    splits = jax.random.split(jax.random.key(seed), 12)
    return {
        "parent_field": gaussian(splits[0], (TAGS, LEVELS, PROWS, PW), 1.0, 6.0, ((0, 4), (1, 4), (2, 16)), jnp.float32),
        "nest_field": gaussian(splits[1], (TAGS, LEVELS, PROWS, PW), 1.0, 6.0, ((0, 4), (1, 4), (2, 16)), jnp.float32),
        "parent_mixing": jnp.clip(jnp.exp(math.log(5.0) - 4.6051702 * jax.random.uniform(splits[2], (LEVELS, PROWS, PW), jnp.float32) ** block_scale(splits[2], (LEVELS, PROWS, PW), ((0, 4), (1, 16)), -0.2, 0.2)), 0.05, 5.0),
        "parent_eastward": jnp.clip(0.02 + 0.09999999776482582 * jax.random.uniform(splits[3], (PROWS, PW), jnp.float32) ** block_scale(splits[3], (PROWS, PW), ((0, 16),), -0.2, 0.2), 0.02, 0.12),
        "parent_northward": jnp.clip(0.02 + 0.09999999776482582 * jax.random.uniform(splits[4], (PROWS, PW), jnp.float32) ** block_scale(splits[4], (PROWS, PW), ((0, 16),), -0.2, 0.2), 0.02, 0.12),
        "nest_eastward": jnp.clip(0.02 + 0.09999999776482582 * jax.random.uniform(splits[5], (PROWS, PW), jnp.float32) ** block_scale(splits[5], (PROWS, PW), ((0, 16),), -0.2, 0.2), 0.02, 0.12),
        "nest_northward": jnp.clip(0.02 + 0.09999999776482582 * jax.random.uniform(splits[6], (PROWS, PW), jnp.float32) ** block_scale(splits[6], (PROWS, PW), ((0, 16),), -0.2, 0.2), 0.02, 0.12),
        "strip_tile": draw_strip_tile(jax.random.fold_in(splits[11], 71), 0),
        "strip_block": place_ends(jax.random.randint(splits[8], (NTILES, SMAX), 0, BLOCKS), jax.random.fold_in(splits[8], 1), 0, BLOCKS - 1).astype(jnp.int32),
        "strip_target": place_ends(jax.random.randint(splits[9], (NTILES, SMAX), 0, BLOCKS), jax.random.fold_in(splits[9], 1), 0, BLOCKS - 1).astype(jnp.int32),
        "strip_count": draw_strip_count(jax.random.fold_in(splits[11], 71), 0),
    }


def tridiagonal(source, mixing):
    level_count = mixing.shape[0]
    mixing_up = jnp.concatenate([mixing[1:], jnp.zeros_like(mixing[:1])], axis=0)
    diagonal = 1.0 + mixing + mixing_up
    ratio_now = jnp.zeros_like(mixing[0])
    carry_now = jnp.zeros_like(source[:, 0])
    ratios = []
    carries = []
    for lev_index in range(level_count):
        pivot_now = diagonal[lev_index] + mixing[lev_index] * ratio_now
        ratio_now = -mixing_up[lev_index] / pivot_now
        carry_now = (source[:, lev_index] + mixing[lev_index] * carry_now) / pivot_now
        ratios.append(ratio_now)
        carries.append(carry_now)
    value_now = carries[level_count - 1]
    results = [value_now]
    for lev_index in range(level_count - 2, -1, -1):
        value_now = carries[lev_index] - ratios[lev_index] * value_now
        results.append(value_now)
    return jnp.stack(results[::-1], axis=1)


def relax(padded, eastward):
    center = padded[:-1, 1:-1]
    row_above = padded[:-1, :-2]
    row_below = padded[:-1, 2:]
    north_here = padded[-1, 1:-1]
    north_above = padded[-1, :-2]
    zero_column = jnp.zeros_like(center[:, :, :1])
    east_cell = jnp.concatenate([center[:, :, 1:], zero_column], axis=2)
    west_cell = jnp.concatenate([zero_column, center[:, :, :-1]], axis=2)
    west_rate = jnp.concatenate([jnp.zeros_like(eastward[:, :1]), eastward[:, :-1]], axis=1)
    return (center + north_here * (row_below - center) + north_above * (row_above - center)
            + eastward * (east_cell - center) + west_rate * (west_cell - center))


def horizontal(values, eastward, northward):
    tag_count, level_count, row_count, col_count = values.shape
    stacked = jnp.concatenate([values.reshape(tag_count * level_count, row_count, col_count), northward[None]], axis=0)
    padded = jnp.pad(stacked, ((0, 0), (1, 1), (0, 0)))
    return relax(padded, eastward).reshape(tag_count, level_count, row_count, col_count)


def strip_forcing(parent_field, strip_tile, strip_block, strip_target, strip_count):
    tag_count, level_count, row_count, col_count = parent_field.shape
    flat = parent_field.reshape(tag_count, level_count, NTILES * BLOCKS, 128)
    positions = jnp.arange(SMAX, dtype=jnp.int32)

    def one_tile(listing):
        tile_row, block_row, target_row, count_now = listing
        is_live = (positions < count_now).astype(flat.dtype)
        source_index = (tile_row * BLOCKS + block_row).astype(jnp.int32)
        taken = jnp.take(flat, source_index, axis=2) * is_live[None, None, :, None]
        empty = jnp.zeros((tag_count, level_count, BLOCKS, 128), flat.dtype)
        return empty.at[:, :, target_row.astype(jnp.int32), :].add(taken)

    pieces = lax.map(one_tile, (strip_tile, strip_block, strip_target, strip_count))
    return jnp.transpose(pieces, (1, 2, 0, 3, 4)).reshape(tag_count, level_count, row_count, col_count)


def reference(parent_field, nest_field, parent_mixing, parent_eastward, parent_northward, nest_eastward, nest_northward, strip_tile, strip_block, strip_target, strip_count):
    solved = tridiagonal(parent_field, parent_mixing)
    parent_adjoint = horizontal(solved, parent_eastward, parent_northward)
    nest_now = nest_field + strip_forcing(parent_field, strip_tile, strip_block, strip_target, strip_count)
    for sub_step in range(NSUB):
        nest_now = horizontal(nest_now, nest_eastward, nest_northward)
    bulk_adjoint = jnp.sum(parent_adjoint, axis=0)
    return parent_adjoint, nest_now, bulk_adjoint
```

```python
import functools

import jax
import jax.numpy as jnp
from jax import lax
from jax.experimental import pallas as pl
from jax.experimental.pallas import tpu as pltpu
from jax.sharding import PartitionSpec as P

MESH = pl.DeviceIdType.MESH
F32 = jnp.float32
BF16 = jnp.bfloat16
TILES = 16
CHIPS = 8
SLOTS = 16
LINES = 16
LEVELS = 8
ROWS = 16
COLS = 1024
LANES = 128
NBLK = 128
ENTRIES = 256
NSUB = 3
FULL = (112, 80, 48, 16)
USUAL = (64, 48, 40, 16)


def iota(shape, dim):
    return lax.broadcasted_iota(jnp.int32, shape, dim)


def chip_gap(to_tile, from_tile):
    return ((to_tile >> 1) - (from_tile >> 1)) & (CHIPS - 1)


def way_counts(gap, count):
    half = jnp.floor(count * 0.5)
    up = jnp.where((gap >= 1) & (gap <= 3), count, jnp.where(gap == 4, count - half, 0.0))
    down = jnp.where(gap >= 5, count, jnp.where(gap == 4, half, 0.0))
    return up, down


def way_keys(gap, tile):
    side = tile & 1
    return (4 - gap) * 2 + side, (gap - 4) * 2 + side


def counts_column(count_ref):
    row = iota((TILES, ENTRIES), 0)
    total = jnp.zeros((TILES, ENTRIES), jnp.int32)
    for tile in range(TILES):
        total = jnp.where(row == tile, count_ref[tile], total)
    return total


def plan_kernel(tile_ref, count_ref, flag_ref):
    live = iota((TILES, ENTRIES), 1) < counts_column(count_ref)
    listed = jnp.where(live, tile_ref[...], -1)
    nest = iota((TILES, 1), 0)

    def one(source, excess):
        count = jnp.sum(jnp.where(listed == source, 1.0, 0.0), axis=1, keepdims=True)
        gap = chip_gap(nest, source)
        up, down = way_counts(gap, count)
        for hop in range(1, 4):
            for load in (jnp.where(gap >= hop, up, 0.0), jnp.where(8 - gap >= hop, down, 0.0)):
                total = jnp.sum(load, axis=0, keepdims=True)
                excess = jnp.maximum(excess, total - USUAL[hop - 1])
        return excess

    excess = lax.fori_loop(0, TILES, one, jnp.zeros((1, 1), F32))
    flag_ref[0] = (jnp.max(excess) > 0.5).astype(jnp.int32)


def split(value):
    high = value.astype(BF16)
    low = (value - high.astype(F32)).astype(BF16)
    return high, low


def routed(matrix, value):
    high, low = split(value)
    return jnp.dot(matrix, high, preferred_element_type=F32) + jnp.dot(
        matrix, low, preferred_element_type=F32
    )


def onehot_product(left, right):
    return lax.dot_general(left, right, (((1,), (1,)), ((), ())), preferred_element_type=F32)


def blocks_of(ref, line):
    return jnp.concatenate(
        [ref[line, :, LANES * c : LANES * (c + 1)] for c in range(COLS // LANES)], axis=0
    )


def relax(x, top, bottom, coef):
    row = iota((ROWS, COLS), 0)
    above = jnp.where(row == 0, top, pltpu.roll(x, 1, 0))
    below = jnp.where(row == ROWS - 1, bottom, pltpu.roll(x, ROWS - 1, 0))
    west = pltpu.roll(x, 1, 1)
    east = pltpu.roll(x, COLS - 1, 1)
    return coef[0] * x + coef[1] * below + coef[2] * above + coef[3] * east + coef[4] * west


def coefficients(eastward, northward, north_above):
    col = iota(eastward.shape, 1)
    west = jnp.where(col == 0, 0.0, pltpu.roll(eastward, 1, 1))
    east = jnp.where(col == COLS - 1, 0.0, eastward)
    center = 1.0 - northward - north_above - eastward - west
    return center, northward, north_above, east, west


def relax_row(x, above, below, eastward, northward, north_above):
    wide = (LINES, COLS)
    center, north, north_up, east, west = coefficients(
        jnp.broadcast_to(eastward, (8, COLS)),
        jnp.broadcast_to(northward, (8, COLS)),
        jnp.broadcast_to(north_above, (8, COLS)),
    )
    center, north, north_up, east, west = (
        jnp.broadcast_to(v[:1], wide) for v in (center, north, north_up, east, west)
    )
    return (
        center * x
        + north * below
        + north_up * above
        + east * pltpu.roll(x, COLS - 1, 1)
        + west * pltpu.roll(x, 1, 1)
    )


def step_kernel(
    cap,
    parent,
    nest,
    mixing,
    parent_e,
    parent_n,
    nest_e,
    nest_n,
    strip_tile,
    strip_block,
    strip_target,
    strip_count,
    parent_out,
    nest_out,
    bulk_out,
    edges,
    pack_top,
    pack_bottom,
    coef_top,
    coef_bottom,
    slot_of,
    block_of,
    outgoing,
    near_out,
    near_in,
    got1,
    got2,
    got3,
    got4,
    route1,
    route2,
    route3,
    route4,
    route_near,
    route_own,
    solved,
    weight,
    message,
    from_outer,
    from_center,
    from_inner,
    rim_out,
    rim_in,
    parent_coef,
    nest_coef,
    tag_sum,
    tag_in,
    start,
    halo_out,
    halo_in,
    halos,
    send_sem,
    recv_sem,
):
    got = (None, got1, got2, got3, got4)
    route = (None, route1, route2, route3, route4)
    first = cap[0]
    tile = lax.axis_index("tile")
    lev = lax.axis_index("lev")
    tag = lax.axis_index("tag")
    sibling = tile + 1 - 2 * (tile % 2)
    ring = ((tile + 2) % TILES, (tile + TILES - 2) % TILES)
    tile_up = (tile + 1) % TILES
    tile_down = (tile + TILES - 1) % TILES
    mate = lev + 1 - 2 * (lev % 2)
    across = 3 - lev
    outer = lev % 3 == 0
    inner = lev % 3 != 0
    down = lev // 2

    barrier = pltpu.get_barrier_semaphore()
    peers = [{"tile": t} for t in (tile_up, tile_down) + ring]
    peers += [{"lev": (lev + d) % 4} for d in (1, 2, 3)]
    peers += [{"tag": (tag + d) % 4} for d in (1, 2, 3)]
    for peer in peers:
        pl.semaphore_signal(barrier, inc=1, device_id=peer, device_id_type=MESH)

    used = [0]
    pending = []

    def remote(src, dst, device, guard=None):
        at = used[0]
        used[0] += 1
        copy = pltpu.make_async_remote_copy(
            src_ref=src,
            dst_ref=dst,
            send_sem=send_sem.at[at],
            recv_sem=recv_sem.at[at],
            device_id=device,
            device_id_type=MESH,
        )
        pending.append((copy, guard))
        return copy

    pack_bottom[0:3] = nest_e[ROWS - 3 : ROWS]
    pack_bottom[3:6] = nest_n[ROWS - 3 : ROWS]
    pack_bottom[6:7] = parent_n[ROWS - 1 : ROWS]
    pack_bottom[7:8] = parent_n[ROWS - 1 : ROWS]
    pack_top[0:3] = nest_e[0:3]
    pack_top[3:6] = nest_n[0:3]
    pack_top[6:8] = parent_n[0:2]
    edges[0:LEVELS] = mixing[...]

    has_above = tile > 0
    has_below = tile < TILES - 1

    row = iota((TILES, ENTRIES), 0)
    entry = iota((TILES, ENTRIES), 1)
    live = entry < counts_column(strip_count)
    listed = jnp.where(live, strip_tile[...], -1)
    mine = jnp.where(listed == tile, 1.0, 0.0)
    upto = jnp.where(
        iota((ENTRIES, ENTRIES), 0) <= iota((ENTRIES, ENTRIES), 1), 1.0, 0.0
    ).astype(BF16)
    rank = jnp.dot(mine.astype(BF16), upto, preferred_element_type=F32) - 1.0
    count = jnp.broadcast_to(jnp.sum(mine, axis=1, keepdims=True), (TILES, ENTRIES))
    gap = chip_gap(row, tile)
    up_count, down_count = way_counts(gap, count)
    up_key, down_key = way_keys(gap, row)
    up_at = jnp.zeros((TILES, ENTRIES), F32)
    down_at = jnp.zeros((TILES, ENTRIES), F32)
    for other in range(TILES):
        up_at += jnp.where(up_key[other : other + 1] < up_key, up_count[other : other + 1], 0.0)
        down_at += jnp.where(
            down_key[other : other + 1] < down_key, down_count[other : other + 1], 0.0
        )
    half = jnp.floor(rank * 0.5)
    odd = rank - 2.0 * half
    goes_up = ((gap >= 1) & (gap <= 3)) | ((gap == 4) & (odd < 0.5))
    goes_down = (gap >= 5) | ((gap == 4) & (odd > 0.5))
    in_row = jnp.where(gap == 4, half, rank)
    slot = jnp.where(
        goes_up,
        up_at + in_row,
        jnp.where(
            goes_down,
            first + down_at + in_row,
            jnp.where((gap == 0) & (row != tile), 2 * first + rank, -1.0),
        ),
    )
    slot_of[...] = jnp.where(mine > 0.5, slot, -1.0)
    blocks = strip_block[...]
    block_of[...] = ((blocks & 7) * ROWS + (blocks >> 3) + 1).astype(F32)

    def gather_matrix(begin, size):
        wanted = (iota((size, ENTRIES), 0) + begin).astype(F32)

        def one(nest_tile, total):
            at = pl.ds(nest_tile, 1)
            return total + jnp.where(slot_of[at, :] == wanted, block_of[at, :], 0.0)

        total = lax.fori_loop(0, TILES, one, jnp.zeros((size, ENTRIES), F32))
        index = jnp.sum(total, axis=1, keepdims=True) - 1.0
        return jnp.where(index == iota((size, NBLK), 1).astype(F32), 1.0, 0.0).astype(BF16)

    gather = jnp.concatenate(
        [gather_matrix(0, first), gather_matrix(first, first), gather_matrix(2 * first, SLOTS)],
        axis=0,
    )

    def pack(pair, _):
        cells = jnp.concatenate([blocks_of(parent, 2 * pair), blocks_of(parent, 2 * pair + 1)], axis=1)
        taken = routed(gather, cells)
        for side in range(2):
            lanes = slice(LANES * side, LANES * (side + 1))
            outgoing[0, 2 * pair + side] = taken[:first, lanes]
            outgoing[1, 2 * pair + side] = taken[first : 2 * first, lanes]
            near_out[2 * pair + side] = taken[2 * first :, lanes]
        return 0

    lax.fori_loop(0, LINES // 2, pack, 0)

    pl.semaphore_wait(barrier, len(peers))

    edge_copy = remote(edges.at[0], edges.at[LEVELS], {"lev": (lev + 3) % 4}, lev > 0)
    pl.when(lev > 0)(edge_copy.start)
    pack_down_copy = remote(pack_bottom, coef_top, {"tile": tile_up}, has_below)
    pl.when(has_below)(pack_down_copy.start)
    pack_up_copy = remote(pack_top, coef_bottom, {"tile": tile_down}, has_above)
    pl.when(has_above)(pack_up_copy.start)

    near_copy = remote(near_out, near_in, {"tile": sibling})
    near_copy.start()
    cuts = (0, cap[3], cap[2], cap[1], cap[0])
    hop_copy = {}
    for hop in range(1, 5):
        for piece in range(5 - hop):
            for way in range(2):
                part = pl.ds(cuts[piece], cuts[piece + 1] - cuts[piece])
                src = outgoing if hop == 1 else got[hop - 1]
                hop_copy[hop, piece, way] = remote(
                    src.at[way, :, part, :], got[hop].at[way, :, part, :], {"tile": ring[way]}
                )
    side_copy = {}
    for hop in range(1, 5):
        for way in range(2):
            side_copy[hop, way] = remote(got[hop].at[way], got[hop].at[2 + way], {"tile": sibling})
    for piece in range(4):
        for way in range(2):
            hop_copy[1, piece, way].start()

    def relay(hop, piece):
        for way in range(2):
            hop_copy[hop - 1, piece, way].wait_recv()
            hop_copy[hop, piece, way].start()

    def share(hop):
        for way in range(2):
            hop_copy[hop, 4 - hop, way].wait_recv()
            side_copy[hop, way].start()

    pl.when(lev < 3)(edge_copy.wait_recv)

    @pl.when(lev == 3)
    def _():
        edges[LEVELS] = jnp.zeros((ROWS, COLS), F32)

    def level(step):
        return step + down * (LEVELS - 1 - 2 * step)

    def field(which, at, rows):
        return parent[which * LEVELS + at, rows, :]

    def sweep(rows, pivot, value0, value1):
        for step in range(LEVELS):
            at = level(step)
            edge = edges[at + 1 - down, rows, :]
            inverse = 1.0 / (pivot + edge)
            ratio = edge * inverse
            carry0 = value0 * inverse
            carry1 = value1 * inverse
            solved[at, rows, :] = carry0
            solved[LEVELS + at, rows, :] = carry1
            weight[at, rows, :] = ratio
            if step < LEVELS - 1:
                follow = level(step + 1)
                pivot = 1.0 + ratio * pivot
                value0 = field(0, follow, rows) + edge * carry0
                value1 = field(1, follow, rows) + edge * carry1
        message[0, rows, :] = pivot
        message[1, rows, :] = value0
        message[2, rows, :] = value1

    def back(rows, value0, value1, last):
        for step in range(last, -1, -1):
            at = level(step)
            ratio = weight[at, rows, :]
            value0 = solved[at, rows, :] + ratio * value0
            value1 = solved[LEVELS + at, rows, :] + ratio * value1
            solved[at, rows, :] = value0
            solved[LEVELS + at, rows, :] = value1

    halves = [pl.ds(0, 8), pl.ds(8, 8)]
    near_level = level(0)
    outer_copy = [
        remote(message.at[:, rows, :], from_outer.at[:, rows, :], {"lev": mate}, outer)
        for rows in halves
    ]
    center_copy = [
        remote(message.at[:, rows, :], from_center.at[:, rows, :], {"lev": across}, inner)
        for rows in halves
    ]
    inner_copy = [
        [
            remote(
                solved.at[which * LEVELS + near_level, rows, :],
                from_inner.at[which, rows, :],
                {"lev": mate},
                inner,
            )
            for which in range(2)
        ]
        for rows in halves
    ]

    @pl.when(outer)
    def _():
        for part, rows in enumerate(halves):
            at = level(0)
            sweep(rows, 1.0 + edges[at + down, rows, :], field(0, at, rows), field(1, at, rows))
            outer_copy[part].start()

    own_tiles = strip_tile[pl.ds(tile, 1), :]
    own_live = iota((1, ENTRIES), 1) < strip_count[tile]
    own_tiles = jnp.where(own_live, own_tiles, -1)
    source_row = iota((TILES, ENTRIES), 0)
    from_source = jnp.where(own_tiles == source_row, 1.0, 0.0)
    own_rank = jnp.sum(
        from_source
        * (jnp.dot(from_source.astype(BF16), upto, preferred_element_type=F32) - 1.0),
        axis=0,
        keepdims=True,
    )
    nest_column = iota((TILES, 1), 0)

    def offsets(source, totals):
        up_total, down_total = totals
        count = jnp.sum(jnp.where(listed == source, 1.0, 0.0), axis=1, keepdims=True)
        gap = chip_gap(nest_column, source)
        up, down_ = way_counts(gap, count)
        up_key, down_key = way_keys(gap, nest_column)
        own_up, own_down = way_keys(chip_gap(tile, source), tile)
        up_here = jnp.sum(jnp.where(up_key < own_up, up, 0.0), axis=0, keepdims=True)
        down_here = jnp.sum(jnp.where(down_key < own_down, down_, 0.0), axis=0, keepdims=True)
        here = own_tiles == source
        return (
            up_total + jnp.where(here, up_here, 0.0),
            down_total + jnp.where(here, down_here, 0.0),
        )

    nothing = jnp.zeros((1, ENTRIES), F32)
    up_start, down_start = lax.fori_loop(0, TILES, offsets, (nothing, nothing))
    own_gap = jnp.where(own_tiles >= 0, chip_gap(tile, own_tiles), -1)
    own_half = jnp.floor(own_rank * 0.5)
    own_odd = own_rank - 2.0 * own_half
    comes_up = ((own_gap >= 1) & (own_gap <= 3)) | ((own_gap == 4) & (own_odd < 0.5))
    place = jnp.where(own_gap == 4, own_half, own_rank) + jnp.where(comes_up, up_start, down_start)
    hops = jnp.where(own_gap >= 1, jnp.where(comes_up, own_gap, CHIPS - own_gap), 0)
    group = jnp.where((own_tiles & 1) == (tile & 1), 0.0, 2.0) + jnp.where(comes_up, 0.0, 1.0)
    targets = strip_target[pl.ds(tile, 1), :]
    targets = jnp.where(own_tiles >= 0, (targets & 7) * ROWS + (targets >> 3), -1)
    lands = jnp.where(targets == iota((NBLK, ENTRIES), 0), 1.0, 0.0).astype(BF16)

    def picks(place, rows):
        return jnp.where(place == iota((rows, ENTRIES), 0).astype(F32), 1.0, 0.0).astype(BF16)

    for hop in range(1, 5):
        size = cap[hop - 1]
        at = jnp.where(hops == hop, group * size + place, -1.0)
        route[hop][...] = onehot_product(lands, picks(at, 4 * size)).astype(BF16)
    at = jnp.where((own_gap == 0) & (own_tiles != tile), own_rank, -1.0)
    route_near[...] = onehot_product(lands, picks(at, SLOTS)).astype(BF16)
    own_blocks = strip_block[pl.ds(tile, 1), :]
    own_blocks = jnp.where(own_tiles == tile, (own_blocks & 7) * ROWS + (own_blocks >> 3), -1)
    route_own[...] = onehot_product(lands, picks(own_blocks.astype(F32), NBLK)).astype(BF16)

    @pl.when(inner)
    def _():
        for part, rows in enumerate(halves):
            at = level(0)
            outer_copy[part].wait_recv()
            edge = edges[at + down, rows, :]
            pivot = from_outer[0, rows, :]
            ratio = edge / (pivot + edge)
            sweep(
                rows,
                1.0 + ratio * pivot,
                field(0, at, rows) + ratio * from_outer[1, rows, :],
                field(1, at, rows) + ratio * from_outer[2, rows, :],
            )
            center_copy[part].start()

    relay(2, 0)
    relay(2, 1)

    @pl.when(inner)
    def _():
        for part, rows in enumerate(halves):
            center_copy[part].wait_recv()
            at = level(LEVELS - 1)
            edge = edges[at + 1 - down, rows, :]
            pivot = from_center[0, rows, :]
            ratio = edge / (pivot + edge)
            inverse = 1.0 / (message[0, rows, :] + ratio * pivot)
            value0 = (message[1, rows, :] + ratio * from_center[1, rows, :]) * inverse
            value1 = (message[2, rows, :] + ratio * from_center[2, rows, :]) * inverse
            solved[at, rows, :] = value0
            solved[LEVELS + at, rows, :] = value1
            back(rows, value0, value1, LEVELS - 2)
            for copy in inner_copy[part]:
                copy.start()

    @pl.when(has_above)
    def _():
        pack_down_copy.wait_recv()

    @pl.when(has_below)
    def _():
        pack_up_copy.wait_recv()

    @pl.when(tile == 0)
    def _():
        coef_top[...] = jnp.zeros((8, COLS), F32)

    @pl.when(tile == TILES - 1)
    def _():
        coef_bottom[...] = jnp.zeros((8, COLS), F32)

    cell_row = iota((ROWS, COLS), 0)
    for target, e_ref, n_ref, above in (
        (parent_coef, parent_e, parent_n, coef_top[6:7]),
        (nest_coef, nest_e, nest_n, coef_top[5:6]),
    ):
        northward = n_ref[...]
        north_above = jnp.where(cell_row == 0, above, pltpu.roll(northward, 1, 0))
        for which, value in enumerate(coefficients(e_ref[...], northward, north_above)):
            target[which] = value

    relay(2, 2)

    @pl.when(outer)
    def _():
        for part, rows in enumerate(halves):
            for copy in inner_copy[part]:
                copy.wait_recv()
            back(rows, from_inner[0, rows, :], from_inner[1, rows, :], LEVELS - 1)

    for line in range(LINES):
        rim_out[0, line : line + 1] = solved[line, 0:1, :]
        rim_out[1, line : line + 1] = solved[line, ROWS - 1 : ROWS, :]
    rim_up = remote(rim_out.at[0], rim_in.at[1], {"tile": tile_down}, has_above)
    rim_down = remote(rim_out.at[1], rim_in.at[0], {"tile": tile_up}, has_below)
    pl.when(has_above)(rim_up.start)
    pl.when(has_below)(rim_down.start)

    share(1)

    near_copy.wait_recv()

    def add_blocks(line, taken):
        for c in range(COLS // LANES):
            start[line, :, LANES * c : LANES * (c + 1)] += taken[ROWS * c : ROWS * (c + 1)]

    def scatter_near(pair, _):
        cells = jnp.concatenate([blocks_of(parent, 2 * pair), blocks_of(parent, 2 * pair + 1)], axis=1)
        near = jnp.concatenate([near_in[2 * pair], near_in[2 * pair + 1]], axis=1)
        taken = routed(route_own[...], cells) + routed(route_near[...], near)
        for side in range(2):
            line = 2 * pair + side
            start[line] = nest[line]
            add_blocks(line, taken[:, LANES * side : LANES * (side + 1)])
        return 0

    lax.fori_loop(0, LINES // 2, scatter_near, 0)

    def scatter(hop):
        for way in range(2):
            side_copy[hop, way].wait_recv()

        def one(pair, _):
            cells = jnp.concatenate(
                [
                    jnp.concatenate([got[hop][g, 2 * pair + side] for g in range(4)], axis=0)
                    for side in range(2)
                ],
                axis=1,
            )
            taken = routed(route[hop][...], cells)
            for side in range(2):
                add_blocks(2 * pair + side, taken[:, LANES * side : LANES * (side + 1)])
            return 0

        lax.fori_loop(0, LINES // 2, one, 0)

    relay(3, 0)
    relay(3, 1)

    pl.when(has_above)(rim_down.wait_recv)
    pl.when(has_below)(rim_up.wait_recv)

    @pl.when(tile == 0)
    def _():
        rim_in[0] = jnp.zeros((LINES, COLS), F32)

    @pl.when(tile == TILES - 1)
    def _():
        rim_in[1] = jnp.zeros((LINES, COLS), F32)

    def parent_level(at, _):
        total = None
        for which in range(2):
            line = which * LEVELS + at
            result = relax(
                solved[line], rim_in[0, pl.ds(line, 1), :], rim_in[1, pl.ds(line, 1), :], parent_coef
            )
            parent_out[line] = result
            total = result if total is None else total + result
        tag_sum[at] = total
        return 0

    lax.fori_loop(0, LEVELS, parent_level, 0)

    quarter = COLS // 4

    def columns(which):
        return pl.ds(pl.multiple_of(which * quarter, quarter), quarter)

    tag_copy = []
    for d in (1, 2, 3):
        to = (tag + d) % 4
        copy = remote(tag_sum.at[:, :, columns(to)], tag_in.at[d - 1], {"tag": to})
        copy.start()
        tag_copy.append(copy)

    share(2)
    scatter(1)
    relay(4, 0)
    share(3)
    scatter(2)
    for copy in tag_copy:
        copy.wait_recv()
    bulk_out[...] = tag_sum[:, :, columns(tag)] + tag_in[0] + tag_in[1] + tag_in[2]
    share(4)
    scatter(3)
    scatter(4)

    for line in range(LINES):
        for r in range(NSUB):
            halo_out[0, r, line : line + 1] = start[line, r : r + 1, :]
            at = ROWS - NSUB + r
            halo_out[1, r, line : line + 1] = start[line, at : at + 1, :]
    halo_up = remote(halo_out.at[0], halo_in.at[1], {"tile": tile_down}, has_above)
    halo_down = remote(halo_out.at[1], halo_in.at[0], {"tile": tile_up}, has_below)
    pl.when(has_above)(halo_up.start)
    pl.when(has_below)(halo_down.start)
    pl.when(has_above)(halo_down.wait_recv)
    pl.when(has_below)(halo_up.wait_recv)

    @pl.when(tile == 0)
    def _():
        halo_in[0] = jnp.zeros((NSUB, LINES, COLS), F32)

    @pl.when(tile == TILES - 1)
    def _():
        halo_in[1] = jnp.zeros((NSUB, LINES, COLS), F32)

    in_grid = jnp.where(has_below, 1.0, 0.0)

    def e_top(r):
        return coef_top[r : r + 1]

    def n_top(r):
        return coef_top[3 + r : 4 + r]

    def e_bottom(r):
        return coef_bottom[r : r + 1]

    def n_bottom(r):
        return coef_bottom[3 + r : 4 + r]

    def own(ref, r):
        return ref[r : r + 1]

    second = relax_row(halo_in[0, 1], halo_in[0, 0], halo_in[0, 2], e_top(1), n_top(1), n_top(0))
    third = relax_row(halo_in[0, 2], halo_in[0, 1], halo_out[0, 0], e_top(2), n_top(2), n_top(1))
    edge_row = relax_row(
        halo_out[0, 0], halo_in[0, 2], halo_out[0, 1], own(nest_e, 0), own(nest_n, 0), n_top(2)
    )
    halos[0, 0] = halo_in[0, 2]
    halos[0, 1] = third
    halos[0, 2] = relax_row(third, second, edge_row, e_top(2), n_top(2), n_top(1))
    last = ROWS - 1
    second = relax_row(
        halo_in[1, 1], halo_in[1, 0], halo_in[1, 2], e_bottom(1), n_bottom(1), n_bottom(0)
    )
    third = in_grid * relax_row(
        halo_in[1, 0], halo_out[1, 2], halo_in[1, 1], e_bottom(0), n_bottom(0), own(nest_n, last)
    )
    edge_row = relax_row(
        halo_out[1, 2],
        halo_out[1, 1],
        halo_in[1, 0],
        own(nest_e, last),
        own(nest_n, last),
        own(nest_n, last - 1),
    )
    halos[1, 0] = halo_in[1, 0]
    halos[1, 1] = third
    halos[1, 2] = in_grid * relax_row(
        third, edge_row, second, e_bottom(0), n_bottom(0), own(nest_n, last)
    )

    def nest_line(line, _):
        value = start[line]
        for step in range(NSUB):
            value = relax(
                value, halos[0, step, pl.ds(line, 1), :], halos[1, step, pl.ds(line, 1), :], nest_coef
            )
        nest_out[line] = value
        return 0

    lax.fori_loop(0, LINES, nest_line, 0)

    for copy, guard in pending:
        if guard is None:
            copy.wait_send()
        else:
            pl.when(guard)(copy.wait_send)


VMEM = pl.BlockSpec(memory_space=pltpu.VMEM)
SMEM = pl.BlockSpec(memory_space=pltpu.SMEM)


def step_call(cap, collective, arrays):
    first = cap[0]
    grid = (LINES, ROWS, COLS)
    copies = 3 + 1 + 20 + 8 + 2 + 2 + 4 + 2 + 3 + 2
    shapes = [
        pltpu.VMEM((LEVELS + 1, ROWS, COLS), F32),
        pltpu.VMEM((8, COLS), F32),
        pltpu.VMEM((8, COLS), F32),
        pltpu.VMEM((8, COLS), F32),
        pltpu.VMEM((8, COLS), F32),
        pltpu.VMEM((TILES, ENTRIES), F32),
        pltpu.VMEM((TILES, ENTRIES), F32),
        pltpu.VMEM((2, LINES, first, LANES), F32),
        pltpu.VMEM((LINES, SLOTS, LANES), F32),
        pltpu.VMEM((LINES, SLOTS, LANES), F32),
    ]
    shapes += [pltpu.VMEM((4, LINES, size, LANES), F32) for size in cap]
    shapes += [pltpu.VMEM((NBLK, 4 * size), BF16) for size in cap]
    shapes += [
        pltpu.VMEM((NBLK, SLOTS), BF16),
        pltpu.VMEM((NBLK, NBLK), BF16),
        pltpu.VMEM(grid, F32),
        pltpu.VMEM((LEVELS, ROWS, COLS), F32),
        pltpu.VMEM((3, ROWS, COLS), F32),
        pltpu.VMEM((3, ROWS, COLS), F32),
        pltpu.VMEM((3, ROWS, COLS), F32),
        pltpu.VMEM((2, ROWS, COLS), F32),
        pltpu.VMEM((2, LINES, COLS), F32),
        pltpu.VMEM((2, LINES, COLS), F32),
        pltpu.VMEM((5, ROWS, COLS), F32),
        pltpu.VMEM((5, ROWS, COLS), F32),
        pltpu.VMEM((LEVELS, ROWS, COLS), F32),
        pltpu.VMEM((3, LEVELS, ROWS, COLS // 4), F32),
        pltpu.VMEM(grid, F32),
        pltpu.VMEM((2, NSUB, LINES, COLS), F32),
        pltpu.VMEM((2, NSUB, LINES, COLS), F32),
        pltpu.VMEM((2, NSUB, LINES, COLS), F32),
        pltpu.SemaphoreType.DMA((copies,)),
        pltpu.SemaphoreType.DMA((copies,)),
    ]
    return pl.pallas_call(
        functools.partial(step_kernel, cap),
        out_shape=[
            jax.ShapeDtypeStruct(grid, F32),
            jax.ShapeDtypeStruct(grid, F32),
            jax.ShapeDtypeStruct((LEVELS, ROWS, COLS // 4), F32),
        ],
        in_specs=[VMEM] * 10 + [SMEM],
        out_specs=[VMEM] * 3,
        scratch_shapes=shapes,
        compiler_params=pltpu.CompilerParams(
            collective_id=collective, has_side_effects=True, vmem_limit_bytes=56 * 1024 * 1024
        ),
    )(*arrays)


def shards(
    parent_field,
    nest_field,
    parent_mixing,
    parent_eastward,
    parent_northward,
    nest_eastward,
    nest_northward,
    strip_tile,
    strip_block,
    strip_target,
    strip_count,
):
    full_shape = parent_field.shape
    grid = (LINES, ROWS, COLS)
    arrays = (
        parent_field.reshape(grid),
        nest_field.reshape(grid),
        parent_mixing,
        parent_eastward,
        parent_northward,
        nest_eastward,
        nest_northward,
        strip_tile,
        strip_block,
        strip_target,
        strip_count,
    )
    flag = pl.pallas_call(
        plan_kernel,
        out_shape=jax.ShapeDtypeStruct((1,), jnp.int32),
        in_specs=[VMEM, SMEM],
        out_specs=SMEM,
    )(strip_tile, strip_count)
    parent_adjoint, nest_adjoint, bulk_adjoint = lax.cond(
        flag[0] > 0,
        lambda *a: step_call(FULL, 1, a),
        lambda *a: step_call(USUAL, 2, a),
        *arrays,
    )
    return parent_adjoint.reshape(full_shape), nest_adjoint.reshape(full_shape), bulk_adjoint


def solution(mesh):
    in_specs = (
        P("tag", "lev", "tile", None),
        P("tag", "lev", "tile", None),
        P("lev", "tile", None),
        P("tile", None),
        P("tile", None),
        P("tile", None),
        P("tile", None),
        P(),
        P(),
        P(),
        P(),
    )
    out_specs = (
        P("tag", "lev", "tile", None),
        P("tag", "lev", "tile", None),
        P("lev", "tile", "tag"),
    )
    return jax.shard_map(shards, mesh=mesh, in_specs=in_specs, out_specs=out_specs, check_vma=False)
```

```python
import functools

import jax
import jax.numpy as jnp
from jax import lax
from jax.experimental import pallas as pl
from jax.experimental.pallas import tpu as pltpu
from jax.sharding import PartitionSpec as P

MESH = pl.DeviceIdType.MESH
F32 = jnp.float32
BF16 = jnp.bfloat16
TILES = 16
CHIPS = 8
SLOTS = 16
LINES = 16
LEVELS = 8
ROWS = 16
COLS = 1024
LANES = 128
NBLK = 128
ENTRIES = 256
NSUB = 3
FULL = (112, 80, 48, 16)
USUAL = (64, 48, 40, 16)
SMALL = (56, 40, 32, 16)


def iota(shape, dim):
    return lax.broadcasted_iota(jnp.int32, shape, dim)


def chip_gap(to_tile, from_tile):
    return ((to_tile >> 1) - (from_tile >> 1)) & (CHIPS - 1)


def way_counts(gap, count):
    half = jnp.floor(count * 0.5)
    up = jnp.where((gap >= 1) & (gap <= 3), count, jnp.where(gap == 4, count - half, 0.0))
    down = jnp.where(gap >= 5, count, jnp.where(gap == 4, half, 0.0))
    return up, down


def way_keys(gap, tile):
    side = tile & 1
    return (4 - gap) * 2 + side, (gap - 4) * 2 + side


def counts_column(count_ref):
    row = iota((TILES, ENTRIES), 0)
    total = jnp.zeros((TILES, ENTRIES), jnp.int32)
    for tile in range(TILES):
        total = jnp.where(row == tile, count_ref[tile], total)
    return total


def plan_kernel(tile_ref, count_ref, flag_ref):
    live = iota((TILES, ENTRIES), 1) < counts_column(count_ref)
    listed = jnp.where(live, tile_ref[...], -1)
    lane = iota((TILES, LANES), 1)
    count = jnp.zeros((TILES, LANES), F32)
    for source in range(TILES):
        total = jnp.sum(jnp.where(listed == source, 1.0, 0.0), axis=1, keepdims=True)
        count = jnp.where(lane == source, total, count)
    gap = chip_gap(iota((TILES, LANES), 0), lane)
    up, down = way_counts(gap, count)
    small = jnp.zeros((1, LANES), F32)
    usual = jnp.zeros((1, LANES), F32)
    for hop in range(1, 4):
        for load in (jnp.where(gap >= hop, up, 0.0), jnp.where(CHIPS - gap >= hop, down, 0.0)):
            total = jnp.sum(load, axis=0, keepdims=True)
            small = jnp.maximum(small, total - SMALL[hop - 1])
            usual = jnp.maximum(usual, total - USUAL[hop - 1])
    over = jnp.where(small > 0.5, 1.0, 0.0) + jnp.where(usual > 0.5, 1.0, 0.0)
    flag_ref[0] = jnp.max(over).astype(jnp.int32)


def split(value):
    high = value.astype(BF16)
    low = (value - high.astype(F32)).astype(BF16)
    return high, low


def routed(matrix, value):
    high, low = split(value)
    return jnp.dot(matrix, high, preferred_element_type=F32) + jnp.dot(
        matrix, low, preferred_element_type=F32
    )


def onehot_product(left, right):
    return lax.dot_general(left, right, (((1,), (1,)), ((), ())), preferred_element_type=F32)


def blocks_of(ref, line):
    return jnp.concatenate(
        [ref[line, :, LANES * c : LANES * (c + 1)] for c in range(COLS // LANES)], axis=0
    )


def relax(halves, top, bottom, coef):
    row = iota((8, COLS), 0)
    later = [pltpu.roll(x, 1, 0) for x in halves]
    sooner = [pltpu.roll(x, 7, 0) for x in halves]
    above = (jnp.where(row == 0, top, later[0]), jnp.where(row == 0, later[0], later[1]))
    below = (jnp.where(row == 7, sooner[1], sooner[0]), jnp.where(row == 7, bottom, sooner[1]))
    results = []
    for part in range(2):
        x = halves[part]
        rows = slice(8 * part, 8 * part + 8)
        results.append(
            coef[0, rows] * x
            + coef[1, rows] * below[part]
            + coef[2, rows] * above[part]
            + coef[3, rows] * pltpu.roll(x, COLS - 1, 1)
            + coef[4, rows] * pltpu.roll(x, 1, 1)
        )
    return results


def halves_of(ref, line):
    return [ref[line, 0:8, :], ref[line, 8:16, :]]


def coefficients(eastward, northward, north_above):
    col = iota(eastward.shape, 1)
    west = jnp.where(col == 0, 0.0, pltpu.roll(eastward, 1, 1))
    east = jnp.where(col == COLS - 1, 0.0, eastward)
    center = 1.0 - northward - north_above - eastward - west
    return center, northward, north_above, east, west


def relax_row(x, above, below, eastward, northward, north_above):
    wide = (LINES, COLS)
    center, north, north_up, east, west = coefficients(
        jnp.broadcast_to(eastward, (8, COLS)),
        jnp.broadcast_to(northward, (8, COLS)),
        jnp.broadcast_to(north_above, (8, COLS)),
    )
    center, north, north_up, east, west = (
        jnp.broadcast_to(v[:1], wide) for v in (center, north, north_up, east, west)
    )
    return (
        center * x
        + north * below
        + north_up * above
        + east * pltpu.roll(x, COLS - 1, 1)
        + west * pltpu.roll(x, 1, 1)
    )


def step_kernel(
    cap,
    parent_hbm,
    nest_hbm,
    mixing_hbm,
    parent_e,
    parent_n,
    nest_e,
    nest_n,
    strip_tile,
    strip_block,
    strip_target,
    strip_count,
    start,
    halos,
    nest_coef,
    parent_out,
    bulk_out,
    parent,
    nest,
    mixing,
    edges,
    pack_top,
    pack_bottom,
    coef_top,
    coef_bottom,
    slot_of,
    block_of,
    outgoing,
    near_out,
    near_in,
    got1,
    got2,
    got3,
    got4,
    route1,
    route2,
    route3,
    route4,
    route_near,
    route_own,
    solved,
    weight,
    message,
    from_outer,
    from_center,
    from_inner,
    rim_out,
    rim_in,
    parent_coef,
    tag_sum,
    tag_in,
    halo_out,
    halo_in,
    send_sem,
    recv_sem,
    load_sem,
):
    loads = [
        pltpu.make_async_copy(src, dst, load_sem.at[at])
        for at, (src, dst) in enumerate(
            ((parent_hbm, parent), (mixing_hbm, mixing), (nest_hbm, nest))
        )
    ]
    for copy in loads:
        copy.start()
    got = (None, got1, got2, got3, got4)
    route = (None, route1, route2, route3, route4)
    first = cap[0]
    tile = lax.axis_index("tile")
    lev = lax.axis_index("lev")
    tag = lax.axis_index("tag")
    sibling = tile + 1 - 2 * (tile % 2)
    ring = ((tile + 2) % TILES, (tile + TILES - 2) % TILES)
    tile_up = (tile + 1) % TILES
    tile_down = (tile + TILES - 1) % TILES
    mate = lev + 1 - 2 * (lev % 2)
    across = 3 - lev
    outer = lev % 3 == 0
    inner = lev % 3 != 0
    down = lev // 2

    barrier = pltpu.get_barrier_semaphore()
    peers = [{"tile": t} for t in (tile_up, tile_down) + ring]
    peers += [{"lev": (lev + d) % 4} for d in (1, 2, 3)]
    peers += [{"tag": (tag + d) % 4} for d in (1, 2, 3)]
    for peer in peers:
        pl.semaphore_signal(barrier, inc=1, device_id=peer, device_id_type=MESH)

    used = [0]
    pending = []

    def remote(src, dst, device, guard=None):
        at = used[0]
        used[0] += 1
        copy = pltpu.make_async_remote_copy(
            src_ref=src,
            dst_ref=dst,
            send_sem=send_sem.at[at],
            recv_sem=recv_sem.at[at],
            device_id=device,
            device_id_type=MESH,
        )
        pending.append((copy, guard))
        return copy

    pack_bottom[0:3] = nest_e[ROWS - 3 : ROWS]
    pack_bottom[3:6] = nest_n[ROWS - 3 : ROWS]
    pack_bottom[6:7] = parent_n[ROWS - 1 : ROWS]
    pack_bottom[7:8] = parent_n[ROWS - 1 : ROWS]
    pack_top[0:3] = nest_e[0:3]
    pack_top[3:6] = nest_n[0:3]
    pack_top[6:8] = parent_n[0:2]
    has_above = tile > 0
    has_below = tile < TILES - 1

    row = iota((TILES, ENTRIES), 0)
    entry = iota((TILES, ENTRIES), 1)
    live = entry < counts_column(strip_count)
    listed = jnp.where(live, strip_tile[...], -1)
    mine = jnp.where(listed == tile, 1.0, 0.0)
    upto = jnp.where(
        iota((ENTRIES, ENTRIES), 0) <= iota((ENTRIES, ENTRIES), 1), 1.0, 0.0
    ).astype(BF16)
    rank = jnp.dot(mine.astype(BF16), upto, preferred_element_type=F32) - 1.0
    count = jnp.broadcast_to(jnp.sum(mine, axis=1, keepdims=True), (TILES, ENTRIES))
    gap = chip_gap(row, tile)
    up_count, down_count = way_counts(gap, count)
    up_key, down_key = way_keys(gap, row)
    up_at = jnp.zeros((TILES, ENTRIES), F32)
    down_at = jnp.zeros((TILES, ENTRIES), F32)
    for other in range(TILES):
        up_at += jnp.where(up_key[other : other + 1] < up_key, up_count[other : other + 1], 0.0)
        down_at += jnp.where(
            down_key[other : other + 1] < down_key, down_count[other : other + 1], 0.0
        )
    half = jnp.floor(rank * 0.5)
    odd = rank - 2.0 * half
    goes_up = ((gap >= 1) & (gap <= 3)) | ((gap == 4) & (odd < 0.5))
    goes_down = (gap >= 5) | ((gap == 4) & (odd > 0.5))
    in_row = jnp.where(gap == 4, half, rank)
    slot = jnp.where(
        goes_up,
        up_at + in_row,
        jnp.where(
            goes_down,
            first + down_at + in_row,
            jnp.where((gap == 0) & (row != tile), 2 * first + rank, -1.0),
        ),
    )
    slot_of[...] = jnp.where(mine > 0.5, slot, -1.0)
    blocks = strip_block[...]
    block_of[...] = ((blocks & 7) * ROWS + (blocks >> 3) + 1).astype(F32)

    def gather_matrix(begin, size):
        wanted = (iota((size, ENTRIES), 0) + begin).astype(F32)

        def one(nest_tile, total):
            at = pl.ds(nest_tile, 1)
            return total + jnp.where(slot_of[at, :] == wanted, block_of[at, :], 0.0)

        total = lax.fori_loop(0, TILES, one, jnp.zeros((size, ENTRIES), F32))
        index = jnp.sum(total, axis=1, keepdims=True) - 1.0
        return jnp.where(index == iota((size, NBLK), 1).astype(F32), 1.0, 0.0).astype(BF16)

    gather = jnp.concatenate(
        [gather_matrix(0, first), gather_matrix(first, first), gather_matrix(2 * first, SLOTS)],
        axis=0,
    )

    def pack(pair, _):
        cells = jnp.concatenate([blocks_of(parent, 2 * pair), blocks_of(parent, 2 * pair + 1)], axis=1)
        taken = routed(gather, cells)
        for side in range(2):
            lanes = slice(LANES * side, LANES * (side + 1))
            outgoing[0, 2 * pair + side] = taken[:first, lanes]
            outgoing[1, 2 * pair + side] = taken[first : 2 * first, lanes]
            near_out[2 * pair + side] = taken[2 * first :, lanes]
        return 0

    loads[0].wait()
    lax.fori_loop(0, LINES // 2, pack, 0)
    loads[1].wait()
    edges[0:LEVELS] = mixing[...]

    pl.semaphore_wait(barrier, len(peers))

    edge_copy = remote(edges.at[0], edges.at[LEVELS], {"lev": (lev + 3) % 4}, lev > 0)
    pl.when(lev > 0)(edge_copy.start)
    pack_down_copy = remote(pack_bottom, coef_top, {"tile": tile_up}, has_below)
    pl.when(has_below)(pack_down_copy.start)
    pack_up_copy = remote(pack_top, coef_bottom, {"tile": tile_down}, has_above)
    pl.when(has_above)(pack_up_copy.start)

    near_copy = remote(near_out, near_in, {"tile": sibling})
    near_copy.start()
    cuts = (0, cap[3], cap[2], cap[1], cap[0])
    hop_copy = {}
    for hop in range(1, 5):
        for piece in range(5 - hop):
            for way in range(2):
                part = pl.ds(cuts[piece], cuts[piece + 1] - cuts[piece])
                src = outgoing if hop == 1 else got[hop - 1]
                hop_copy[hop, piece, way] = remote(
                    src.at[way, :, part, :], got[hop].at[way, :, part, :], {"tile": ring[way]}
                )
    side_copy = {}
    for hop in range(1, 5):
        for way in range(2):
            side_copy[hop, way] = remote(got[hop].at[way], got[hop].at[2 + way], {"tile": sibling})
    for piece in range(4):
        for way in range(2):
            hop_copy[1, piece, way].start()

    def relay(hop, piece):
        for way in range(2):
            hop_copy[hop - 1, piece, way].wait_recv()
            hop_copy[hop, piece, way].start()

    def share(hop):
        for way in range(2):
            hop_copy[hop, 4 - hop, way].wait_recv()
            side_copy[hop, way].start()

    pl.when(lev < 3)(edge_copy.wait_recv)

    @pl.when(lev == 3)
    def _():
        edges[LEVELS] = jnp.zeros((ROWS, COLS), F32)

    def level(step):
        return step + down * (LEVELS - 1 - 2 * step)

    def field(which, at, rows):
        return parent[which * LEVELS + at, rows, :]

    def sweep(rows, pivot, value0, value1):
        for step in range(LEVELS):
            at = level(step)
            edge = edges[at + 1 - down, rows, :]
            inverse = 1.0 / (pivot + edge)
            ratio = edge * inverse
            carry0 = value0 * inverse
            carry1 = value1 * inverse
            solved[at, rows, :] = carry0
            solved[LEVELS + at, rows, :] = carry1
            weight[at, rows, :] = ratio
            if step < LEVELS - 1:
                follow = level(step + 1)
                pivot = 1.0 + ratio * pivot
                value0 = field(0, follow, rows) + edge * carry0
                value1 = field(1, follow, rows) + edge * carry1
        message[0, rows, :] = pivot
        message[1, rows, :] = value0
        message[2, rows, :] = value1

    def back(rows, value0, value1, last):
        for step in range(last, -1, -1):
            at = level(step)
            ratio = weight[at, rows, :]
            value0 = solved[at, rows, :] + ratio * value0
            value1 = solved[LEVELS + at, rows, :] + ratio * value1
            solved[at, rows, :] = value0
            solved[LEVELS + at, rows, :] = value1

    halves = [pl.ds(0, 8), pl.ds(8, 8)]
    near_level = level(0)
    outer_copy = [
        remote(message.at[:, rows, :], from_outer.at[:, rows, :], {"lev": mate}, outer)
        for rows in halves
    ]
    center_copy = [
        remote(message.at[:, rows, :], from_center.at[:, rows, :], {"lev": across}, inner)
        for rows in halves
    ]
    inner_copy = [
        [
            remote(
                solved.at[which * LEVELS + near_level, rows, :],
                from_inner.at[which, rows, :],
                {"lev": mate},
                inner,
            )
            for which in range(2)
        ]
        for rows in halves
    ]

    @pl.when(outer)
    def _():
        for part, rows in enumerate(halves):
            at = level(0)
            sweep(rows, 1.0 + edges[at + down, rows, :], field(0, at, rows), field(1, at, rows))
            outer_copy[part].start()

    own_tiles = strip_tile[pl.ds(tile, 1), :]
    own_live = iota((1, ENTRIES), 1) < strip_count[tile]
    own_tiles = jnp.where(own_live, own_tiles, -1)
    source_row = iota((TILES, ENTRIES), 0)
    from_source = jnp.where(own_tiles == source_row, 1.0, 0.0)
    own_rank = jnp.sum(
        from_source
        * (jnp.dot(from_source.astype(BF16), upto, preferred_element_type=F32) - 1.0),
        axis=0,
        keepdims=True,
    )
    nest_column = iota((TILES, 1), 0)

    def offsets(source, totals):
        up_total, down_total = totals
        count = jnp.sum(jnp.where(listed == source, 1.0, 0.0), axis=1, keepdims=True)
        gap = chip_gap(nest_column, source)
        up, down_ = way_counts(gap, count)
        up_key, down_key = way_keys(gap, nest_column)
        own_up, own_down = way_keys(chip_gap(tile, source), tile)
        up_here = jnp.sum(jnp.where(up_key < own_up, up, 0.0), axis=0, keepdims=True)
        down_here = jnp.sum(jnp.where(down_key < own_down, down_, 0.0), axis=0, keepdims=True)
        here = own_tiles == source
        return (
            up_total + jnp.where(here, up_here, 0.0),
            down_total + jnp.where(here, down_here, 0.0),
        )

    nothing = jnp.zeros((1, ENTRIES), F32)
    up_start, down_start = lax.fori_loop(0, TILES, offsets, (nothing, nothing))
    own_gap = jnp.where(own_tiles >= 0, chip_gap(tile, own_tiles), -1)
    own_half = jnp.floor(own_rank * 0.5)
    own_odd = own_rank - 2.0 * own_half
    comes_up = ((own_gap >= 1) & (own_gap <= 3)) | ((own_gap == 4) & (own_odd < 0.5))
    place = jnp.where(own_gap == 4, own_half, own_rank) + jnp.where(comes_up, up_start, down_start)
    hops = jnp.where(own_gap >= 1, jnp.where(comes_up, own_gap, CHIPS - own_gap), 0)
    group = jnp.where((own_tiles & 1) == (tile & 1), 0.0, 2.0) + jnp.where(comes_up, 0.0, 1.0)
    targets = strip_target[pl.ds(tile, 1), :]
    targets = jnp.where(own_tiles >= 0, (targets & 7) * ROWS + (targets >> 3), -1)
    lands = jnp.where(targets == iota((NBLK, ENTRIES), 0), 1.0, 0.0).astype(BF16)

    def picks(place, rows):
        return jnp.where(place == iota((rows, ENTRIES), 0).astype(F32), 1.0, 0.0).astype(BF16)

    for hop in range(1, 5):
        size = cap[hop - 1]
        at = jnp.where(hops == hop, group * size + place, -1.0)
        route[hop][...] = onehot_product(lands, picks(at, 4 * size)).astype(BF16)
    at = jnp.where((own_gap == 0) & (own_tiles != tile), own_rank, -1.0)
    route_near[...] = onehot_product(lands, picks(at, SLOTS)).astype(BF16)
    own_blocks = strip_block[pl.ds(tile, 1), :]
    own_blocks = jnp.where(own_tiles == tile, (own_blocks & 7) * ROWS + (own_blocks >> 3), -1)
    route_own[...] = onehot_product(lands, picks(own_blocks.astype(F32), NBLK)).astype(BF16)

    @pl.when(inner)
    def _():
        for part, rows in enumerate(halves):
            at = level(0)
            outer_copy[part].wait_recv()
            edge = edges[at + down, rows, :]
            pivot = from_outer[0, rows, :]
            ratio = edge / (pivot + edge)
            sweep(
                rows,
                1.0 + ratio * pivot,
                field(0, at, rows) + ratio * from_outer[1, rows, :],
                field(1, at, rows) + ratio * from_outer[2, rows, :],
            )
            center_copy[part].start()

    relay(2, 0)
    relay(2, 1)

    @pl.when(inner)
    def _():
        for part, rows in enumerate(halves):
            center_copy[part].wait_recv()
            at = level(LEVELS - 1)
            edge = edges[at + 1 - down, rows, :]
            pivot = from_center[0, rows, :]
            ratio = edge / (pivot + edge)
            inverse = 1.0 / (message[0, rows, :] + ratio * pivot)
            value0 = (message[1, rows, :] + ratio * from_center[1, rows, :]) * inverse
            value1 = (message[2, rows, :] + ratio * from_center[2, rows, :]) * inverse
            solved[at, rows, :] = value0
            solved[LEVELS + at, rows, :] = value1
            back(rows, value0, value1, LEVELS - 2)
            for copy in inner_copy[part]:
                copy.start()

    @pl.when(has_above)
    def _():
        pack_down_copy.wait_recv()

    @pl.when(has_below)
    def _():
        pack_up_copy.wait_recv()

    @pl.when(tile == 0)
    def _():
        coef_top[...] = jnp.zeros((8, COLS), F32)

    @pl.when(tile == TILES - 1)
    def _():
        coef_bottom[...] = jnp.zeros((8, COLS), F32)

    cell_row = iota((ROWS, COLS), 0)
    for target, e_ref, n_ref, above in (
        (parent_coef, parent_e, parent_n, coef_top[6:7]),
        (nest_coef, nest_e, nest_n, coef_top[5:6]),
    ):
        northward = n_ref[...]
        north_above = jnp.where(cell_row == 0, above, pltpu.roll(northward, 1, 0))
        for which, value in enumerate(coefficients(e_ref[...], northward, north_above)):
            target[which] = value

    relay(2, 2)

    @pl.when(outer)
    def _():
        for part, rows in enumerate(halves):
            for copy in inner_copy[part]:
                copy.wait_recv()
            back(rows, from_inner[0, rows, :], from_inner[1, rows, :], LEVELS - 1)

    for line in range(LINES):
        rim_out[0, line : line + 1] = solved[line, 0:1, :]
        rim_out[1, line : line + 1] = solved[line, ROWS - 1 : ROWS, :]
    rim_up = remote(rim_out.at[0], rim_in.at[1], {"tile": tile_down}, has_above)
    rim_down = remote(rim_out.at[1], rim_in.at[0], {"tile": tile_up}, has_below)
    pl.when(has_above)(rim_up.start)
    pl.when(has_below)(rim_down.start)

    share(1)

    near_copy.wait_recv()
    loads[2].wait()

    def add_blocks(line, taken):
        for c in range(COLS // LANES):
            start[line, :, LANES * c : LANES * (c + 1)] += taken[ROWS * c : ROWS * (c + 1)]

    def scatter_near(pair, _):
        cells = jnp.concatenate([blocks_of(parent, 2 * pair), blocks_of(parent, 2 * pair + 1)], axis=1)
        near = jnp.concatenate([near_in[2 * pair], near_in[2 * pair + 1]], axis=1)
        taken = routed(route_own[...], cells) + routed(route_near[...], near)
        for side in range(2):
            line = 2 * pair + side
            start[line] = nest[line]
            add_blocks(line, taken[:, LANES * side : LANES * (side + 1)])
        return 0

    lax.fori_loop(0, LINES // 2, scatter_near, 0)

    def scatter(hop):
        for way in range(2):
            side_copy[hop, way].wait_recv()

        def one(pair, _):
            cells = jnp.concatenate(
                [
                    jnp.concatenate([got[hop][g, 2 * pair + side] for g in range(4)], axis=0)
                    for side in range(2)
                ],
                axis=1,
            )
            taken = routed(route[hop][...], cells)
            for side in range(2):
                add_blocks(2 * pair + side, taken[:, LANES * side : LANES * (side + 1)])
            return 0

        lax.fori_loop(0, LINES // 2, one, 0)

    relay(3, 0)
    relay(3, 1)

    pl.when(has_above)(rim_down.wait_recv)
    pl.when(has_below)(rim_up.wait_recv)

    @pl.when(tile == 0)
    def _():
        rim_in[0] = jnp.zeros((LINES, COLS), F32)

    @pl.when(tile == TILES - 1)
    def _():
        rim_in[1] = jnp.zeros((LINES, COLS), F32)

    def parent_level(at, _):
        results = []
        for which in range(2):
            line = which * LEVELS + at
            results.append(
                relax(
                    halves_of(solved, line),
                    rim_in[0, pl.ds(line, 1), :],
                    rim_in[1, pl.ds(line, 1), :],
                    parent_coef,
                )
            )
            for part in range(2):
                parent_out[line, 8 * part : 8 * part + 8] = results[which][part]
        for part in range(2):
            tag_sum[at, 8 * part : 8 * part + 8] = results[0][part] + results[1][part]
        return 0

    lax.fori_loop(0, LEVELS, parent_level, 0)

    quarter = COLS // 4

    def columns(which):
        return pl.ds(pl.multiple_of(which * quarter, quarter), quarter)

    tag_copy = []
    for d in (1, 2, 3):
        to = (tag + d) % 4
        copy = remote(tag_sum.at[:, :, columns(to)], tag_in.at[d - 1], {"tag": to})
        copy.start()
        tag_copy.append(copy)

    share(2)
    scatter(1)
    relay(4, 0)
    share(3)
    scatter(2)
    for copy in tag_copy:
        copy.wait_recv()
    bulk_out[...] = tag_sum[:, :, columns(tag)] + tag_in[0] + tag_in[1] + tag_in[2]
    share(4)
    scatter(3)
    scatter(4)

    for line in range(LINES):
        for r in range(NSUB):
            halo_out[0, r, line : line + 1] = start[line, r : r + 1, :]
            at = ROWS - NSUB + r
            halo_out[1, r, line : line + 1] = start[line, at : at + 1, :]
    halo_up = remote(halo_out.at[0], halo_in.at[1], {"tile": tile_down}, has_above)
    halo_down = remote(halo_out.at[1], halo_in.at[0], {"tile": tile_up}, has_below)
    pl.when(has_above)(halo_up.start)
    pl.when(has_below)(halo_down.start)
    pl.when(has_above)(halo_down.wait_recv)
    pl.when(has_below)(halo_up.wait_recv)

    @pl.when(tile == 0)
    def _():
        halo_in[0] = jnp.zeros((NSUB, LINES, COLS), F32)

    @pl.when(tile == TILES - 1)
    def _():
        halo_in[1] = jnp.zeros((NSUB, LINES, COLS), F32)

    in_grid = jnp.where(has_below, 1.0, 0.0)

    def e_top(r):
        return coef_top[r : r + 1]

    def n_top(r):
        return coef_top[3 + r : 4 + r]

    def e_bottom(r):
        return coef_bottom[r : r + 1]

    def n_bottom(r):
        return coef_bottom[3 + r : 4 + r]

    def own(ref, r):
        return ref[r : r + 1]

    second = relax_row(halo_in[0, 1], halo_in[0, 0], halo_in[0, 2], e_top(1), n_top(1), n_top(0))
    third = relax_row(halo_in[0, 2], halo_in[0, 1], halo_out[0, 0], e_top(2), n_top(2), n_top(1))
    edge_row = relax_row(
        halo_out[0, 0], halo_in[0, 2], halo_out[0, 1], own(nest_e, 0), own(nest_n, 0), n_top(2)
    )
    halos[0, 0] = halo_in[0, 2]
    halos[0, 1] = third
    halos[0, 2] = relax_row(third, second, edge_row, e_top(2), n_top(2), n_top(1))
    last = ROWS - 1
    second = relax_row(
        halo_in[1, 1], halo_in[1, 0], halo_in[1, 2], e_bottom(1), n_bottom(1), n_bottom(0)
    )
    third = in_grid * relax_row(
        halo_in[1, 0], halo_out[1, 2], halo_in[1, 1], e_bottom(0), n_bottom(0), own(nest_n, last)
    )
    edge_row = relax_row(
        halo_out[1, 2],
        halo_out[1, 1],
        halo_in[1, 0],
        own(nest_e, last),
        own(nest_n, last),
        own(nest_n, last - 1),
    )
    halos[1, 0] = halo_in[1, 0]
    halos[1, 1] = third
    halos[1, 2] = in_grid * relax_row(
        third, edge_row, second, e_bottom(0), n_bottom(0), own(nest_n, last)
    )

    for copy, guard in pending:
        if guard is None:
            copy.wait_send()
        else:
            pl.when(guard)(copy.wait_send)


def finish_kernel(
    group, start, halos, coef, parent, bulk, parent_out, nest_out, bulk_out, held, sems
):
    copies = [
        pltpu.make_async_copy(parent, parent_out, sems.at[0]),
        pltpu.make_async_copy(bulk, bulk_out, sems.at[1]),
    ]
    for copy in copies:
        copy.start()

    def part_copy(at):
        lines = pl.ds(group * at, group)
        return pltpu.make_async_copy(held.at[lines], nest_out.at[lines], sems.at[2 + at])

    def lines_at(at, _):
        lines = [group * at + k for k in range(group)]
        values = [halves_of(start, line) for line in lines]
        for step in range(NSUB):
            for k, line in enumerate(lines):
                values[k] = relax(
                    values[k],
                    halos[0, step, pl.ds(line, 1), :],
                    halos[1, step, pl.ds(line, 1), :],
                    coef,
                )
        for k, line in enumerate(lines):
            for part in range(2):
                held[line, 8 * part : 8 * part + 8] = values[k][part]
        part_copy(at).start()
        return 0

    lax.fori_loop(0, LINES // group, lines_at, 0)
    for copy in copies:
        copy.wait()
    for at in range(LINES // group):
        part_copy(at).wait()


VMEM = pl.BlockSpec(memory_space=pltpu.VMEM)
ANY = pl.BlockSpec(memory_space=pl.ANY)
GROUP = 4
SMEM = pl.BlockSpec(memory_space=pltpu.SMEM)


def step_call(cap, collective, arrays):
    first = cap[0]
    grid = (LINES, ROWS, COLS)
    copies = 3 + 1 + 20 + 8 + 2 + 2 + 4 + 2 + 3 + 2
    shapes = [
        pltpu.VMEM(grid, F32),
        pltpu.VMEM(grid, F32),
        pltpu.VMEM((LEVELS, ROWS, COLS), F32),
        pltpu.VMEM((LEVELS + 1, ROWS, COLS), F32),
        pltpu.VMEM((8, COLS), F32),
        pltpu.VMEM((8, COLS), F32),
        pltpu.VMEM((8, COLS), F32),
        pltpu.VMEM((8, COLS), F32),
        pltpu.VMEM((TILES, ENTRIES), F32),
        pltpu.VMEM((TILES, ENTRIES), F32),
        pltpu.VMEM((2, LINES, first, LANES), F32),
        pltpu.VMEM((LINES, SLOTS, LANES), F32),
        pltpu.VMEM((LINES, SLOTS, LANES), F32),
    ]
    shapes += [pltpu.VMEM((4, LINES, size, LANES), F32) for size in cap]
    shapes += [pltpu.VMEM((NBLK, 4 * size), BF16) for size in cap]
    shapes += [
        pltpu.VMEM((NBLK, SLOTS), BF16),
        pltpu.VMEM((NBLK, NBLK), BF16),
        pltpu.VMEM(grid, F32),
        pltpu.VMEM((LEVELS, ROWS, COLS), F32),
        pltpu.VMEM((3, ROWS, COLS), F32),
        pltpu.VMEM((3, ROWS, COLS), F32),
        pltpu.VMEM((3, ROWS, COLS), F32),
        pltpu.VMEM((2, ROWS, COLS), F32),
        pltpu.VMEM((2, LINES, COLS), F32),
        pltpu.VMEM((2, LINES, COLS), F32),
        pltpu.VMEM((5, ROWS, COLS), F32),
        pltpu.VMEM((LEVELS, ROWS, COLS), F32),
        pltpu.VMEM((3, LEVELS, ROWS, COLS // 4), F32),
        pltpu.VMEM((2, NSUB, LINES, COLS), F32),
        pltpu.VMEM((2, NSUB, LINES, COLS), F32),
        pltpu.SemaphoreType.DMA((copies,)),
        pltpu.SemaphoreType.DMA((copies,)),
        pltpu.SemaphoreType.DMA((3,)),
    ]
    return pl.pallas_call(
        functools.partial(step_kernel, cap),
        out_shape=[
            jax.ShapeDtypeStruct(grid, F32),
            jax.ShapeDtypeStruct((2, NSUB, LINES, COLS), F32),
            jax.ShapeDtypeStruct((5, ROWS, COLS), F32),
            jax.ShapeDtypeStruct(grid, F32),
            jax.ShapeDtypeStruct((LEVELS, ROWS, COLS // 4), F32),
        ],
        in_specs=[ANY] * 3 + [VMEM] * 7 + [SMEM],
        out_specs=[VMEM] * 5,
        scratch_shapes=shapes,
        compiler_params=pltpu.CompilerParams(
            collective_id=collective, has_side_effects=True, vmem_limit_bytes=56 * 1024 * 1024
        ),
    )(*arrays)


def shards(
    parent_field,
    nest_field,
    parent_mixing,
    parent_eastward,
    parent_northward,
    nest_eastward,
    nest_northward,
    strip_tile,
    strip_block,
    strip_target,
    strip_count,
):
    full_shape = parent_field.shape
    grid = (LINES, ROWS, COLS)
    arrays = (
        parent_field.reshape(grid),
        nest_field.reshape(grid),
        parent_mixing,
        parent_eastward,
        parent_northward,
        nest_eastward,
        nest_northward,
        strip_tile,
        strip_block,
        strip_target,
        strip_count,
    )
    flag = pl.pallas_call(
        plan_kernel,
        out_shape=jax.ShapeDtypeStruct((1,), jnp.int32),
        in_specs=[VMEM, SMEM],
        out_specs=SMEM,
    )(strip_tile, strip_count)
    states = lax.switch(
        flag[0],
        [
            lambda *a: step_call(SMALL, 3, a),
            lambda *a: step_call(USUAL, 2, a),
            lambda *a: step_call(FULL, 1, a),
        ],
        *arrays,
    )
    parent_adjoint, nest_adjoint, bulk_adjoint = pl.pallas_call(
        functools.partial(finish_kernel, GROUP),
        out_shape=[
            jax.ShapeDtypeStruct(grid, F32),
            jax.ShapeDtypeStruct(grid, F32),
            jax.ShapeDtypeStruct((LEVELS, ROWS, COLS // 4), F32),
        ],
        in_specs=[VMEM] * 5,
        out_specs=[ANY] * 3,
        scratch_shapes=[
            pltpu.VMEM(grid, F32),
            pltpu.SemaphoreType.DMA((2 + LINES // GROUP,)),
        ],
        compiler_params=pltpu.CompilerParams(vmem_limit_bytes=32 * 1024 * 1024),
    )(*states)
    return parent_adjoint.reshape(full_shape), nest_adjoint.reshape(full_shape), bulk_adjoint


def solution(mesh):
    in_specs = (
        P("tag", "lev", "tile", None),
        P("tag", "lev", "tile", None),
        P("lev", "tile", None),
        P("tile", None),
        P("tile", None),
        P("tile", None),
        P("tile", None),
        P(),
        P(),
        P(),
        P(),
    )
    out_specs = (
        P("tag", "lev", "tile", None),
        P("tag", "lev", "tile", None),
        P("lev", "tile", "tag"),
    )
    return jax.shard_map(shards, mesh=mesh, in_specs=in_specs, out_specs=out_specs, check_vma=False)
```

```python
import functools

import jax
import jax.numpy as jnp
from jax import lax
from jax.experimental import pallas as pl
from jax.experimental.pallas import tpu as pltpu
from jax.sharding import PartitionSpec as P

MESH = pl.DeviceIdType.MESH
F32 = jnp.float32
BF16 = jnp.bfloat16
TILES = 16
CHIPS = 8
SLOTS = 16
LINES = 16
LEVELS = 8
ROWS = 16
COLS = 1024
LANES = 128
NBLK = 128
ENTRIES = 256
NSUB = 3
FULL = (112, 80, 48, 16)
USUAL = (64, 48, 40, 16)
SMALL = (56, 40, 32, 16)


def iota(shape, dim):
    return lax.broadcasted_iota(jnp.int32, shape, dim)


def chip_gap(to_tile, from_tile):
    return ((to_tile >> 1) - (from_tile >> 1)) & (CHIPS - 1)


def way_counts(gap, count):
    half = jnp.floor(count * 0.5)
    up = jnp.where((gap >= 1) & (gap <= 3), count, jnp.where(gap == 4, count - half, 0.0))
    down = jnp.where(gap >= 5, count, jnp.where(gap == 4, half, 0.0))
    return up, down


def way_keys(gap, tile):
    side = tile & 1
    return (4 - gap) * 2 + side, (gap - 4) * 2 + side


def counts_column(count_ref):
    row = iota((TILES, ENTRIES), 0)
    total = jnp.zeros((TILES, ENTRIES), jnp.int32)
    for tile in range(TILES):
        total = jnp.where(row == tile, count_ref[tile], total)
    return total


def plan_kernel(tile_ref, count_ref, flag_ref, listed_ref):
    live = iota((TILES, ENTRIES), 1) < counts_column(count_ref)
    listed = jnp.where(live, tile_ref[...], -1)
    listed_ref[...] = listed
    lane = iota((TILES, LANES), 1)
    count = jnp.zeros((TILES, LANES), F32)
    for source in range(TILES):
        total = jnp.sum(jnp.where(listed == source, 1.0, 0.0), axis=1, keepdims=True)
        count = jnp.where(lane == source, total, count)
    gap = chip_gap(iota((TILES, LANES), 0), lane)
    up, down = way_counts(gap, count)
    small = jnp.zeros((1, LANES), F32)
    usual = jnp.zeros((1, LANES), F32)
    for hop in range(1, 4):
        for load in (jnp.where(gap >= hop, up, 0.0), jnp.where(CHIPS - gap >= hop, down, 0.0)):
            total = jnp.sum(load, axis=0, keepdims=True)
            small = jnp.maximum(small, total - SMALL[hop - 1])
            usual = jnp.maximum(usual, total - USUAL[hop - 1])
    over = jnp.where(small > 0.5, 1.0, 0.0) + jnp.where(usual > 0.5, 1.0, 0.0)
    flag_ref[0] = jnp.max(over).astype(jnp.int32)


def split(value):
    high = value.astype(BF16)
    low = (value - high.astype(F32)).astype(BF16)
    return high, low


def routed(matrix, value):
    high, low = split(value)
    return jnp.dot(matrix, high, preferred_element_type=F32) + jnp.dot(
        matrix, low, preferred_element_type=F32
    )


def onehot_product(left, right):
    return lax.dot_general(left, right, (((1,), (1,)), ((), ())), preferred_element_type=F32)


def blocks_of(ref, line):
    return jnp.concatenate(
        [ref[line, :, LANES * c : LANES * (c + 1)] for c in range(COLS // LANES)], axis=0
    )


def relax(halves, top, bottom, coef):
    row = iota((8, COLS), 0)
    later = [pltpu.roll(x, 1, 0) for x in halves]
    sooner = [pltpu.roll(x, 7, 0) for x in halves]
    above = (jnp.where(row == 0, top, later[0]), jnp.where(row == 0, later[0], later[1]))
    below = (jnp.where(row == 7, sooner[1], sooner[0]), jnp.where(row == 7, bottom, sooner[1]))
    results = []
    for part in range(2):
        x = halves[part]
        rows = slice(8 * part, 8 * part + 8)
        results.append(
            coef[0, rows] * x
            + coef[1, rows] * below[part]
            + coef[2, rows] * above[part]
            + coef[3, rows] * pltpu.roll(x, COLS - 1, 1)
            + coef[4, rows] * pltpu.roll(x, 1, 1)
        )
    return results


def halves_of(ref, line):
    return [ref[line, 0:8, :], ref[line, 8:16, :]]


def coefficients(eastward, northward, north_above):
    col = iota(eastward.shape, 1)
    west = jnp.where(col == 0, 0.0, pltpu.roll(eastward, 1, 1))
    east = jnp.where(col == COLS - 1, 0.0, eastward)
    center = 1.0 - northward - north_above - eastward - west
    return center, northward, north_above, east, west


def relax_row(x, above, below, eastward, northward, north_above):
    wide = (LINES, COLS)
    center, north, north_up, east, west = coefficients(
        jnp.broadcast_to(eastward, (8, COLS)),
        jnp.broadcast_to(northward, (8, COLS)),
        jnp.broadcast_to(north_above, (8, COLS)),
    )
    center, north, north_up, east, west = (
        jnp.broadcast_to(v[:1], wide) for v in (center, north, north_up, east, west)
    )
    return (
        center * x
        + north * below
        + north_up * above
        + east * pltpu.roll(x, COLS - 1, 1)
        + west * pltpu.roll(x, 1, 1)
    )


def step_kernel(
    cap,
    parent_hbm,
    nest_hbm,
    mixing_hbm,
    parent_e_hbm,
    parent_n_hbm,
    nest_e_hbm,
    nest_n_hbm,
    block_hbm,
    target_hbm,
    listed_hbm,
    start,
    halos,
    nest_coef,
    parent_out,
    bulk_out,
    parent,
    nest,
    mixing,
    parent_e,
    parent_n,
    nest_e,
    nest_n,
    strip_block,
    strip_target,
    strip_listed,
    edges,
    pack_top,
    pack_bottom,
    coef_top,
    coef_bottom,
    slot_of,
    block_of,
    outgoing,
    near_out,
    near_in,
    got1,
    got2,
    got3,
    got4,
    route1,
    route2,
    route3,
    route4,
    route_near,
    route_own,
    solved,
    weight,
    message,
    from_outer,
    from_center,
    from_inner,
    rim_out,
    rim_in,
    parent_coef,
    tag_sum,
    tag_in,
    halo_out,
    halo_in,
    send_sem,
    recv_sem,
    load_sem,
):
    loads = [
        pltpu.make_async_copy(src, dst, load_sem.at[at])
        for at, (src, dst) in enumerate(
            (
                (listed_hbm, strip_listed),
                (block_hbm, strip_block),
                (parent_hbm, parent),
                (mixing_hbm, mixing),
                (nest_e_hbm, nest_e),
                (nest_n_hbm, nest_n),
                (parent_n_hbm, parent_n),
                (parent_e_hbm, parent_e),
                (target_hbm, strip_target),
                (nest_hbm, nest),
            )
        )
    ]
    for copy in loads:
        copy.start()
    got = (None, got1, got2, got3, got4)
    route = (None, route1, route2, route3, route4)
    first = cap[0]
    tile = lax.axis_index("tile")
    lev = lax.axis_index("lev")
    tag = lax.axis_index("tag")
    sibling = tile + 1 - 2 * (tile % 2)
    ring = ((tile + 2) % TILES, (tile + TILES - 2) % TILES)
    tile_up = (tile + 1) % TILES
    tile_down = (tile + TILES - 1) % TILES
    mate = lev + 1 - 2 * (lev % 2)
    across = 3 - lev
    outer = lev % 3 == 0
    inner = lev % 3 != 0
    down = lev // 2

    barrier = pltpu.get_barrier_semaphore()
    peers = [{"tile": t} for t in (tile_up, tile_down) + ring]
    peers += [{"lev": (lev + d) % 4} for d in (1, 2, 3)]
    peers += [{"tag": (tag + d) % 4} for d in (1, 2, 3)]
    for peer in peers:
        pl.semaphore_signal(barrier, inc=1, device_id=peer, device_id_type=MESH)

    used = [0]
    pending = []

    def remote(src, dst, device, guard=None):
        at = used[0]
        used[0] += 1
        copy = pltpu.make_async_remote_copy(
            src_ref=src,
            dst_ref=dst,
            send_sem=send_sem.at[at],
            recv_sem=recv_sem.at[at],
            device_id=device,
            device_id_type=MESH,
        )
        pending.append((copy, guard))
        return copy

    has_above = tile > 0
    has_below = tile < TILES - 1

    loads[0].wait()
    loads[1].wait()
    row = iota((TILES, ENTRIES), 0)
    listed = strip_listed[...]
    mine = jnp.where(listed == tile, 1.0, 0.0)
    upto = jnp.where(
        iota((ENTRIES, ENTRIES), 0) <= iota((ENTRIES, ENTRIES), 1), 1.0, 0.0
    ).astype(BF16)
    rank = jnp.dot(mine.astype(BF16), upto, preferred_element_type=F32) - 1.0
    count = jnp.broadcast_to(jnp.sum(mine, axis=1, keepdims=True), (TILES, ENTRIES))
    gap = chip_gap(row, tile)
    up_count, down_count = way_counts(gap, count)
    up_key, down_key = way_keys(gap, row)
    up_at = jnp.zeros((TILES, ENTRIES), F32)
    down_at = jnp.zeros((TILES, ENTRIES), F32)
    for other in range(TILES):
        up_at += jnp.where(up_key[other : other + 1] < up_key, up_count[other : other + 1], 0.0)
        down_at += jnp.where(
            down_key[other : other + 1] < down_key, down_count[other : other + 1], 0.0
        )
    half = jnp.floor(rank * 0.5)
    odd = rank - 2.0 * half
    goes_up = ((gap >= 1) & (gap <= 3)) | ((gap == 4) & (odd < 0.5))
    goes_down = (gap >= 5) | ((gap == 4) & (odd > 0.5))
    in_row = jnp.where(gap == 4, half, rank)
    slot = jnp.where(
        goes_up,
        up_at + in_row,
        jnp.where(
            goes_down,
            first + down_at + in_row,
            jnp.where((gap == 0) & (row != tile), 2 * first + rank, -1.0),
        ),
    )
    slot_of[...] = jnp.where(mine > 0.5, slot, -1.0)
    blocks = strip_block[...]
    block_of[...] = ((blocks & 7) * ROWS + (blocks >> 3) + 1).astype(F32)

    def gather_matrix(begin, size):
        wanted = (iota((size, ENTRIES), 0) + begin).astype(F32)

        def one(nest_tile, total):
            at = pl.ds(nest_tile, 1)
            return total + jnp.where(slot_of[at, :] == wanted, block_of[at, :], 0.0)

        total = lax.fori_loop(0, TILES, one, jnp.zeros((size, ENTRIES), F32))
        index = jnp.sum(total, axis=1, keepdims=True) - 1.0
        return jnp.where(index == iota((size, NBLK), 1).astype(F32), 1.0, 0.0).astype(BF16)

    gather = jnp.concatenate(
        [gather_matrix(0, first), gather_matrix(first, first), gather_matrix(2 * first, SLOTS)],
        axis=0,
    )

    def pack(pair, _):
        cells = jnp.concatenate([blocks_of(parent, 2 * pair), blocks_of(parent, 2 * pair + 1)], axis=1)
        taken = routed(gather, cells)
        for side in range(2):
            lanes = slice(LANES * side, LANES * (side + 1))
            outgoing[0, 2 * pair + side] = taken[:first, lanes]
            outgoing[1, 2 * pair + side] = taken[first : 2 * first, lanes]
            near_out[2 * pair + side] = taken[2 * first :, lanes]
        return 0

    loads[2].wait()
    lax.fori_loop(0, LINES // 2, pack, 0)
    for copy in loads[3:7]:
        copy.wait()
    edges[0:LEVELS] = mixing[...]

    pack_bottom[0:3] = nest_e[ROWS - 3 : ROWS]
    pack_bottom[3:6] = nest_n[ROWS - 3 : ROWS]
    pack_bottom[6:7] = parent_n[ROWS - 1 : ROWS]
    pack_bottom[7:8] = parent_n[ROWS - 1 : ROWS]
    pack_top[0:3] = nest_e[0:3]
    pack_top[3:6] = nest_n[0:3]
    pack_top[6:8] = parent_n[0:2]

    pl.semaphore_wait(barrier, len(peers))

    edge_copy = remote(edges.at[0], edges.at[LEVELS], {"lev": (lev + 3) % 4}, lev > 0)
    pl.when(lev > 0)(edge_copy.start)
    pack_down_copy = remote(pack_bottom, coef_top, {"tile": tile_up}, has_below)
    pl.when(has_below)(pack_down_copy.start)
    pack_up_copy = remote(pack_top, coef_bottom, {"tile": tile_down}, has_above)
    pl.when(has_above)(pack_up_copy.start)

    near_copy = remote(near_out, near_in, {"tile": sibling})
    near_copy.start()
    cuts = (0, cap[3], cap[2], cap[1], cap[0])
    hop_copy = {}
    for hop in range(1, 5):
        for piece in range(5 - hop):
            for way in range(2):
                part = pl.ds(cuts[piece], cuts[piece + 1] - cuts[piece])
                src = outgoing if hop == 1 else got[hop - 1]
                hop_copy[hop, piece, way] = remote(
                    src.at[way, :, part, :], got[hop].at[way, :, part, :], {"tile": ring[way]}
                )
    side_copy = {}
    for hop in range(1, 5):
        for way in range(2):
            side_copy[hop, way] = remote(got[hop].at[way], got[hop].at[2 + way], {"tile": sibling})
    for piece in range(4):
        for way in range(2):
            hop_copy[1, piece, way].start()

    def relay(hop, piece):
        for way in range(2):
            hop_copy[hop - 1, piece, way].wait_recv()
            hop_copy[hop, piece, way].start()

    def share(hop):
        for way in range(2):
            hop_copy[hop, 4 - hop, way].wait_recv()
            side_copy[hop, way].start()

    pl.when(lev < 3)(edge_copy.wait_recv)

    @pl.when(lev == 3)
    def _():
        edges[LEVELS] = jnp.zeros((ROWS, COLS), F32)

    def level(step):
        return step + down * (LEVELS - 1 - 2 * step)

    def field(which, at, rows):
        return parent[which * LEVELS + at, rows, :]

    def sweep(rows, pivot, value0, value1):
        for step in range(LEVELS):
            at = level(step)
            edge = edges[at + 1 - down, rows, :]
            inverse = 1.0 / (pivot + edge)
            ratio = edge * inverse
            carry0 = value0 * inverse
            carry1 = value1 * inverse
            solved[at, rows, :] = carry0
            solved[LEVELS + at, rows, :] = carry1
            weight[at, rows, :] = ratio
            if step < LEVELS - 1:
                follow = level(step + 1)
                pivot = 1.0 + ratio * pivot
                value0 = field(0, follow, rows) + edge * carry0
                value1 = field(1, follow, rows) + edge * carry1
        message[0, rows, :] = pivot
        message[1, rows, :] = value0
        message[2, rows, :] = value1

    def back(rows, value0, value1, last):
        for step in range(last, -1, -1):
            at = level(step)
            ratio = weight[at, rows, :]
            value0 = solved[at, rows, :] + ratio * value0
            value1 = solved[LEVELS + at, rows, :] + ratio * value1
            solved[at, rows, :] = value0
            solved[LEVELS + at, rows, :] = value1

    halves = [pl.ds(0, 8), pl.ds(8, 8)]
    near_level = level(0)
    outer_copy = [
        remote(message.at[:, rows, :], from_outer.at[:, rows, :], {"lev": mate}, outer)
        for rows in halves
    ]
    center_copy = [
        remote(message.at[:, rows, :], from_center.at[:, rows, :], {"lev": across}, inner)
        for rows in halves
    ]
    inner_copy = [
        [
            remote(
                solved.at[which * LEVELS + near_level, rows, :],
                from_inner.at[which, rows, :],
                {"lev": mate},
                inner,
            )
            for which in range(2)
        ]
        for rows in halves
    ]

    @pl.when(outer)
    def _():
        for part, rows in enumerate(halves):
            at = level(0)
            sweep(rows, 1.0 + edges[at + down, rows, :], field(0, at, rows), field(1, at, rows))
            outer_copy[part].start()

    for copy in loads[7:]:
        copy.wait()
    own_tiles = strip_listed[pl.ds(tile, 1), :]
    source_row = iota((TILES, ENTRIES), 0)
    from_source = jnp.where(own_tiles == source_row, 1.0, 0.0)
    own_rank = jnp.sum(
        from_source
        * (jnp.dot(from_source.astype(BF16), upto, preferred_element_type=F32) - 1.0),
        axis=0,
        keepdims=True,
    )
    nest_column = iota((TILES, 1), 0)

    def offsets(source, totals):
        up_total, down_total = totals
        count = jnp.sum(jnp.where(listed == source, 1.0, 0.0), axis=1, keepdims=True)
        gap = chip_gap(nest_column, source)
        up, down_ = way_counts(gap, count)
        up_key, down_key = way_keys(gap, nest_column)
        own_up, own_down = way_keys(chip_gap(tile, source), tile)
        up_here = jnp.sum(jnp.where(up_key < own_up, up, 0.0), axis=0, keepdims=True)
        down_here = jnp.sum(jnp.where(down_key < own_down, down_, 0.0), axis=0, keepdims=True)
        here = own_tiles == source
        return (
            up_total + jnp.where(here, up_here, 0.0),
            down_total + jnp.where(here, down_here, 0.0),
        )

    nothing = jnp.zeros((1, ENTRIES), F32)
    up_start, down_start = lax.fori_loop(0, TILES, offsets, (nothing, nothing))
    own_gap = jnp.where(own_tiles >= 0, chip_gap(tile, own_tiles), -1)
    own_half = jnp.floor(own_rank * 0.5)
    own_odd = own_rank - 2.0 * own_half
    comes_up = ((own_gap >= 1) & (own_gap <= 3)) | ((own_gap == 4) & (own_odd < 0.5))
    place = jnp.where(own_gap == 4, own_half, own_rank) + jnp.where(comes_up, up_start, down_start)
    hops = jnp.where(own_gap >= 1, jnp.where(comes_up, own_gap, CHIPS - own_gap), 0)
    group = jnp.where((own_tiles & 1) == (tile & 1), 0.0, 2.0) + jnp.where(comes_up, 0.0, 1.0)
    targets = strip_target[pl.ds(tile, 1), :]
    targets = jnp.where(own_tiles >= 0, (targets & 7) * ROWS + (targets >> 3), -1)
    lands = jnp.where(targets == iota((NBLK, ENTRIES), 0), 1.0, 0.0).astype(BF16)

    def picks(place, rows):
        return jnp.where(place == iota((rows, ENTRIES), 0).astype(F32), 1.0, 0.0).astype(BF16)

    for hop in range(1, 5):
        size = cap[hop - 1]
        at = jnp.where(hops == hop, group * size + place, -1.0)
        route[hop][...] = onehot_product(lands, picks(at, 4 * size)).astype(BF16)
    at = jnp.where((own_gap == 0) & (own_tiles != tile), own_rank, -1.0)
    route_near[...] = onehot_product(lands, picks(at, SLOTS)).astype(BF16)
    own_blocks = strip_block[pl.ds(tile, 1), :]
    own_blocks = jnp.where(own_tiles == tile, (own_blocks & 7) * ROWS + (own_blocks >> 3), -1)
    route_own[...] = onehot_product(lands, picks(own_blocks.astype(F32), NBLK)).astype(BF16)

    @pl.when(inner)
    def _():
        for part, rows in enumerate(halves):
            at = level(0)
            outer_copy[part].wait_recv()
            edge = edges[at + down, rows, :]
            pivot = from_outer[0, rows, :]
            ratio = edge / (pivot + edge)
            sweep(
                rows,
                1.0 + ratio * pivot,
                field(0, at, rows) + ratio * from_outer[1, rows, :],
                field(1, at, rows) + ratio * from_outer[2, rows, :],
            )
            center_copy[part].start()

    relay(2, 0)
    relay(2, 1)

    @pl.when(inner)
    def _():
        for part, rows in enumerate(halves):
            center_copy[part].wait_recv()
            at = level(LEVELS - 1)
            edge = edges[at + 1 - down, rows, :]
            pivot = from_center[0, rows, :]
            ratio = edge / (pivot + edge)
            inverse = 1.0 / (message[0, rows, :] + ratio * pivot)
            value0 = (message[1, rows, :] + ratio * from_center[1, rows, :]) * inverse
            value1 = (message[2, rows, :] + ratio * from_center[2, rows, :]) * inverse
            solved[at, rows, :] = value0
            solved[LEVELS + at, rows, :] = value1
            back(rows, value0, value1, LEVELS - 2)
            for copy in inner_copy[part]:
                copy.start()

    @pl.when(has_above)
    def _():
        pack_down_copy.wait_recv()

    @pl.when(has_below)
    def _():
        pack_up_copy.wait_recv()

    @pl.when(tile == 0)
    def _():
        coef_top[...] = jnp.zeros((8, COLS), F32)

    @pl.when(tile == TILES - 1)
    def _():
        coef_bottom[...] = jnp.zeros((8, COLS), F32)

    cell_row = iota((ROWS, COLS), 0)
    for target, e_ref, n_ref, above in (
        (parent_coef, parent_e, parent_n, coef_top[6:7]),
        (nest_coef, nest_e, nest_n, coef_top[5:6]),
    ):
        northward = n_ref[...]
        north_above = jnp.where(cell_row == 0, above, pltpu.roll(northward, 1, 0))
        for which, value in enumerate(coefficients(e_ref[...], northward, north_above)):
            target[which] = value

    relay(2, 2)

    @pl.when(outer)
    def _():
        for part, rows in enumerate(halves):
            for copy in inner_copy[part]:
                copy.wait_recv()
            back(rows, from_inner[0, rows, :], from_inner[1, rows, :], LEVELS - 1)

    for line in range(LINES):
        rim_out[0, line : line + 1] = solved[line, 0:1, :]
        rim_out[1, line : line + 1] = solved[line, ROWS - 1 : ROWS, :]
    rim_up = remote(rim_out.at[0], rim_in.at[1], {"tile": tile_down}, has_above)
    rim_down = remote(rim_out.at[1], rim_in.at[0], {"tile": tile_up}, has_below)
    pl.when(has_above)(rim_up.start)
    pl.when(has_below)(rim_down.start)

    share(1)

    near_copy.wait_recv()

    def add_blocks(line, taken):
        for c in range(COLS // LANES):
            start[line, :, LANES * c : LANES * (c + 1)] += taken[ROWS * c : ROWS * (c + 1)]

    def scatter_near(pair, _):
        cells = jnp.concatenate([blocks_of(parent, 2 * pair), blocks_of(parent, 2 * pair + 1)], axis=1)
        near = jnp.concatenate([near_in[2 * pair], near_in[2 * pair + 1]], axis=1)
        taken = routed(route_own[...], cells) + routed(route_near[...], near)
        for side in range(2):
            line = 2 * pair + side
            start[line] = nest[line]
            add_blocks(line, taken[:, LANES * side : LANES * (side + 1)])
        return 0

    lax.fori_loop(0, LINES // 2, scatter_near, 0)

    def scatter(hop):
        for way in range(2):
            side_copy[hop, way].wait_recv()

        def one(pair, _):
            cells = jnp.concatenate(
                [
                    jnp.concatenate([got[hop][g, 2 * pair + side] for g in range(4)], axis=0)
                    for side in range(2)
                ],
                axis=1,
            )
            taken = routed(route[hop][...], cells)
            for side in range(2):
                add_blocks(2 * pair + side, taken[:, LANES * side : LANES * (side + 1)])
            return 0

        lax.fori_loop(0, LINES // 2, one, 0)

    relay(3, 0)
    relay(3, 1)

    pl.when(has_above)(rim_down.wait_recv)
    pl.when(has_below)(rim_up.wait_recv)

    @pl.when(tile == 0)
    def _():
        rim_in[0] = jnp.zeros((LINES, COLS), F32)

    @pl.when(tile == TILES - 1)
    def _():
        rim_in[1] = jnp.zeros((LINES, COLS), F32)

    def parent_level(at, _):
        results = []
        for which in range(2):
            line = which * LEVELS + at
            results.append(
                relax(
                    halves_of(solved, line),
                    rim_in[0, pl.ds(line, 1), :],
                    rim_in[1, pl.ds(line, 1), :],
                    parent_coef,
                )
            )
            for part in range(2):
                parent_out[line, 8 * part : 8 * part + 8] = results[which][part]
        for part in range(2):
            tag_sum[at, 8 * part : 8 * part + 8] = results[0][part] + results[1][part]
        return 0

    lax.fori_loop(0, LEVELS, parent_level, 0)

    quarter = COLS // 4

    def columns(which):
        return pl.ds(pl.multiple_of(which * quarter, quarter), quarter)

    tag_copy = []
    for d in (1, 2, 3):
        to = (tag + d) % 4
        copy = remote(tag_sum.at[:, :, columns(to)], tag_in.at[d - 1], {"tag": to})
        copy.start()
        tag_copy.append(copy)

    share(2)
    scatter(1)
    relay(4, 0)
    share(3)
    scatter(2)
    for copy in tag_copy:
        copy.wait_recv()
    bulk_out[...] = tag_sum[:, :, columns(tag)] + tag_in[0] + tag_in[1] + tag_in[2]
    share(4)
    scatter(3)
    scatter(4)

    for line in range(LINES):
        for r in range(NSUB):
            halo_out[0, r, line : line + 1] = start[line, r : r + 1, :]
            at = ROWS - NSUB + r
            halo_out[1, r, line : line + 1] = start[line, at : at + 1, :]
    halo_up = remote(halo_out.at[0], halo_in.at[1], {"tile": tile_down}, has_above)
    halo_down = remote(halo_out.at[1], halo_in.at[0], {"tile": tile_up}, has_below)
    pl.when(has_above)(halo_up.start)
    pl.when(has_below)(halo_down.start)
    pl.when(has_above)(halo_down.wait_recv)
    pl.when(has_below)(halo_up.wait_recv)

    @pl.when(tile == 0)
    def _():
        halo_in[0] = jnp.zeros((NSUB, LINES, COLS), F32)

    @pl.when(tile == TILES - 1)
    def _():
        halo_in[1] = jnp.zeros((NSUB, LINES, COLS), F32)

    in_grid = jnp.where(has_below, 1.0, 0.0)

    def e_top(r):
        return coef_top[r : r + 1]

    def n_top(r):
        return coef_top[3 + r : 4 + r]

    def e_bottom(r):
        return coef_bottom[r : r + 1]

    def n_bottom(r):
        return coef_bottom[3 + r : 4 + r]

    def own(ref, r):
        return ref[r : r + 1]

    second = relax_row(halo_in[0, 1], halo_in[0, 0], halo_in[0, 2], e_top(1), n_top(1), n_top(0))
    third = relax_row(halo_in[0, 2], halo_in[0, 1], halo_out[0, 0], e_top(2), n_top(2), n_top(1))
    edge_row = relax_row(
        halo_out[0, 0], halo_in[0, 2], halo_out[0, 1], own(nest_e, 0), own(nest_n, 0), n_top(2)
    )
    halos[0, 0] = halo_in[0, 2]
    halos[0, 1] = third
    halos[0, 2] = relax_row(third, second, edge_row, e_top(2), n_top(2), n_top(1))
    last = ROWS - 1
    second = relax_row(
        halo_in[1, 1], halo_in[1, 0], halo_in[1, 2], e_bottom(1), n_bottom(1), n_bottom(0)
    )
    third = in_grid * relax_row(
        halo_in[1, 0], halo_out[1, 2], halo_in[1, 1], e_bottom(0), n_bottom(0), own(nest_n, last)
    )
    edge_row = relax_row(
        halo_out[1, 2],
        halo_out[1, 1],
        halo_in[1, 0],
        own(nest_e, last),
        own(nest_n, last),
        own(nest_n, last - 1),
    )
    halos[1, 0] = halo_in[1, 0]
    halos[1, 1] = third
    halos[1, 2] = in_grid * relax_row(
        third, edge_row, second, e_bottom(0), n_bottom(0), own(nest_n, last)
    )

    for copy, guard in pending:
        if guard is None:
            copy.wait_send()
        else:
            pl.when(guard)(copy.wait_send)


def finish_kernel(
    group, start, halos, coef, parent, bulk, parent_out, nest_out, bulk_out, held, sems
):
    copies = [
        pltpu.make_async_copy(parent, parent_out, sems.at[0]),
        pltpu.make_async_copy(bulk, bulk_out, sems.at[1]),
    ]
    for copy in copies:
        copy.start()

    def part_copy(at):
        lines = pl.ds(group * at, group)
        return pltpu.make_async_copy(held.at[lines], nest_out.at[lines], sems.at[2 + at])

    def lines_at(at, _):
        lines = [group * at + k for k in range(group)]
        values = [halves_of(start, line) for line in lines]
        for step in range(NSUB):
            for k, line in enumerate(lines):
                values[k] = relax(
                    values[k],
                    halos[0, step, pl.ds(line, 1), :],
                    halos[1, step, pl.ds(line, 1), :],
                    coef,
                )
        for k, line in enumerate(lines):
            for part in range(2):
                held[line, 8 * part : 8 * part + 8] = values[k][part]
        part_copy(at).start()
        return 0

    lax.fori_loop(0, LINES // group, lines_at, 0)
    for copy in copies:
        copy.wait()
    for at in range(LINES // group):
        part_copy(at).wait()


VMEM = pl.BlockSpec(memory_space=pltpu.VMEM)
ANY = pl.BlockSpec(memory_space=pl.ANY)
GROUP = 4
SMEM = pl.BlockSpec(memory_space=pltpu.SMEM)


def step_call(cap, collective, arrays):
    first = cap[0]
    grid = (LINES, ROWS, COLS)
    copies = 3 + 1 + 20 + 8 + 2 + 2 + 4 + 2 + 3 + 2
    shapes = [
        pltpu.VMEM(grid, F32),
        pltpu.VMEM(grid, F32),
        pltpu.VMEM((LEVELS, ROWS, COLS), F32),
        pltpu.VMEM((ROWS, COLS), F32),
        pltpu.VMEM((ROWS, COLS), F32),
        pltpu.VMEM((ROWS, COLS), F32),
        pltpu.VMEM((ROWS, COLS), F32),
        pltpu.VMEM((TILES, ENTRIES), jnp.int32),
        pltpu.VMEM((TILES, ENTRIES), jnp.int32),
        pltpu.VMEM((TILES, ENTRIES), jnp.int32),
        pltpu.VMEM((LEVELS + 1, ROWS, COLS), F32),
        pltpu.VMEM((8, COLS), F32),
        pltpu.VMEM((8, COLS), F32),
        pltpu.VMEM((8, COLS), F32),
        pltpu.VMEM((8, COLS), F32),
        pltpu.VMEM((TILES, ENTRIES), F32),
        pltpu.VMEM((TILES, ENTRIES), F32),
        pltpu.VMEM((2, LINES, first, LANES), F32),
        pltpu.VMEM((LINES, SLOTS, LANES), F32),
        pltpu.VMEM((LINES, SLOTS, LANES), F32),
    ]
    shapes += [pltpu.VMEM((4, LINES, size, LANES), F32) for size in cap]
    shapes += [pltpu.VMEM((NBLK, 4 * size), BF16) for size in cap]
    shapes += [
        pltpu.VMEM((NBLK, SLOTS), BF16),
        pltpu.VMEM((NBLK, NBLK), BF16),
        pltpu.VMEM(grid, F32),
        pltpu.VMEM((LEVELS, ROWS, COLS), F32),
        pltpu.VMEM((3, ROWS, COLS), F32),
        pltpu.VMEM((3, ROWS, COLS), F32),
        pltpu.VMEM((3, ROWS, COLS), F32),
        pltpu.VMEM((2, ROWS, COLS), F32),
        pltpu.VMEM((2, LINES, COLS), F32),
        pltpu.VMEM((2, LINES, COLS), F32),
        pltpu.VMEM((5, ROWS, COLS), F32),
        pltpu.VMEM((LEVELS, ROWS, COLS), F32),
        pltpu.VMEM((3, LEVELS, ROWS, COLS // 4), F32),
        pltpu.VMEM((2, NSUB, LINES, COLS), F32),
        pltpu.VMEM((2, NSUB, LINES, COLS), F32),
        pltpu.SemaphoreType.DMA((copies,)),
        pltpu.SemaphoreType.DMA((copies,)),
        pltpu.SemaphoreType.DMA((10,)),
    ]
    return pl.pallas_call(
        functools.partial(step_kernel, cap),
        out_shape=[
            jax.ShapeDtypeStruct(grid, F32),
            jax.ShapeDtypeStruct((2, NSUB, LINES, COLS), F32),
            jax.ShapeDtypeStruct((5, ROWS, COLS), F32),
            jax.ShapeDtypeStruct(grid, F32),
            jax.ShapeDtypeStruct((LEVELS, ROWS, COLS // 4), F32),
        ],
        in_specs=[ANY] * 10,
        out_specs=[VMEM] * 5,
        scratch_shapes=shapes,
        compiler_params=pltpu.CompilerParams(
            collective_id=collective, has_side_effects=True, vmem_limit_bytes=56 * 1024 * 1024
        ),
    )(*arrays)


def shards(
    parent_field,
    nest_field,
    parent_mixing,
    parent_eastward,
    parent_northward,
    nest_eastward,
    nest_northward,
    strip_tile,
    strip_block,
    strip_target,
    strip_count,
):
    full_shape = parent_field.shape
    grid = (LINES, ROWS, COLS)
    flag, strip_listed = pl.pallas_call(
        plan_kernel,
        out_shape=[
            jax.ShapeDtypeStruct((1,), jnp.int32),
            jax.ShapeDtypeStruct((TILES, ENTRIES), jnp.int32),
        ],
        in_specs=[VMEM, SMEM],
        out_specs=[SMEM, VMEM],
    )(strip_tile, strip_count)
    arrays = (
        parent_field.reshape(grid),
        nest_field.reshape(grid),
        parent_mixing,
        parent_eastward,
        parent_northward,
        nest_eastward,
        nest_northward,
        strip_block,
        strip_target,
        strip_listed,
    )
    states = lax.switch(
        flag[0],
        [
            lambda *a: step_call(SMALL, 3, a),
            lambda *a: step_call(USUAL, 2, a),
            lambda *a: step_call(FULL, 1, a),
        ],
        *arrays,
    )
    parent_adjoint, nest_adjoint, bulk_adjoint = pl.pallas_call(
        functools.partial(finish_kernel, GROUP),
        out_shape=[
            jax.ShapeDtypeStruct(grid, F32),
            jax.ShapeDtypeStruct(grid, F32),
            jax.ShapeDtypeStruct((LEVELS, ROWS, COLS // 4), F32),
        ],
        in_specs=[VMEM] * 5,
        out_specs=[ANY] * 3,
        scratch_shapes=[
            pltpu.VMEM(grid, F32),
            pltpu.SemaphoreType.DMA((2 + LINES // GROUP,)),
        ],
        compiler_params=pltpu.CompilerParams(vmem_limit_bytes=32 * 1024 * 1024),
    )(*states)
    return parent_adjoint.reshape(full_shape), nest_adjoint.reshape(full_shape), bulk_adjoint


def solution(mesh):
    in_specs = (
        P("tag", "lev", "tile", None),
        P("tag", "lev", "tile", None),
        P("lev", "tile", None),
        P("tile", None),
        P("tile", None),
        P("tile", None),
        P("tile", None),
        P(),
        P(),
        P(),
        P(),
    )
    out_specs = (
        P("tag", "lev", "tile", None),
        P("tag", "lev", "tile", None),
        P("lev", "tile", "tag"),
    )
    return jax.shard_map(shards, mesh=mesh, in_specs=in_specs, out_specs=out_specs, check_vma=False)
```

```python
import functools

import jax
import jax.numpy as jnp
from jax import lax
from jax.experimental import pallas as pl
from jax.experimental.pallas import tpu as pltpu
from jax.sharding import PartitionSpec as P

MESH = pl.DeviceIdType.MESH
F32 = jnp.float32
BF16 = jnp.bfloat16
TILES = 16
CHIPS = 8
SLOTS = 16
LINES = 16
LEVELS = 8
ROWS = 16
COLS = 1024
LANES = 128
NBLK = 128
ENTRIES = 256
NSUB = 3
HALF = LINES // 2
PARTS = 1
FULL = (112, 80, 48, 16)
USUAL = (64, 48, 40, 16)
SMALL = (56, 40, 32, 16)


def iota(shape, dim):
    return lax.broadcasted_iota(jnp.int32, shape, dim)


def chip_gap(to_tile, from_tile):
    return ((to_tile >> 1) - (from_tile >> 1)) & (CHIPS - 1)


def way_counts(gap, count):
    half = jnp.floor(count * 0.5)
    up = jnp.where((gap >= 1) & (gap <= 3), count, jnp.where(gap == 4, count - half, 0.0))
    down = jnp.where(gap >= 5, count, jnp.where(gap == 4, half, 0.0))
    return up, down


def way_keys(gap, tile):
    side = tile & 1
    return (4 - gap) * 2 + side, (gap - 4) * 2 + side


def counts_column(count_ref):
    row = iota((TILES, ENTRIES), 0)
    total = jnp.zeros((TILES, ENTRIES), jnp.int32)
    for tile in range(TILES):
        total = jnp.where(row == tile, count_ref[tile], total)
    return total


def plan_kernel(tile_ref, count_ref, flag_ref, listed_ref):
    live = iota((TILES, ENTRIES), 1) < counts_column(count_ref)
    listed = jnp.where(live, tile_ref[...], -1)
    listed_ref[...] = listed
    lane = iota((TILES, LANES), 1)
    count = jnp.zeros((TILES, LANES), F32)
    for source in range(TILES):
        total = jnp.sum(jnp.where(listed == source, 1.0, 0.0), axis=1, keepdims=True)
        count = jnp.where(lane == source, total, count)
    gap = chip_gap(iota((TILES, LANES), 0), lane)
    up, down = way_counts(gap, count)
    small = jnp.zeros((1, LANES), F32)
    usual = jnp.zeros((1, LANES), F32)
    for hop in range(1, 4):
        for load in (jnp.where(gap >= hop, up, 0.0), jnp.where(CHIPS - gap >= hop, down, 0.0)):
            total = jnp.sum(load, axis=0, keepdims=True)
            small = jnp.maximum(small, total - SMALL[hop - 1])
            usual = jnp.maximum(usual, total - USUAL[hop - 1])
    over = jnp.where(small > 0.5, 1.0, 0.0) + jnp.where(usual > 0.5, 1.0, 0.0)
    flag_ref[0] = jnp.max(over).astype(jnp.int32)


def split(value):
    high = value.astype(BF16)
    low = (value - high.astype(F32)).astype(BF16)
    return high, low


def routed(matrix, value):
    high, low = split(value)
    return jnp.dot(matrix, high, preferred_element_type=F32) + jnp.dot(
        matrix, low, preferred_element_type=F32
    )


def onehot_product(left, right):
    return lax.dot_general(left, right, (((1,), (1,)), ((), ())), preferred_element_type=F32)


def blocks_of(ref, line):
    return jnp.concatenate(
        [ref[line, :, LANES * c : LANES * (c + 1)] for c in range(COLS // LANES)], axis=0
    )


def relax(halves, top, bottom, coef):
    row = iota((8, COLS), 0)
    later = [pltpu.roll(x, 1, 0) for x in halves]
    sooner = [pltpu.roll(x, 7, 0) for x in halves]
    above = (jnp.where(row == 0, top, later[0]), jnp.where(row == 0, later[0], later[1]))
    below = (jnp.where(row == 7, sooner[1], sooner[0]), jnp.where(row == 7, bottom, sooner[1]))
    results = []
    for part in range(2):
        x = halves[part]
        rows = slice(8 * part, 8 * part + 8)
        results.append(
            coef[0, rows] * x
            + coef[1, rows] * below[part]
            + coef[2, rows] * above[part]
            + coef[3, rows] * pltpu.roll(x, COLS - 1, 1)
            + coef[4, rows] * pltpu.roll(x, 1, 1)
        )
    return results


def halves_of(ref, line):
    return [ref[line, 0:8, :], ref[line, 8:16, :]]


def coefficients(eastward, northward, north_above):
    col = iota(eastward.shape, 1)
    west = jnp.where(col == 0, 0.0, pltpu.roll(eastward, 1, 1))
    east = jnp.where(col == COLS - 1, 0.0, eastward)
    center = 1.0 - northward - north_above - eastward - west
    return center, northward, north_above, east, west


def relax_row(x, above, below, eastward, northward, north_above):
    wide = x.shape
    center, north, north_up, east, west = coefficients(
        jnp.broadcast_to(eastward, (8, COLS)),
        jnp.broadcast_to(northward, (8, COLS)),
        jnp.broadcast_to(north_above, (8, COLS)),
    )
    center, north, north_up, east, west = (
        jnp.broadcast_to(v[:1], wide) for v in (center, north, north_up, east, west)
    )
    return (
        center * x
        + north * below
        + north_up * above
        + east * pltpu.roll(x, COLS - 1, 1)
        + west * pltpu.roll(x, 1, 1)
    )


def step_kernel(
    cap,
    parent_hbm,
    nest_hbm,
    mixing_hbm,
    parent_e_hbm,
    parent_n_hbm,
    nest_e_hbm,
    nest_n_hbm,
    block_hbm,
    target_hbm,
    listed_hbm,
    start,
    halos,
    nest_coef,
    parent_out,
    bulk_out,
    parent,
    nest,
    mixing,
    parent_e,
    parent_n,
    nest_e,
    nest_n,
    strip_block,
    strip_target,
    strip_listed,
    edges,
    pack_top,
    pack_bottom,
    coef_top,
    coef_bottom,
    slot_of,
    block_of,
    outgoing,
    near_out,
    near_in,
    got1,
    got2,
    got3,
    got4,
    route1,
    route2,
    route3,
    route4,
    route_near,
    route_own,
    solved,
    weight,
    message,
    from_outer,
    from_center,
    from_inner,
    rim_out,
    rim_in,
    parent_coef,
    tag_sum,
    tag_in,
    halo_out,
    halo_in,
    send_sem,
    recv_sem,
    load_sem,
):
    loads = [
        pltpu.make_async_copy(src, dst, load_sem.at[at])
        for at, (src, dst) in enumerate(
            (
                (listed_hbm, strip_listed),
                (block_hbm, strip_block),
                (parent_hbm, parent),
                (mixing_hbm, mixing),
                (nest_e_hbm, nest_e),
                (nest_n_hbm, nest_n),
                (parent_n_hbm, parent_n),
                (parent_e_hbm, parent_e),
                (target_hbm, strip_target),
                (nest_hbm, nest),
            )
        )
    ]
    for copy in loads:
        copy.start()
    got = (None, got1, got2, got3, got4)
    route = (None, route1, route2, route3, route4)
    first = cap[0]
    tile = lax.axis_index("tile")
    lev = lax.axis_index("lev")
    tag = lax.axis_index("tag")
    sibling = tile + 1 - 2 * (tile % 2)
    ring = ((tile + 2) % TILES, (tile + TILES - 2) % TILES)
    tile_up = (tile + 1) % TILES
    tile_down = (tile + TILES - 1) % TILES
    mate = lev + 1 - 2 * (lev % 2)
    across = 3 - lev
    outer = lev % 3 == 0
    inner = lev % 3 != 0
    down = lev // 2

    barrier = pltpu.get_barrier_semaphore()
    peers = [{"tile": t} for t in (tile_up, tile_down) + ring]
    peers += [{"lev": (lev + d) % 4} for d in (1, 2, 3)]
    peers += [{"tag": (tag + d) % 4} for d in (1, 2, 3)]
    for peer in peers:
        pl.semaphore_signal(barrier, inc=1, device_id=peer, device_id_type=MESH)

    used = [0]
    pending = []

    def remote(src, dst, device, guard=None):
        at = used[0]
        used[0] += 1
        copy = pltpu.make_async_remote_copy(
            src_ref=src,
            dst_ref=dst,
            send_sem=send_sem.at[at],
            recv_sem=recv_sem.at[at],
            device_id=device,
            device_id_type=MESH,
        )
        pending.append((copy, guard))
        return copy

    has_above = tile > 0
    has_below = tile < TILES - 1

    loads[0].wait()
    loads[1].wait()
    row = iota((TILES, ENTRIES), 0)
    listed = strip_listed[...]
    mine = jnp.where(listed == tile, 1.0, 0.0)
    upto = jnp.where(
        iota((ENTRIES, ENTRIES), 0) <= iota((ENTRIES, ENTRIES), 1), 1.0, 0.0
    ).astype(BF16)
    rank = jnp.dot(mine.astype(BF16), upto, preferred_element_type=F32) - 1.0
    count = jnp.broadcast_to(jnp.sum(mine, axis=1, keepdims=True), (TILES, ENTRIES))
    gap = chip_gap(row, tile)
    up_count, down_count = way_counts(gap, count)
    up_key, down_key = way_keys(gap, row)
    up_at = jnp.zeros((TILES, ENTRIES), F32)
    down_at = jnp.zeros((TILES, ENTRIES), F32)
    for other in range(TILES):
        up_at += jnp.where(up_key[other : other + 1] < up_key, up_count[other : other + 1], 0.0)
        down_at += jnp.where(
            down_key[other : other + 1] < down_key, down_count[other : other + 1], 0.0
        )
    half = jnp.floor(rank * 0.5)
    odd = rank - 2.0 * half
    goes_up = ((gap >= 1) & (gap <= 3)) | ((gap == 4) & (odd < 0.5))
    goes_down = (gap >= 5) | ((gap == 4) & (odd > 0.5))
    in_row = jnp.where(gap == 4, half, rank)
    slot = jnp.where(
        goes_up,
        up_at + in_row,
        jnp.where(
            goes_down,
            first + down_at + in_row,
            jnp.where((gap == 0) & (row != tile), 2 * first + rank, -1.0),
        ),
    )
    slot_of[...] = jnp.where(mine > 0.5, slot, -1.0)
    blocks = strip_block[...]
    block_of[...] = ((blocks & 7) * ROWS + (blocks >> 3) + 1).astype(F32)

    def gather_matrix(begin, size):
        wanted = (iota((size, ENTRIES), 0) + begin).astype(F32)

        total = jnp.zeros((size, ENTRIES), F32)
        for nest_tile in range(TILES):
            at = slice(nest_tile, nest_tile + 1)
            total = jnp.where(slot_of[at, :] == wanted, block_of[at, :], total)
        index = jnp.sum(total, axis=1, keepdims=True) - 1.0
        return jnp.where(index == iota((size, NBLK), 1).astype(F32), 1.0, 0.0).astype(BF16)

    gather = jnp.concatenate(
        [gather_matrix(0, first), gather_matrix(first, first), gather_matrix(2 * first, SLOTS)],
        axis=0,
    )

    def lines_of(part):
        return pl.ds(HALF * part, HALF)

    def pack(quad, _):
        for pair in (2 * quad, 2 * quad + 1):
            pack_pair(pair)
        return 0

    def pack_pair(pair):
        cells = jnp.concatenate([blocks_of(parent, 2 * pair), blocks_of(parent, 2 * pair + 1)], axis=1)
        taken = routed(gather, cells)
        for side in range(2):
            lanes = slice(LANES * side, LANES * (side + 1))
            outgoing[0, 2 * pair + side] = taken[:first, lanes]
            outgoing[1, 2 * pair + side] = taken[first : 2 * first, lanes]
            near_out[2 * pair + side] = taken[2 * first :, lanes]

    cuts = (0, cap[3], cap[2], cap[1], cap[0])
    hop_copy = {}
    side_copy = {}
    for part in range(PARTS):
        lines = pl.ds(LINES // PARTS * part, LINES // PARTS)
        for hop in range(1, 5):
            src = outgoing if hop == 1 else got[hop - 1]
            for way in range(2):
                for piece in range(5 - hop):
                    slots = pl.ds(cuts[piece], cuts[piece + 1] - cuts[piece])
                    hop_copy[hop, piece, way, part] = remote(
                        src.at[way, lines, slots, :],
                        got[hop].at[way, lines, slots, :],
                        {"tile": ring[way]},
                    )
                side_copy[hop, way, part] = remote(
                    got[hop].at[way, lines], got[hop].at[2 + way, lines], {"tile": sibling}
                )

    def send(part):
        for piece in range(4):
            for way in range(2):
                hop_copy[1, piece, way, part].start()

    loads[2].wait()
    for part in range(PARTS):
        lax.fori_loop(HALF // 2 // PARTS * part, HALF // 2 // PARTS * (part + 1), pack, 0)
        if part == 0:
            pl.semaphore_wait(barrier, len(peers))
        send(part)

    def level(step):
        return step + down * (LEVELS - 1 - 2 * step)

    def field(which, at, rows):
        return parent[which * LEVELS + at, rows, :]

    def sweep(rows, pivot, value0, value1):
        for step in range(LEVELS - 1):
            at = level(step)
            edge = edges[at + 1 - down, rows, :]
            inverse = 1.0 / (pivot + edge)
            ratio = edge * inverse
            carry0 = value0 * inverse
            carry1 = value1 * inverse
            solved[at, rows, :] = carry0
            solved[LEVELS + at, rows, :] = carry1
            weight[at, rows, :] = ratio
            follow = level(step + 1)
            pivot = 1.0 + ratio * pivot
            value0 = field(0, follow, rows) + edge * carry0
            value1 = field(1, follow, rows) + edge * carry1
        message[0, rows, :] = pivot
        message[1, rows, :] = value0
        message[2, rows, :] = value1

    def back(rows, value0, value1):
        at = level(LEVELS - 1)
        solved[at, rows, :] = value0
        solved[LEVELS + at, rows, :] = value1
        for step in range(LEVELS - 2, -1, -1):
            at = level(step)
            ratio = weight[at, rows, :]
            value0 = solved[at, rows, :] + ratio * value0
            value1 = solved[LEVELS + at, rows, :] + ratio * value1
            solved[at, rows, :] = value0
            solved[LEVELS + at, rows, :] = value1

    halves = [pl.ds(0, 8), pl.ds(8, 8)]
    near_level = level(0)
    outer_copy = [
        remote(message.at[:, rows, :], from_outer.at[:, rows, :], {"lev": mate}, outer)
        for rows in halves
    ]
    center_copy = [
        remote(message.at[:, rows, :], from_center.at[:, rows, :], {"lev": across}, inner)
        for rows in halves
    ]
    inner_copy = [
        [
            remote(
                solved.at[which * LEVELS + near_level, rows, :],
                from_inner.at[which, rows, :],
                {"lev": mate},
                inner,
            )
            for which in range(2)
        ]
        for rows in halves
    ]

    for copy in loads[3:4]:
        copy.wait()
    edges[0:LEVELS] = mixing[...]

    @pl.when(lev == 3)
    def _():
        edges[LEVELS] = jnp.zeros((ROWS, COLS), F32)

    edge_copy = remote(edges.at[0], edges.at[LEVELS], {"lev": (lev + 3) % 4}, lev > 0)
    pl.when(lev > 0)(edge_copy.start)

    @pl.when(outer)
    def _():
        for part, rows in enumerate(halves):
            at = level(0)
            sweep(rows, 1.0 + edges[at + down, rows, :], field(0, at, rows), field(1, at, rows))
            outer_copy[part].start()

    for copy in loads[4:7]:
        copy.wait()

    pack_bottom[0:3] = nest_e[ROWS - 3 : ROWS]
    pack_bottom[3:6] = nest_n[ROWS - 3 : ROWS]
    pack_bottom[6:7] = parent_n[ROWS - 1 : ROWS]
    pack_bottom[7:8] = parent_n[ROWS - 1 : ROWS]
    pack_top[0:3] = nest_e[0:3]
    pack_top[3:6] = nest_n[0:3]
    pack_top[6:8] = parent_n[0:2]

    pack_down_copy = remote(pack_bottom, coef_top, {"tile": tile_up}, has_below)
    pl.when(has_below)(pack_down_copy.start)
    pack_up_copy = remote(pack_top, coef_bottom, {"tile": tile_down}, has_above)
    pl.when(has_above)(pack_up_copy.start)
    near_copy = remote(near_out, near_in, {"tile": sibling})
    near_copy.start()

    def relay(hop, *pieces):
        for part in range(PARTS):
            for piece in pieces:
                for way in range(2):
                    hop_copy[hop - 1, piece, way, part].wait_recv()
                    hop_copy[hop, piece, way, part].start()

    def share(hop):
        for part in range(PARTS):
            for way in range(2):
                hop_copy[hop, 4 - hop, way, part].wait_recv()
                side_copy[hop, way, part].start()

    for copy in loads[7:]:
        copy.wait()
    own_tiles = strip_listed[pl.ds(tile, 1), :]
    source_row = iota((TILES, ENTRIES), 0)
    from_source = jnp.where(own_tiles == source_row, 1.0, 0.0)
    own_rank = jnp.sum(
        from_source
        * (jnp.dot(from_source.astype(BF16), upto, preferred_element_type=F32) - 1.0),
        axis=0,
        keepdims=True,
    )
    nest_column = iota((TILES, 1), 0)

    def offsets(source, totals):
        up_total, down_total = totals
        count = jnp.sum(jnp.where(listed == source, 1.0, 0.0), axis=1, keepdims=True)
        gap = chip_gap(nest_column, source)
        up, down_ = way_counts(gap, count)
        up_key, down_key = way_keys(gap, nest_column)
        own_up, own_down = way_keys(chip_gap(tile, source), tile)
        up_here = jnp.sum(jnp.where(up_key < own_up, up, 0.0), axis=0, keepdims=True)
        down_here = jnp.sum(jnp.where(down_key < own_down, down_, 0.0), axis=0, keepdims=True)
        here = own_tiles == source
        return (
            up_total + jnp.where(here, up_here, 0.0),
            down_total + jnp.where(here, down_here, 0.0),
        )

    nothing = jnp.zeros((1, ENTRIES), F32)
    up_start, down_start = lax.fori_loop(0, TILES, offsets, (nothing, nothing))
    own_gap = jnp.where(own_tiles >= 0, chip_gap(tile, own_tiles), -1)
    own_half = jnp.floor(own_rank * 0.5)
    own_odd = own_rank - 2.0 * own_half
    comes_up = ((own_gap >= 1) & (own_gap <= 3)) | ((own_gap == 4) & (own_odd < 0.5))
    place = jnp.where(own_gap == 4, own_half, own_rank) + jnp.where(comes_up, up_start, down_start)
    hops = jnp.where(own_gap >= 1, jnp.where(comes_up, own_gap, CHIPS - own_gap), 0)
    group = jnp.where((own_tiles & 1) == (tile & 1), 0.0, 2.0) + jnp.where(comes_up, 0.0, 1.0)
    targets = strip_target[pl.ds(tile, 1), :]
    targets = jnp.where(own_tiles >= 0, (targets & 7) * ROWS + (targets >> 3), -1)
    lands = jnp.where(targets == iota((NBLK, ENTRIES), 0), 1.0, 0.0).astype(BF16)

    def picks(place, rows):
        return jnp.where(place == iota((rows, ENTRIES), 0).astype(F32), 1.0, 0.0).astype(BF16)

    for hop in range(1, 5):
        size = cap[hop - 1]
        at = jnp.where(hops == hop, group * size + place, -1.0)
        route[hop][...] = onehot_product(lands, picks(at, 4 * size)).astype(BF16)
    at = jnp.where((own_gap == 0) & (own_tiles != tile), own_rank, -1.0)
    route_near[...] = onehot_product(lands, picks(at, SLOTS)).astype(BF16)
    own_blocks = strip_block[pl.ds(tile, 1), :]
    own_blocks = jnp.where(own_tiles == tile, (own_blocks & 7) * ROWS + (own_blocks >> 3), -1)
    route_own[...] = onehot_product(lands, picks(own_blocks.astype(F32), NBLK)).astype(BF16)

    pl.when(lev < 3)(edge_copy.wait_recv)

    @pl.when(inner)
    def _():
        for part, rows in enumerate(halves):
            at = level(0)
            outer_copy[part].wait_recv()
            edge = edges[at + down, rows, :]
            pivot = from_outer[0, rows, :]
            ratio = edge / (pivot + edge)
            sweep(
                rows,
                1.0 + ratio * pivot,
                field(0, at, rows) + ratio * from_outer[1, rows, :],
                field(1, at, rows) + ratio * from_outer[2, rows, :],
            )
            center_copy[part].start()

    relay(2, 0, 1)

    @pl.when(inner)
    def _():
        for part, rows in enumerate(halves):
            center_copy[part].wait_recv()
            at = level(LEVELS - 1)
            edge = edges[at + 1 - down, rows, :]
            pivot = from_center[0, rows, :]
            ratio = edge / (pivot + edge)
            inverse = 1.0 / (message[0, rows, :] + ratio * pivot)
            value0 = (message[1, rows, :] + ratio * from_center[1, rows, :]) * inverse
            value1 = (message[2, rows, :] + ratio * from_center[2, rows, :]) * inverse
            back(rows, value0, value1)
            for copy in inner_copy[part]:
                copy.start()

    @pl.when(has_above)
    def _():
        pack_down_copy.wait_recv()

    @pl.when(has_below)
    def _():
        pack_up_copy.wait_recv()

    @pl.when(tile == 0)
    def _():
        coef_top[...] = jnp.zeros((8, COLS), F32)

    @pl.when(tile == TILES - 1)
    def _():
        coef_bottom[...] = jnp.zeros((8, COLS), F32)

    cell_row = iota((ROWS, COLS), 0)
    for target, e_ref, n_ref, above in (
        (parent_coef, parent_e, parent_n, coef_top[6:7]),
        (nest_coef, nest_e, nest_n, coef_top[5:6]),
    ):
        northward = n_ref[...]
        north_above = jnp.where(cell_row == 0, above, pltpu.roll(northward, 1, 0))
        for which, value in enumerate(coefficients(e_ref[...], northward, north_above)):
            target[which] = value

    relay(2, 2)

    @pl.when(outer)
    def _():
        for part, rows in enumerate(halves):
            for copy in inner_copy[part]:
                copy.wait_recv()
            edge = edges[level(LEVELS - 1) + 1 - down, rows, :]
            inverse = 1.0 / (message[0, rows, :] + edge)
            back(
                rows,
                (message[1, rows, :] + edge * from_inner[0, rows, :]) * inverse,
                (message[2, rows, :] + edge * from_inner[1, rows, :]) * inverse,
            )

    for line in range(LINES):
        rim_out[0, line : line + 1] = solved[line, 0:1, :]
        rim_out[1, line : line + 1] = solved[line, ROWS - 1 : ROWS, :]
    rim_up = remote(rim_out.at[0], rim_in.at[1], {"tile": tile_down}, has_above)
    rim_down = remote(rim_out.at[1], rim_in.at[0], {"tile": tile_up}, has_below)
    pl.when(has_above)(rim_up.start)
    pl.when(has_below)(rim_down.start)

    share(1)

    near_copy.wait_recv()

    def add_blocks(line, taken):
        for c in range(COLS // LANES):
            start[line, :, LANES * c : LANES * (c + 1)] += taken[ROWS * c : ROWS * (c + 1)]

    def scatter_near(pair, _):
        cells = jnp.concatenate([blocks_of(parent, 2 * pair), blocks_of(parent, 2 * pair + 1)], axis=1)
        near = jnp.concatenate([near_in[2 * pair], near_in[2 * pair + 1]], axis=1)
        taken = routed(route_own[...], cells) + routed(route_near[...], near)
        for side in range(2):
            line = 2 * pair + side
            start[line] = nest[line]
            add_blocks(line, taken[:, LANES * side : LANES * (side + 1)])
        return 0

    lax.fori_loop(0, LINES // 2, scatter_near, 0)

    def scatter(hop, part):
        if part < PARTS:
            for way in range(2):
                side_copy[hop, way, part].wait_recv()

        def one(quad, _):
            for pair in (2 * quad, 2 * quad + 1):
                one_pair(pair)
            return 0

        def one_pair(pair):
            cells = jnp.concatenate(
                [
                    jnp.concatenate([got[hop][g, 2 * pair + side] for g in range(4)], axis=0)
                    for side in range(2)
                ],
                axis=1,
            )
            taken = routed(route[hop][...], cells)
            for side in range(2):
                add_blocks(2 * pair + side, taken[:, LANES * side : LANES * (side + 1)])

        lax.fori_loop(HALF // 4 * part, HALF // 4 * (part + 1), one, 0)

    relay(3, 0, 1)

    share(2)
    scatter(1, 0)
    scatter(1, 1)
    relay(4, 0)
    share(3)
    pl.when(has_above)(rim_down.wait_recv)
    pl.when(has_below)(rim_up.wait_recv)

    @pl.when(tile == 0)
    def _():
        rim_in[0] = jnp.zeros((LINES, COLS), F32)

    @pl.when(tile == TILES - 1)
    def _():
        rim_in[1] = jnp.zeros((LINES, COLS), F32)

    def parent_level(at, _):
        results = []
        for which in range(2):
            line = which * LEVELS + at
            results.append(
                relax(
                    halves_of(solved, line),
                    rim_in[0, pl.ds(line, 1), :],
                    rim_in[1, pl.ds(line, 1), :],
                    parent_coef,
                )
            )
            for part in range(2):
                parent_out[line, 8 * part : 8 * part + 8] = results[which][part]
        for part in range(2):
            tag_sum[at, 8 * part : 8 * part + 8] = results[0][part] + results[1][part]
        return 0

    lax.fori_loop(0, LEVELS, parent_level, 0)

    quarter = COLS // 4

    def columns(which):
        return pl.ds(pl.multiple_of(which * quarter, quarter), quarter)

    tag_copy = []
    for d in (1, 2, 3):
        to = (tag + d) % 4
        copy = remote(tag_sum.at[:, :, columns(to)], tag_in.at[d - 1], {"tag": to})
        copy.start()
        tag_copy.append(copy)

    halo_up = []
    halo_down = []
    for part in range(2):
        lines = lines_of(part)
        halo_up.append(
            remote(
                halo_out.at[0, :, lines, :],
                halo_in.at[1, :, lines, :],
                {"tile": tile_down},
                has_above,
            )
        )
        halo_down.append(
            remote(
                halo_out.at[1, :, lines, :],
                halo_in.at[0, :, lines, :],
                {"tile": tile_up},
                has_below,
            )
        )

    def send_halo(part):
        for line in range(HALF * part, HALF * (part + 1)):
            for r in range(NSUB):
                halo_out[0, r, line : line + 1] = start[line, r : r + 1, :]
                at = ROWS - NSUB + r
                halo_out[1, r, line : line + 1] = start[line, at : at + 1, :]
        pl.when(has_above)(halo_up[part].start)
        pl.when(has_below)(halo_down[part].start)

    in_grid = jnp.where(has_below, 1.0, 0.0)

    def e_top(r):
        return coef_top[r : r + 1]

    def n_top(r):
        return coef_top[3 + r : 4 + r]

    def e_bottom(r):
        return coef_bottom[r : r + 1]

    def n_bottom(r):
        return coef_bottom[3 + r : 4 + r]

    def own(ref, r):
        return ref[r : r + 1]

    def receive_halo(part):
        lines = slice(HALF * part, HALF * (part + 1))
        pl.when(has_above)(halo_down[part].wait_recv)
        pl.when(has_below)(halo_up[part].wait_recv)

        @pl.when(tile == 0)
        def _():
            halo_in[0, :, lines] = jnp.zeros((NSUB, HALF, COLS), F32)

        @pl.when(tile == TILES - 1)
        def _():
            halo_in[1, :, lines] = jnp.zeros((NSUB, HALF, COLS), F32)

        far, mid, close = (halo_in[0, r, lines] for r in range(3))
        inner0, inner1 = (halo_out[0, r, lines] for r in range(2))
        second = relax_row(mid, far, close, e_top(1), n_top(1), n_top(0))
        third = relax_row(close, mid, inner0, e_top(2), n_top(2), n_top(1))
        edge_row = relax_row(inner0, close, inner1, own(nest_e, 0), own(nest_n, 0), n_top(2))
        halos[0, 0, lines] = close
        halos[0, 1, lines] = third
        halos[0, 2, lines] = relax_row(third, second, edge_row, e_top(2), n_top(2), n_top(1))
        last = ROWS - 1
        close, mid, far = (halo_in[1, r, lines] for r in range(3))
        inner1, inner0 = (halo_out[1, r, lines] for r in (1, 2))
        second = relax_row(mid, close, far, e_bottom(1), n_bottom(1), n_bottom(0))
        third = in_grid * relax_row(
            close, inner0, mid, e_bottom(0), n_bottom(0), own(nest_n, last)
        )
        edge_row = relax_row(
            inner0, inner1, close, own(nest_e, last), own(nest_n, last), own(nest_n, last - 1)
        )
        halos[1, 0, lines] = close
        halos[1, 1, lines] = third
        halos[1, 2, lines] = in_grid * relax_row(
            third, edge_row, second, e_bottom(0), n_bottom(0), own(nest_n, last)
        )

    scatter(2, 0)
    scatter(2, 1)
    share(4)
    scatter(3, 0)
    scatter(4, 0)
    send_halo(0)
    scatter(3, 1)
    scatter(4, 1)
    send_halo(1)
    receive_halo(0)

    def first_lines(at, _):
        sub_steps(start, [GROUP * at + k for k in range(GROUP)], start, halos, nest_coef)
        return 0

    lax.fori_loop(0, HALF // GROUP, first_lines, 0)
    for copy in tag_copy:
        copy.wait_recv()
    bulk_out[...] = tag_sum[:, :, columns(tag)] + tag_in[0] + tag_in[1] + tag_in[2]
    receive_halo(1)

    for copy, guard in pending:
        if guard is None:
            copy.wait_send()
        else:
            pl.when(guard)(copy.wait_send)


GROUP = 4


def sub_steps(start, lines, result, halos, coef):
    values = [halves_of(start, line) for line in lines]
    for step in range(NSUB):
        for k, line in enumerate(lines):
            values[k] = relax(
                values[k],
                halos[0, step, pl.ds(line, 1), :],
                halos[1, step, pl.ds(line, 1), :],
                coef,
            )
    for k, line in enumerate(lines):
        for part in range(2):
            result[line, 8 * part : 8 * part + 8] = values[k][part]


def finish_kernel(start, halos, coef, parent, bulk, parent_out, nest_out, bulk_out, held, sems):
    ready = pl.ds(0, HALF)
    copies = [
        pltpu.make_async_copy(parent, parent_out, sems.at[0]),
        pltpu.make_async_copy(start.at[ready], nest_out.at[ready], sems.at[1]),
        pltpu.make_async_copy(bulk, bulk_out, sems.at[2]),
    ]
    for copy in copies:
        copy.start()

    def part_copy(at):
        lines = pl.ds(GROUP * at, GROUP)
        return pltpu.make_async_copy(held.at[lines], nest_out.at[lines], sems.at[3 + at])

    def lines_at(at, _):
        sub_steps(start, [GROUP * at + k for k in range(GROUP)], held, halos, coef)
        part_copy(at).start()
        return 0

    lax.fori_loop(HALF // GROUP, LINES // GROUP, lines_at, 0)
    for copy in copies:
        copy.wait()
    for at in range(HALF // GROUP, LINES // GROUP):
        part_copy(at).wait()


VMEM = pl.BlockSpec(memory_space=pltpu.VMEM)
ANY = pl.BlockSpec(memory_space=pl.ANY)
SMEM = pl.BlockSpec(memory_space=pltpu.SMEM)


def step_call(cap, collective, arrays):
    first = cap[0]
    grid = (LINES, ROWS, COLS)
    copies = 3 + 1 + 28 * PARTS + 2 + 2 + 4 + 2 + 3 + 4
    shapes = [
        pltpu.VMEM(grid, F32),
        pltpu.VMEM(grid, F32),
        pltpu.VMEM((LEVELS, ROWS, COLS), F32),
        pltpu.VMEM((ROWS, COLS), F32),
        pltpu.VMEM((ROWS, COLS), F32),
        pltpu.VMEM((ROWS, COLS), F32),
        pltpu.VMEM((ROWS, COLS), F32),
        pltpu.VMEM((TILES, ENTRIES), jnp.int32),
        pltpu.VMEM((TILES, ENTRIES), jnp.int32),
        pltpu.VMEM((TILES, ENTRIES), jnp.int32),
        pltpu.VMEM((LEVELS + 1, ROWS, COLS), F32),
        pltpu.VMEM((8, COLS), F32),
        pltpu.VMEM((8, COLS), F32),
        pltpu.VMEM((8, COLS), F32),
        pltpu.VMEM((8, COLS), F32),
        pltpu.VMEM((TILES, ENTRIES), F32),
        pltpu.VMEM((TILES, ENTRIES), F32),
        pltpu.VMEM((2, LINES, first, LANES), F32),
        pltpu.VMEM((LINES, SLOTS, LANES), F32),
        pltpu.VMEM((LINES, SLOTS, LANES), F32),
    ]
    shapes += [pltpu.VMEM((4, LINES, size, LANES), F32) for size in cap]
    shapes += [pltpu.VMEM((NBLK, 4 * size), BF16) for size in cap]
    shapes += [
        pltpu.VMEM((NBLK, SLOTS), BF16),
        pltpu.VMEM((NBLK, NBLK), BF16),
        pltpu.VMEM(grid, F32),
        pltpu.VMEM((LEVELS, ROWS, COLS), F32),
        pltpu.VMEM((3, ROWS, COLS), F32),
        pltpu.VMEM((3, ROWS, COLS), F32),
        pltpu.VMEM((3, ROWS, COLS), F32),
        pltpu.VMEM((2, ROWS, COLS), F32),
        pltpu.VMEM((2, LINES, COLS), F32),
        pltpu.VMEM((2, LINES, COLS), F32),
        pltpu.VMEM((5, ROWS, COLS), F32),
        pltpu.VMEM((LEVELS, ROWS, COLS), F32),
        pltpu.VMEM((3, LEVELS, ROWS, COLS // 4), F32),
        pltpu.VMEM((2, NSUB, LINES, COLS), F32),
        pltpu.VMEM((2, NSUB, LINES, COLS), F32),
        pltpu.SemaphoreType.DMA((copies,)),
        pltpu.SemaphoreType.DMA((copies,)),
        pltpu.SemaphoreType.DMA((10,)),
    ]
    return pl.pallas_call(
        functools.partial(step_kernel, cap),
        out_shape=[
            jax.ShapeDtypeStruct(grid, F32),
            jax.ShapeDtypeStruct((2, NSUB, LINES, COLS), F32),
            jax.ShapeDtypeStruct((5, ROWS, COLS), F32),
            jax.ShapeDtypeStruct(grid, F32),
            jax.ShapeDtypeStruct((LEVELS, ROWS, COLS // 4), F32),
        ],
        in_specs=[ANY] * 10,
        out_specs=[VMEM] * 5,
        scratch_shapes=shapes,
        compiler_params=pltpu.CompilerParams(
            collective_id=collective, has_side_effects=True, vmem_limit_bytes=56 * 1024 * 1024
        ),
    )(*arrays)


def shards(
    parent_field,
    nest_field,
    parent_mixing,
    parent_eastward,
    parent_northward,
    nest_eastward,
    nest_northward,
    strip_tile,
    strip_block,
    strip_target,
    strip_count,
):
    full_shape = parent_field.shape
    grid = (LINES, ROWS, COLS)
    flag, strip_listed = pl.pallas_call(
        plan_kernel,
        out_shape=[
            jax.ShapeDtypeStruct((1,), jnp.int32),
            jax.ShapeDtypeStruct((TILES, ENTRIES), jnp.int32),
        ],
        in_specs=[VMEM, SMEM],
        out_specs=[SMEM, VMEM],
    )(strip_tile, strip_count)
    arrays = (
        parent_field.reshape(grid),
        nest_field.reshape(grid),
        parent_mixing,
        parent_eastward,
        parent_northward,
        nest_eastward,
        nest_northward,
        strip_block,
        strip_target,
        strip_listed,
    )
    states = lax.switch(
        flag[0],
        [
            lambda *a: step_call(SMALL, 3, a),
            lambda *a: step_call(USUAL, 2, a),
            lambda *a: step_call(FULL, 1, a),
        ],
        *arrays,
    )
    parent_adjoint, nest_adjoint, bulk_adjoint = pl.pallas_call(
        finish_kernel,
        out_shape=[
            jax.ShapeDtypeStruct(grid, F32),
            jax.ShapeDtypeStruct(grid, F32),
            jax.ShapeDtypeStruct((LEVELS, ROWS, COLS // 4), F32),
        ],
        in_specs=[VMEM] * 5,
        out_specs=[ANY] * 3,
        scratch_shapes=[
            pltpu.VMEM(grid, F32),
            pltpu.SemaphoreType.DMA((3 + LINES // GROUP,)),
        ],
        compiler_params=pltpu.CompilerParams(vmem_limit_bytes=32 * 1024 * 1024),
    )(*states)
    return parent_adjoint.reshape(full_shape), nest_adjoint.reshape(full_shape), bulk_adjoint


def solution(mesh):
    in_specs = (
        P("tag", "lev", "tile", None),
        P("tag", "lev", "tile", None),
        P("lev", "tile", None),
        P("tile", None),
        P("tile", None),
        P("tile", None),
        P("tile", None),
        P(),
        P(),
        P(),
        P(),
    )
    out_specs = (
        P("tag", "lev", "tile", None),
        P("tag", "lev", "tile", None),
        P("lev", "tile", "tag"),
    )
    return jax.shard_map(shards, mesh=mesh, in_specs=in_specs, out_specs=out_specs, check_vma=False)
```

```python
import functools

import jax
import jax.numpy as jnp
from jax import lax
from jax.experimental import pallas as pl
from jax.experimental.pallas import tpu as pltpu
from jax.sharding import PartitionSpec as P

MESH = pl.DeviceIdType.MESH
F32 = jnp.float32
BF16 = jnp.bfloat16
TILES = 16
CHIPS = 8
SLOTS = 16
LINES = 16
LEVELS = 8
ROWS = 16
COLS = 1024
LANES = 128
NBLK = 128
ENTRIES = 256
NSUB = 3
HALF = LINES // 2
PARTS = 1
SIZES = ((48, 40, 32, 16), (56, 40, 32, 16), (64, 48, 40, 16), (112, 80, 48, 16))


def iota(shape, dim):
    return lax.broadcasted_iota(jnp.int32, shape, dim)


def chip_gap(to_tile, from_tile):
    return ((to_tile >> 1) - (from_tile >> 1)) & (CHIPS - 1)


def way_counts(gap, count):
    half = jnp.floor(count * 0.5)
    up = jnp.where((gap >= 1) & (gap <= 3), count, jnp.where(gap == 4, count - half, 0.0))
    down = jnp.where(gap >= 5, count, jnp.where(gap == 4, half, 0.0))
    return up, down


def way_keys(gap, tile):
    side = tile & 1
    return (4 - gap) * 2 + side, (gap - 4) * 2 + side


def counts_column(count_ref):
    row = iota((TILES, ENTRIES), 0)
    total = jnp.zeros((TILES, ENTRIES), jnp.int32)
    for tile in range(TILES):
        total = jnp.where(row == tile, count_ref[tile], total)
    return total


def plan_kernel(tile_ref, block_ref, target_ref, count_ref, flag_ref, lists_ref):
    live = iota((TILES, ENTRIES), 1) < counts_column(count_ref)
    listed = jnp.where(live, tile_ref[...], -1)
    lists_ref[0] = listed
    lists_ref[1] = block_ref[...]
    lists_ref[2] = target_ref[...]
    lane = iota((TILES, LANES), 1)
    count = jnp.zeros((TILES, LANES), F32)
    for source in range(TILES):
        total = jnp.sum(jnp.where(listed == source, 1.0, 0.0), axis=1, keepdims=True)
        count = jnp.where(lane == source, total, count)
    gap = chip_gap(iota((TILES, LANES), 0), lane)
    up, down = way_counts(gap, count)
    loads = []
    for hop in range(1, 4):
        for load in (jnp.where(gap >= hop, up, 0.0), jnp.where(CHIPS - gap >= hop, down, 0.0)):
            loads.append((hop, jnp.sum(load, axis=0, keepdims=True)))
    over = jnp.zeros((1, LANES), F32)
    for size in SIZES[:-1]:
        excess = functools.reduce(jnp.maximum, [load - size[hop - 1] for hop, load in loads])
        over += jnp.where(excess > 0.5, 1.0, 0.0)
    flag_ref[0] = jnp.max(over).astype(jnp.int32)


def split(value):
    high = value.astype(BF16)
    low = (value - high.astype(F32)).astype(BF16)
    return high, low


def routed(matrix, value):
    high, low = split(value)
    return jnp.dot(matrix, high, preferred_element_type=F32) + jnp.dot(
        matrix, low, preferred_element_type=F32
    )


def onehot_product(left, right):
    return lax.dot_general(left, right, (((1,), (1,)), ((), ())), preferred_element_type=F32)


def blocks_of(ref, line):
    return jnp.concatenate(
        [ref[line, :, LANES * c : LANES * (c + 1)] for c in range(COLS // LANES)], axis=0
    )


def relax(halves, top, bottom, coef):
    row = iota((8, COLS), 0)
    later = [pltpu.roll(x, 1, 0) for x in halves]
    sooner = [pltpu.roll(x, 7, 0) for x in halves]
    above = (jnp.where(row == 0, top, later[0]), jnp.where(row == 0, later[0], later[1]))
    below = (jnp.where(row == 7, sooner[1], sooner[0]), jnp.where(row == 7, bottom, sooner[1]))
    results = []
    for part in range(2):
        x = halves[part]
        rows = slice(8 * part, 8 * part + 8)
        results.append(
            coef[0, rows] * x
            + coef[1, rows] * below[part]
            + coef[2, rows] * above[part]
            + coef[3, rows] * pltpu.roll(x, COLS - 1, 1)
            + coef[4, rows] * pltpu.roll(x, 1, 1)
        )
    return results


def halves_of(ref, line):
    return [ref[line, 0:8, :], ref[line, 8:16, :]]


def coefficients(eastward, northward, north_above):
    col = iota(eastward.shape, 1)
    west = jnp.where(col == 0, 0.0, pltpu.roll(eastward, 1, 1))
    east = jnp.where(col == COLS - 1, 0.0, eastward)
    center = 1.0 - northward - north_above - eastward - west
    return center, northward, north_above, east, west


def relax_row(x, above, below, eastward, northward, north_above):
    wide = x.shape
    center, north, north_up, east, west = coefficients(
        jnp.broadcast_to(eastward, (8, COLS)),
        jnp.broadcast_to(northward, (8, COLS)),
        jnp.broadcast_to(north_above, (8, COLS)),
    )
    center, north, north_up, east, west = (
        jnp.broadcast_to(v[:1], wide) for v in (center, north, north_up, east, west)
    )
    return (
        center * x
        + north * below
        + north_up * above
        + east * pltpu.roll(x, COLS - 1, 1)
        + west * pltpu.roll(x, 1, 1)
    )


def step_kernel(
    cap,
    parent_hbm,
    nest_hbm,
    mixing_hbm,
    parent_e_hbm,
    parent_n_hbm,
    nest_e_hbm,
    nest_n_hbm,
    lists,
    start,
    halos,
    nest_coef,
    parent_out,
    bulk_out,
    parent,
    nest,
    mixing,
    parent_e,
    parent_n,
    nest_e,
    nest_n,
    edges,
    pack_top,
    pack_bottom,
    coef_top,
    coef_bottom,
    slot_of,
    block_of,
    outgoing,
    near_out,
    near_in,
    got1,
    got2,
    got3,
    got4,
    route1,
    route2,
    route3,
    route4,
    route_near,
    route_own,
    solved,
    weight,
    message,
    from_outer,
    from_center,
    from_inner,
    rim_out,
    rim_in,
    parent_coef,
    tag_sum,
    tag_in,
    halo_out,
    halo_in,
    send_sem,
    recv_sem,
    load_sem,
):
    loads = [
        pltpu.make_async_copy(src, dst, load_sem.at[at])
        for at, (src, dst) in enumerate(
            (
                (parent_hbm, parent),
                (mixing_hbm, mixing),
                (nest_e_hbm, nest_e),
                (nest_n_hbm, nest_n),
                (parent_n_hbm, parent_n),
                (parent_e_hbm, parent_e),
                (nest_hbm, nest),
            )
        )
    ]
    for copy in loads:
        copy.start()
    strip_listed, strip_block, strip_target = (lists.at[which] for which in range(3))
    got = (None, got1, got2, got3, got4)
    route = (None, route1, route2, route3, route4)
    first = cap[0]
    tile = lax.axis_index("tile")
    lev = lax.axis_index("lev")
    tag = lax.axis_index("tag")
    sibling = tile + 1 - 2 * (tile % 2)
    ring = ((tile + 2) % TILES, (tile + TILES - 2) % TILES)
    tile_up = (tile + 1) % TILES
    tile_down = (tile + TILES - 1) % TILES
    mate = lev + 1 - 2 * (lev % 2)
    across = 3 - lev
    outer = lev % 3 == 0
    inner = lev % 3 != 0
    down = lev // 2

    barrier = pltpu.get_barrier_semaphore()
    peers = [{"tile": t} for t in (tile_up, tile_down) + ring]
    peers += [{"lev": (lev + d) % 4} for d in (1, 2, 3)]
    peers += [{"tag": (tag + d) % 4} for d in (1, 2, 3)]
    for peer in peers:
        pl.semaphore_signal(barrier, inc=1, device_id=peer, device_id_type=MESH)

    used = [0]
    pending = []

    def remote(src, dst, device, guard=None):
        at = used[0]
        used[0] += 1
        copy = pltpu.make_async_remote_copy(
            src_ref=src,
            dst_ref=dst,
            send_sem=send_sem.at[at],
            recv_sem=recv_sem.at[at],
            device_id=device,
            device_id_type=MESH,
        )
        pending.append((copy, guard))
        return copy

    has_above = tile > 0
    has_below = tile < TILES - 1

    row = iota((TILES, ENTRIES), 0)
    listed = strip_listed[...]
    mine = jnp.where(listed == tile, 1.0, 0.0)
    upto = jnp.where(
        iota((ENTRIES, ENTRIES), 0) <= iota((ENTRIES, ENTRIES), 1), 1.0, 0.0
    ).astype(BF16)
    rank = jnp.dot(mine.astype(BF16), upto, preferred_element_type=F32) - 1.0
    count = jnp.broadcast_to(jnp.sum(mine, axis=1, keepdims=True), (TILES, ENTRIES))
    gap = chip_gap(row, tile)
    up_count, down_count = way_counts(gap, count)
    up_key, down_key = way_keys(gap, row)
    up_at = jnp.zeros((TILES, ENTRIES), F32)
    down_at = jnp.zeros((TILES, ENTRIES), F32)
    for other in range(TILES):
        up_at += jnp.where(up_key[other : other + 1] < up_key, up_count[other : other + 1], 0.0)
        down_at += jnp.where(
            down_key[other : other + 1] < down_key, down_count[other : other + 1], 0.0
        )
    half = jnp.floor(rank * 0.5)
    odd = rank - 2.0 * half
    goes_up = ((gap >= 1) & (gap <= 3)) | ((gap == 4) & (odd < 0.5))
    goes_down = (gap >= 5) | ((gap == 4) & (odd > 0.5))
    in_row = jnp.where(gap == 4, half, rank)
    slot = jnp.where(
        goes_up,
        up_at + in_row,
        jnp.where(
            goes_down,
            first + down_at + in_row,
            jnp.where((gap == 0) & (row != tile), 2 * first + rank, -1.0),
        ),
    )
    slot_of[...] = jnp.where(mine > 0.5, slot, -1.0)
    blocks = strip_block[...]
    block_of[...] = ((blocks & 7) * ROWS + (blocks >> 3) + 1).astype(F32)

    def gather_matrix(begin, size):
        wanted = (iota((size, ENTRIES), 0) + begin).astype(F32)

        total = jnp.zeros((size, ENTRIES), F32)
        for nest_tile in range(TILES):
            at = slice(nest_tile, nest_tile + 1)
            total = jnp.where(slot_of[at, :] == wanted, block_of[at, :], total)
        index = jnp.sum(total, axis=1, keepdims=True) - 1.0
        return jnp.where(index == iota((size, NBLK), 1).astype(F32), 1.0, 0.0).astype(BF16)

    gather = jnp.concatenate(
        [gather_matrix(0, first), gather_matrix(first, first), gather_matrix(2 * first, SLOTS)],
        axis=0,
    )

    def lines_of(part):
        return pl.ds(HALF * part, HALF)

    def pack(quad, _):
        for pair in (2 * quad, 2 * quad + 1):
            pack_pair(pair)
        return 0

    def pack_pair(pair):
        cells = jnp.concatenate([blocks_of(parent, 2 * pair), blocks_of(parent, 2 * pair + 1)], axis=1)
        taken = routed(gather, cells)
        for side in range(2):
            lanes = slice(LANES * side, LANES * (side + 1))
            outgoing[0, 2 * pair + side] = taken[:first, lanes]
            outgoing[1, 2 * pair + side] = taken[first : 2 * first, lanes]
            near_out[2 * pair + side] = taken[2 * first :, lanes]

    cuts = (0, cap[3], cap[2], cap[1], cap[0])
    hop_copy = {}
    side_copy = {}
    for part in range(PARTS):
        lines = pl.ds(LINES // PARTS * part, LINES // PARTS)
        for hop in range(1, 5):
            src = outgoing if hop == 1 else got[hop - 1]
            for way in range(2):
                for piece in range(5 - hop):
                    slots = pl.ds(cuts[piece], cuts[piece + 1] - cuts[piece])
                    hop_copy[hop, piece, way, part] = remote(
                        src.at[way, lines, slots, :],
                        got[hop].at[way, lines, slots, :],
                        {"tile": ring[way]},
                    )
                side_copy[hop, way, part] = remote(
                    got[hop].at[way, lines], got[hop].at[2 + way, lines], {"tile": sibling}
                )

    def send(part):
        for piece in range(4):
            for way in range(2):
                hop_copy[1, piece, way, part].start()

    loads[0].wait()
    for part in range(PARTS):
        lax.fori_loop(HALF // 2 // PARTS * part, HALF // 2 // PARTS * (part + 1), pack, 0)
        if part == 0:
            pl.semaphore_wait(barrier, len(peers))
        send(part)

    def level(step):
        return step + down * (LEVELS - 1 - 2 * step)

    def field(which, at, rows):
        return parent[which * LEVELS + at, rows, :]

    def sweep(rows, pivot, value0, value1):
        for step in range(LEVELS - 1):
            at = level(step)
            edge = edges[at + 1 - down, rows, :]
            inverse = 1.0 / (pivot + edge)
            ratio = edge * inverse
            carry0 = value0 * inverse
            carry1 = value1 * inverse
            solved[at, rows, :] = carry0
            solved[LEVELS + at, rows, :] = carry1
            weight[at, rows, :] = ratio
            follow = level(step + 1)
            pivot = 1.0 + ratio * pivot
            value0 = field(0, follow, rows) + edge * carry0
            value1 = field(1, follow, rows) + edge * carry1
        message[0, rows, :] = pivot
        message[1, rows, :] = value0
        message[2, rows, :] = value1

    def back(rows, value0, value1):
        at = level(LEVELS - 1)
        solved[at, rows, :] = value0
        solved[LEVELS + at, rows, :] = value1
        for step in range(LEVELS - 2, -1, -1):
            at = level(step)
            ratio = weight[at, rows, :]
            value0 = solved[at, rows, :] + ratio * value0
            value1 = solved[LEVELS + at, rows, :] + ratio * value1
            solved[at, rows, :] = value0
            solved[LEVELS + at, rows, :] = value1

    halves = [pl.ds(0, 8), pl.ds(8, 8)]
    near_level = level(0)
    outer_copy = [
        remote(message.at[:, rows, :], from_outer.at[:, rows, :], {"lev": mate}, outer)
        for rows in halves
    ]
    center_copy = [
        remote(message.at[:, rows, :], from_center.at[:, rows, :], {"lev": across}, inner)
        for rows in halves
    ]
    inner_copy = [
        [
            remote(
                solved.at[which * LEVELS + near_level, rows, :],
                from_inner.at[which, rows, :],
                {"lev": mate},
                inner,
            )
            for which in range(2)
        ]
        for rows in halves
    ]

    for copy in loads[1:2]:
        copy.wait()
    edges[0:LEVELS] = mixing[...]

    @pl.when(lev == 3)
    def _():
        edges[LEVELS] = jnp.zeros((ROWS, COLS), F32)

    edge_copy = remote(edges.at[0], edges.at[LEVELS], {"lev": (lev + 3) % 4}, lev > 0)
    pl.when(lev > 0)(edge_copy.start)

    @pl.when(outer)
    def _():
        for part, rows in enumerate(halves):
            at = level(0)
            sweep(rows, 1.0 + edges[at + down, rows, :], field(0, at, rows), field(1, at, rows))
            outer_copy[part].start()

    for copy in loads[2:5]:
        copy.wait()

    pack_bottom[0:3] = nest_e[ROWS - 3 : ROWS]
    pack_bottom[3:6] = nest_n[ROWS - 3 : ROWS]
    pack_bottom[6:7] = parent_n[ROWS - 1 : ROWS]
    pack_bottom[7:8] = parent_n[ROWS - 1 : ROWS]
    pack_top[0:3] = nest_e[0:3]
    pack_top[3:6] = nest_n[0:3]
    pack_top[6:8] = parent_n[0:2]

    pack_down_copy = remote(pack_bottom, coef_top, {"tile": tile_up}, has_below)
    pl.when(has_below)(pack_down_copy.start)
    pack_up_copy = remote(pack_top, coef_bottom, {"tile": tile_down}, has_above)
    pl.when(has_above)(pack_up_copy.start)
    near_copy = remote(near_out, near_in, {"tile": sibling})
    near_copy.start()

    def relay(hop, *pieces):
        for part in range(PARTS):
            for piece in pieces:
                for way in range(2):
                    hop_copy[hop - 1, piece, way, part].wait_recv()
                    hop_copy[hop, piece, way, part].start()

    def share(hop):
        for part in range(PARTS):
            for way in range(2):
                hop_copy[hop, 4 - hop, way, part].wait_recv()
                side_copy[hop, way, part].start()

    for copy in loads[5:]:
        copy.wait()
    own_tiles = strip_listed[pl.ds(tile, 1), :]
    source_row = iota((TILES, ENTRIES), 0)
    from_source = jnp.where(own_tiles == source_row, 1.0, 0.0)
    own_rank = jnp.sum(
        from_source
        * (jnp.dot(from_source.astype(BF16), upto, preferred_element_type=F32) - 1.0),
        axis=0,
        keepdims=True,
    )
    nest_column = iota((TILES, 1), 0)

    def offsets(source, totals):
        up_total, down_total = totals
        count = jnp.sum(jnp.where(listed == source, 1.0, 0.0), axis=1, keepdims=True)
        gap = chip_gap(nest_column, source)
        up, down_ = way_counts(gap, count)
        up_key, down_key = way_keys(gap, nest_column)
        own_up, own_down = way_keys(chip_gap(tile, source), tile)
        up_here = jnp.sum(jnp.where(up_key < own_up, up, 0.0), axis=0, keepdims=True)
        down_here = jnp.sum(jnp.where(down_key < own_down, down_, 0.0), axis=0, keepdims=True)
        here = own_tiles == source
        return (
            up_total + jnp.where(here, up_here, 0.0),
            down_total + jnp.where(here, down_here, 0.0),
        )

    nothing = jnp.zeros((1, ENTRIES), F32)
    up_start, down_start = lax.fori_loop(0, TILES, offsets, (nothing, nothing))
    own_gap = jnp.where(own_tiles >= 0, chip_gap(tile, own_tiles), -1)
    own_half = jnp.floor(own_rank * 0.5)
    own_odd = own_rank - 2.0 * own_half
    comes_up = ((own_gap >= 1) & (own_gap <= 3)) | ((own_gap == 4) & (own_odd < 0.5))
    place = jnp.where(own_gap == 4, own_half, own_rank) + jnp.where(comes_up, up_start, down_start)
    hops = jnp.where(own_gap >= 1, jnp.where(comes_up, own_gap, CHIPS - own_gap), 0)
    group = jnp.where((own_tiles & 1) == (tile & 1), 0.0, 2.0) + jnp.where(comes_up, 0.0, 1.0)
    targets = strip_target[pl.ds(tile, 1), :]
    targets = jnp.where(own_tiles >= 0, (targets & 7) * ROWS + (targets >> 3), -1)
    lands = jnp.where(targets == iota((NBLK, ENTRIES), 0), 1.0, 0.0).astype(BF16)

    def picks(place, rows):
        return jnp.where(place == iota((rows, ENTRIES), 0).astype(F32), 1.0, 0.0).astype(BF16)

    for hop in range(1, 5):
        size = cap[hop - 1]
        at = jnp.where(hops == hop, group * size + place, -1.0)
        route[hop][...] = onehot_product(lands, picks(at, 4 * size)).astype(BF16)
    at = jnp.where((own_gap == 0) & (own_tiles != tile), own_rank, -1.0)
    route_near[...] = onehot_product(lands, picks(at, SLOTS)).astype(BF16)
    own_blocks = strip_block[pl.ds(tile, 1), :]
    own_blocks = jnp.where(own_tiles == tile, (own_blocks & 7) * ROWS + (own_blocks >> 3), -1)
    route_own[...] = onehot_product(lands, picks(own_blocks.astype(F32), NBLK)).astype(BF16)

    pl.when(lev < 3)(edge_copy.wait_recv)

    @pl.when(inner)
    def _():
        for part, rows in enumerate(halves):
            at = level(0)
            outer_copy[part].wait_recv()
            edge = edges[at + down, rows, :]
            pivot = from_outer[0, rows, :]
            ratio = edge / (pivot + edge)
            sweep(
                rows,
                1.0 + ratio * pivot,
                field(0, at, rows) + ratio * from_outer[1, rows, :],
                field(1, at, rows) + ratio * from_outer[2, rows, :],
            )
            center_copy[part].start()

    relay(2, 0, 1)

    @pl.when(inner)
    def _():
        for part, rows in enumerate(halves):
            center_copy[part].wait_recv()
            at = level(LEVELS - 1)
            edge = edges[at + 1 - down, rows, :]
            pivot = from_center[0, rows, :]
            ratio = edge / (pivot + edge)
            inverse = 1.0 / (message[0, rows, :] + ratio * pivot)
            value0 = (message[1, rows, :] + ratio * from_center[1, rows, :]) * inverse
            value1 = (message[2, rows, :] + ratio * from_center[2, rows, :]) * inverse
            back(rows, value0, value1)
            for copy in inner_copy[part]:
                copy.start()

    @pl.when(has_above)
    def _():
        pack_down_copy.wait_recv()

    @pl.when(has_below)
    def _():
        pack_up_copy.wait_recv()

    @pl.when(tile == 0)
    def _():
        coef_top[...] = jnp.zeros((8, COLS), F32)

    @pl.when(tile == TILES - 1)
    def _():
        coef_bottom[...] = jnp.zeros((8, COLS), F32)

    cell_row = iota((ROWS, COLS), 0)
    for target, e_ref, n_ref, above in (
        (parent_coef, parent_e, parent_n, coef_top[6:7]),
        (nest_coef, nest_e, nest_n, coef_top[5:6]),
    ):
        northward = n_ref[...]
        north_above = jnp.where(cell_row == 0, above, pltpu.roll(northward, 1, 0))
        for which, value in enumerate(coefficients(e_ref[...], northward, north_above)):
            target[which] = value

    relay(2, 2)

    @pl.when(outer)
    def _():
        for part, rows in enumerate(halves):
            for copy in inner_copy[part]:
                copy.wait_recv()
            edge = edges[level(LEVELS - 1) + 1 - down, rows, :]
            inverse = 1.0 / (message[0, rows, :] + edge)
            back(
                rows,
                (message[1, rows, :] + edge * from_inner[0, rows, :]) * inverse,
                (message[2, rows, :] + edge * from_inner[1, rows, :]) * inverse,
            )

    for line in range(LINES):
        rim_out[0, line : line + 1] = solved[line, 0:1, :]
        rim_out[1, line : line + 1] = solved[line, ROWS - 1 : ROWS, :]
    rim_up = remote(rim_out.at[0], rim_in.at[1], {"tile": tile_down}, has_above)
    rim_down = remote(rim_out.at[1], rim_in.at[0], {"tile": tile_up}, has_below)
    pl.when(has_above)(rim_up.start)
    pl.when(has_below)(rim_down.start)

    relay(3, 0, 1)
    share(1)

    near_copy.wait_recv()

    def add_blocks(line, taken):
        for c in range(COLS // LANES):
            start[line, :, LANES * c : LANES * (c + 1)] += taken[ROWS * c : ROWS * (c + 1)]

    def scatter_near(pair, _):
        cells = jnp.concatenate([blocks_of(parent, 2 * pair), blocks_of(parent, 2 * pair + 1)], axis=1)
        near = jnp.concatenate([near_in[2 * pair], near_in[2 * pair + 1]], axis=1)
        taken = routed(route_own[...], cells) + routed(route_near[...], near)
        for side in range(2):
            line = 2 * pair + side
            start[line] = nest[line]
            add_blocks(line, taken[:, LANES * side : LANES * (side + 1)])
        return 0

    lax.fori_loop(0, LINES // 2, scatter_near, 0)

    def scatter(hop, part):
        if part < PARTS:
            for way in range(2):
                side_copy[hop, way, part].wait_recv()

        def one(quad, _):
            for pair in (2 * quad, 2 * quad + 1):
                one_pair(pair)
            return 0

        def one_pair(pair):
            cells = jnp.concatenate(
                [
                    jnp.concatenate([got[hop][g, 2 * pair + side] for g in range(4)], axis=0)
                    for side in range(2)
                ],
                axis=1,
            )
            taken = routed(route[hop][...], cells)
            for side in range(2):
                add_blocks(2 * pair + side, taken[:, LANES * side : LANES * (side + 1)])

        lax.fori_loop(HALF // 4 * part, HALF // 4 * (part + 1), one, 0)

    share(2)
    scatter(1, 0)
    scatter(1, 1)
    relay(4, 0)
    share(3)
    pl.when(has_above)(rim_down.wait_recv)
    pl.when(has_below)(rim_up.wait_recv)

    @pl.when(tile == 0)
    def _():
        rim_in[0] = jnp.zeros((LINES, COLS), F32)

    @pl.when(tile == TILES - 1)
    def _():
        rim_in[1] = jnp.zeros((LINES, COLS), F32)

    def parent_level(at, _):
        results = []
        for which in range(2):
            line = which * LEVELS + at
            results.append(
                relax(
                    halves_of(solved, line),
                    rim_in[0, pl.ds(line, 1), :],
                    rim_in[1, pl.ds(line, 1), :],
                    parent_coef,
                )
            )
            for part in range(2):
                parent_out[line, 8 * part : 8 * part + 8] = results[which][part]
        for part in range(2):
            tag_sum[at, 8 * part : 8 * part + 8] = results[0][part] + results[1][part]
        return 0

    lax.fori_loop(0, LEVELS, parent_level, 0)

    quarter = COLS // 4

    def columns(which):
        return pl.ds(pl.multiple_of(which * quarter, quarter), quarter)

    tag_copy = []
    for d in (1, 2, 3):
        to = (tag + d) % 4
        copy = remote(tag_sum.at[:, :, columns(to)], tag_in.at[d - 1], {"tag": to})
        copy.start()
        tag_copy.append(copy)

    halo_up = []
    halo_down = []
    for part in range(2):
        lines = lines_of(part)
        halo_up.append(
            remote(
                halo_out.at[0, :, lines, :],
                halo_in.at[1, :, lines, :],
                {"tile": tile_down},
                has_above,
            )
        )
        halo_down.append(
            remote(
                halo_out.at[1, :, lines, :],
                halo_in.at[0, :, lines, :],
                {"tile": tile_up},
                has_below,
            )
        )

    def send_halo(part):
        for line in range(HALF * part, HALF * (part + 1)):
            for r in range(NSUB):
                halo_out[0, r, line : line + 1] = start[line, r : r + 1, :]
                at = ROWS - NSUB + r
                halo_out[1, r, line : line + 1] = start[line, at : at + 1, :]
        pl.when(has_above)(halo_up[part].start)
        pl.when(has_below)(halo_down[part].start)

    in_grid = jnp.where(has_below, 1.0, 0.0)

    def e_top(r):
        return coef_top[r : r + 1]

    def n_top(r):
        return coef_top[3 + r : 4 + r]

    def e_bottom(r):
        return coef_bottom[r : r + 1]

    def n_bottom(r):
        return coef_bottom[3 + r : 4 + r]

    def own(ref, r):
        return ref[r : r + 1]

    def receive_halo(part):
        lines = slice(HALF * part, HALF * (part + 1))
        pl.when(has_above)(halo_down[part].wait_recv)
        pl.when(has_below)(halo_up[part].wait_recv)

        @pl.when(tile == 0)
        def _():
            halo_in[0, :, lines] = jnp.zeros((NSUB, HALF, COLS), F32)

        @pl.when(tile == TILES - 1)
        def _():
            halo_in[1, :, lines] = jnp.zeros((NSUB, HALF, COLS), F32)

        far, mid, close = (halo_in[0, r, lines] for r in range(3))
        inner0, inner1 = (halo_out[0, r, lines] for r in range(2))
        second = relax_row(mid, far, close, e_top(1), n_top(1), n_top(0))
        third = relax_row(close, mid, inner0, e_top(2), n_top(2), n_top(1))
        edge_row = relax_row(inner0, close, inner1, own(nest_e, 0), own(nest_n, 0), n_top(2))
        halos[0, 0, lines] = close
        halos[0, 1, lines] = third
        halos[0, 2, lines] = relax_row(third, second, edge_row, e_top(2), n_top(2), n_top(1))
        last = ROWS - 1
        close, mid, far = (halo_in[1, r, lines] for r in range(3))
        inner1, inner0 = (halo_out[1, r, lines] for r in (1, 2))
        second = relax_row(mid, close, far, e_bottom(1), n_bottom(1), n_bottom(0))
        third = in_grid * relax_row(
            close, inner0, mid, e_bottom(0), n_bottom(0), own(nest_n, last)
        )
        edge_row = relax_row(
            inner0, inner1, close, own(nest_e, last), own(nest_n, last), own(nest_n, last - 1)
        )
        halos[1, 0, lines] = close
        halos[1, 1, lines] = third
        halos[1, 2, lines] = in_grid * relax_row(
            third, edge_row, second, e_bottom(0), n_bottom(0), own(nest_n, last)
        )

    scatter(2, 0)
    scatter(2, 1)
    share(4)
    scatter(3, 0)
    scatter(3, 1)
    scatter(4, 0)
    send_halo(0)
    scatter(4, 1)
    send_halo(1)
    receive_halo(0)

    def first_lines(at, _):
        sub_steps(start, [GROUP * at + k for k in range(GROUP)], start, halos, nest_coef)
        return 0

    lax.fori_loop(0, HALF // GROUP, first_lines, 0)
    for copy in tag_copy:
        copy.wait_recv()
    bulk_out[...] = tag_sum[:, :, columns(tag)] + tag_in[0] + tag_in[1] + tag_in[2]
    receive_halo(1)

    for copy, guard in pending:
        if guard is None:
            copy.wait_send()
        else:
            pl.when(guard)(copy.wait_send)


GROUP = 4


def sub_steps(start, lines, result, halos, coef):
    values = [halves_of(start, line) for line in lines]
    for step in range(NSUB):
        for k, line in enumerate(lines):
            values[k] = relax(
                values[k],
                halos[0, step, pl.ds(line, 1), :],
                halos[1, step, pl.ds(line, 1), :],
                coef,
            )
    for k, line in enumerate(lines):
        for part in range(2):
            result[line, 8 * part : 8 * part + 8] = values[k][part]


def finish_kernel(start, halos, coef, parent, bulk, parent_out, nest_out, bulk_out, held, sems):
    ready = pl.ds(0, HALF)
    copies = [
        pltpu.make_async_copy(parent, parent_out, sems.at[0]),
        pltpu.make_async_copy(start.at[ready], nest_out.at[ready], sems.at[1]),
        pltpu.make_async_copy(bulk, bulk_out, sems.at[2]),
    ]
    for copy in copies:
        copy.start()

    def part_copy(at):
        lines = pl.ds(GROUP * at, GROUP)
        return pltpu.make_async_copy(held.at[lines], nest_out.at[lines], sems.at[3 + at])

    def lines_at(at, _):
        sub_steps(start, [GROUP * at + k for k in range(GROUP)], held, halos, coef)
        part_copy(at).start()
        return 0

    lax.fori_loop(HALF // GROUP, LINES // GROUP, lines_at, 0)
    for copy in copies:
        copy.wait()
    for at in range(HALF // GROUP, LINES // GROUP):
        part_copy(at).wait()


VMEM = pl.BlockSpec(memory_space=pltpu.VMEM)
ANY = pl.BlockSpec(memory_space=pl.ANY)
HBM = pl.BlockSpec(memory_space=pltpu.HBM)
SMEM = pl.BlockSpec(memory_space=pltpu.SMEM)


def step_call(cap, collective, arrays):
    first = cap[0]
    grid = (LINES, ROWS, COLS)
    copies = 3 + 1 + 28 * PARTS + 2 + 2 + 4 + 2 + 3 + 4
    shapes = [
        pltpu.VMEM(grid, F32),
        pltpu.VMEM(grid, F32),
        pltpu.VMEM((LEVELS, ROWS, COLS), F32),
        pltpu.VMEM((ROWS, COLS), F32),
        pltpu.VMEM((ROWS, COLS), F32),
        pltpu.VMEM((ROWS, COLS), F32),
        pltpu.VMEM((ROWS, COLS), F32),
        pltpu.VMEM((LEVELS + 1, ROWS, COLS), F32),
        pltpu.VMEM((8, COLS), F32),
        pltpu.VMEM((8, COLS), F32),
        pltpu.VMEM((8, COLS), F32),
        pltpu.VMEM((8, COLS), F32),
        pltpu.VMEM((TILES, ENTRIES), F32),
        pltpu.VMEM((TILES, ENTRIES), F32),
        pltpu.VMEM((2, LINES, first, LANES), F32),
        pltpu.VMEM((LINES, SLOTS, LANES), F32),
        pltpu.VMEM((LINES, SLOTS, LANES), F32),
    ]
    shapes += [pltpu.VMEM((4, LINES, size, LANES), F32) for size in cap]
    shapes += [pltpu.VMEM((NBLK, 4 * size), BF16) for size in cap]
    shapes += [
        pltpu.VMEM((NBLK, SLOTS), BF16),
        pltpu.VMEM((NBLK, NBLK), BF16),
        pltpu.VMEM(grid, F32),
        pltpu.VMEM((LEVELS, ROWS, COLS), F32),
        pltpu.VMEM((3, ROWS, COLS), F32),
        pltpu.VMEM((3, ROWS, COLS), F32),
        pltpu.VMEM((3, ROWS, COLS), F32),
        pltpu.VMEM((2, ROWS, COLS), F32),
        pltpu.VMEM((2, LINES, COLS), F32),
        pltpu.VMEM((2, LINES, COLS), F32),
        pltpu.VMEM((5, ROWS, COLS), F32),
        pltpu.VMEM((LEVELS, ROWS, COLS), F32),
        pltpu.VMEM((3, LEVELS, ROWS, COLS // 4), F32),
        pltpu.VMEM((2, NSUB, LINES, COLS), F32),
        pltpu.VMEM((2, NSUB, LINES, COLS), F32),
        pltpu.SemaphoreType.DMA((copies,)),
        pltpu.SemaphoreType.DMA((copies,)),
        pltpu.SemaphoreType.DMA((7,)),
    ]
    return pl.pallas_call(
        functools.partial(step_kernel, cap),
        out_shape=[
            jax.ShapeDtypeStruct(grid, F32),
            jax.ShapeDtypeStruct((2, NSUB, LINES, COLS), F32),
            jax.ShapeDtypeStruct((5, ROWS, COLS), F32),
            jax.ShapeDtypeStruct(grid, F32),
            jax.ShapeDtypeStruct((LEVELS, ROWS, COLS // 4), F32),
        ],
        in_specs=[HBM] * 7 + [VMEM],
        out_specs=[VMEM] * 5,
        scratch_shapes=shapes,
        compiler_params=pltpu.CompilerParams(
            collective_id=collective, has_side_effects=True, vmem_limit_bytes=56 * 1024 * 1024
        ),
    )(*arrays)


def shards(
    parent_field,
    nest_field,
    parent_mixing,
    parent_eastward,
    parent_northward,
    nest_eastward,
    nest_northward,
    strip_tile,
    strip_block,
    strip_target,
    strip_count,
):
    full_shape = parent_field.shape
    grid = (LINES, ROWS, COLS)
    flag, lists = pl.pallas_call(
        plan_kernel,
        out_shape=[
            jax.ShapeDtypeStruct((1,), jnp.int32),
            jax.ShapeDtypeStruct((3, TILES, ENTRIES), jnp.int32),
        ],
        in_specs=[VMEM, VMEM, VMEM, SMEM],
        out_specs=[SMEM, VMEM],
    )(strip_tile, strip_block, strip_target, strip_count)
    arrays = (
        parent_field.reshape(grid),
        nest_field.reshape(grid),
        parent_mixing,
        parent_eastward,
        parent_northward,
        nest_eastward,
        nest_northward,
        lists,
    )

    def step(size, collective, *operands):
        return step_call(size, collective, operands)

    states = lax.switch(
        flag[0],
        [functools.partial(step, size, at) for at, size in enumerate(SIZES)],
        *arrays,
    )
    parent_adjoint, nest_adjoint, bulk_adjoint = pl.pallas_call(
        finish_kernel,
        out_shape=[
            jax.ShapeDtypeStruct(grid, F32),
            jax.ShapeDtypeStruct(grid, F32),
            jax.ShapeDtypeStruct((LEVELS, ROWS, COLS // 4), F32),
        ],
        in_specs=[VMEM] * 5,
        out_specs=[ANY] * 3,
        scratch_shapes=[
            pltpu.VMEM(grid, F32),
            pltpu.SemaphoreType.DMA((3 + LINES // GROUP,)),
        ],
        compiler_params=pltpu.CompilerParams(vmem_limit_bytes=32 * 1024 * 1024),
    )(*states)
    return parent_adjoint.reshape(full_shape), nest_adjoint.reshape(full_shape), bulk_adjoint


def solution(mesh):
    in_specs = (
        P("tag", "lev", "tile", None),
        P("tag", "lev", "tile", None),
        P("lev", "tile", None),
        P("tile", None),
        P("tile", None),
        P("tile", None),
        P("tile", None),
        P(),
        P(),
        P(),
        P(),
    )
    out_specs = (
        P("tag", "lev", "tile", None),
        P("tag", "lev", "tile", None),
        P("lev", "tile", "tag"),
    )
    return jax.shard_map(shards, mesh=mesh, in_specs=in_specs, out_specs=out_specs, check_vma=False)
```

```python
import functools

import jax
import jax.numpy as jnp
from jax import lax
from jax.experimental import pallas as pl
from jax.experimental.pallas import tpu as pltpu
from jax.sharding import PartitionSpec as P

MESH = pl.DeviceIdType.MESH
F32 = jnp.float32
BF16 = jnp.bfloat16
TILES = 16
CHIPS = 8
SLOTS = 16
LINES = 16
LEVELS = 8
ROWS = 16
COLS = 1024
LANES = 128
NBLK = 128
ENTRIES = 256
NSUB = 3
HALF = LINES // 2
PARTS = 1
SIZES = ((48, 40, 32, 16), (56, 40, 32, 16), (56, 48, 32, 16), (64, 48, 40, 16), (112, 80, 48, 16))


def iota(shape, dim):
    return lax.broadcasted_iota(jnp.int32, shape, dim)


def chip_gap(to_tile, from_tile):
    return ((to_tile >> 1) - (from_tile >> 1)) & (CHIPS - 1)


def way_counts(gap, count):
    half = jnp.floor(count * 0.5)
    up = jnp.where((gap >= 1) & (gap <= 3), count, jnp.where(gap == 4, count - half, 0.0))
    down = jnp.where(gap >= 5, count, jnp.where(gap == 4, half, 0.0))
    return up, down


def way_keys(gap, tile):
    side = tile & 1
    return (4 - gap) * 2 + side, (gap - 4) * 2 + side


def counts_column(count_ref):
    row = iota((TILES, ENTRIES), 0)
    total = jnp.zeros((TILES, ENTRIES), jnp.int32)
    for tile in range(TILES):
        total = jnp.where(row == tile, count_ref[tile], total)
    return total


def plan_kernel(tile_ref, block_ref, target_ref, count_ref, flag_ref, lists_ref):
    live = iota((TILES, ENTRIES), 1) < counts_column(count_ref)
    listed = jnp.where(live, tile_ref[...], -1)
    lists_ref[0] = listed
    lists_ref[1] = block_ref[...]
    lists_ref[2] = target_ref[...]
    lane = iota((TILES, LANES), 1)
    count = jnp.zeros((TILES, LANES), F32)
    for source in range(TILES):
        total = jnp.sum(jnp.where(listed == source, 1.0, 0.0), axis=1, keepdims=True)
        count = jnp.where(lane == source, total, count)
    gap = chip_gap(iota((TILES, LANES), 0), lane)
    up, down = way_counts(gap, count)
    loads = []
    for hop in range(1, 4):
        for load in (jnp.where(gap >= hop, up, 0.0), jnp.where(CHIPS - gap >= hop, down, 0.0)):
            loads.append((hop, jnp.sum(load, axis=0, keepdims=True)))
    over = jnp.zeros((1, LANES), F32)
    for size in SIZES[:-1]:
        excess = functools.reduce(jnp.maximum, [load - size[hop - 1] for hop, load in loads])
        over += jnp.where(excess > 0.5, 1.0, 0.0)
    flag_ref[0] = jnp.max(over).astype(jnp.int32)


def split(value):
    high = value.astype(BF16)
    low = (value - high.astype(F32)).astype(BF16)
    return high, low


def routed(matrix, value):
    high, low = split(value)
    return jnp.dot(matrix, high, preferred_element_type=F32) + jnp.dot(
        matrix, low, preferred_element_type=F32
    )


def onehot_product(left, right):
    return lax.dot_general(left, right, (((1,), (1,)), ((), ())), preferred_element_type=F32)


def blocks_of(ref, line):
    return jnp.concatenate(
        [ref[line, :, LANES * c : LANES * (c + 1)] for c in range(COLS // LANES)], axis=0
    )


def relax(halves, top, bottom, coef):
    row = iota((8, COLS), 0)
    later = [pltpu.roll(x, 1, 0) for x in halves]
    sooner = [pltpu.roll(x, 7, 0) for x in halves]
    above = (jnp.where(row == 0, top, later[0]), jnp.where(row == 0, later[0], later[1]))
    below = (jnp.where(row == 7, sooner[1], sooner[0]), jnp.where(row == 7, bottom, sooner[1]))
    results = []
    for part in range(2):
        x = halves[part]
        rows = slice(8 * part, 8 * part + 8)
        results.append(
            coef[0, rows] * x
            + coef[1, rows] * below[part]
            + coef[2, rows] * above[part]
            + coef[3, rows] * pltpu.roll(x, COLS - 1, 1)
            + coef[4, rows] * pltpu.roll(x, 1, 1)
        )
    return results


def halves_of(ref, line):
    return [ref[line, 0:8, :], ref[line, 8:16, :]]


def coefficients(eastward, northward, north_above):
    col = iota(eastward.shape, 1)
    west = jnp.where(col == 0, 0.0, pltpu.roll(eastward, 1, 1))
    east = jnp.where(col == COLS - 1, 0.0, eastward)
    center = 1.0 - northward - north_above - eastward - west
    return center, northward, north_above, east, west


def relax_row(x, above, below, eastward, northward, north_above):
    wide = x.shape
    center, north, north_up, east, west = coefficients(
        jnp.broadcast_to(eastward, (8, COLS)),
        jnp.broadcast_to(northward, (8, COLS)),
        jnp.broadcast_to(north_above, (8, COLS)),
    )
    center, north, north_up, east, west = (
        jnp.broadcast_to(v[:1], wide) for v in (center, north, north_up, east, west)
    )
    return (
        center * x
        + north * below
        + north_up * above
        + east * pltpu.roll(x, COLS - 1, 1)
        + west * pltpu.roll(x, 1, 1)
    )


def step_kernel(
    cap,
    parent_hbm,
    nest_hbm,
    mixing_hbm,
    parent_e_hbm,
    parent_n_hbm,
    nest_e_hbm,
    nest_n_hbm,
    lists,
    start,
    halos,
    nest_coef,
    parent_out,
    bulk_out,
    parent,
    nest,
    mixing,
    parent_e,
    parent_n,
    nest_e,
    nest_n,
    edges,
    pack_top,
    pack_bottom,
    coef_top,
    coef_bottom,
    slot_of,
    block_of,
    outgoing,
    near_out,
    near_in,
    got1,
    got2,
    got3,
    got4,
    route1,
    route2,
    route3,
    route4,
    route_near,
    route_own,
    solved,
    weight,
    message,
    from_outer,
    from_center,
    from_inner,
    rim_out,
    rim_in,
    parent_coef,
    tag_sum,
    tag_in,
    halo_out,
    halo_in,
    send_sem,
    recv_sem,
    load_sem,
):
    loads = [
        pltpu.make_async_copy(src, dst, load_sem.at[at])
        for at, (src, dst) in enumerate(
            (
                (parent_hbm, parent),
                (mixing_hbm, mixing),
                (nest_e_hbm, nest_e),
                (nest_n_hbm, nest_n),
                (parent_n_hbm, parent_n),
                (parent_e_hbm, parent_e),
                (nest_hbm, nest),
            )
        )
    ]
    loads[0].start()
    strip_listed, strip_block, strip_target = (lists.at[which] for which in range(3))
    got = (None, got1, got2, got3, got4)
    route = (None, route1, route2, route3, route4)
    first = cap[0]
    tile = lax.axis_index("tile")
    lev = lax.axis_index("lev")
    tag = lax.axis_index("tag")
    sibling = tile + 1 - 2 * (tile % 2)
    ring = ((tile + 2) % TILES, (tile + TILES - 2) % TILES)
    tile_up = (tile + 1) % TILES
    tile_down = (tile + TILES - 1) % TILES
    mate = lev + 1 - 2 * (lev % 2)
    across = 3 - lev
    outer = lev % 3 == 0
    inner = lev % 3 != 0
    down = lev // 2

    barrier = pltpu.get_barrier_semaphore()
    peers = [{"tile": t} for t in (tile_up, tile_down) + ring]
    peers += [{"lev": (lev + d) % 4} for d in (1, 2, 3)]
    peers += [{"tag": (tag + d) % 4} for d in (1, 2, 3)]
    for peer in peers:
        pl.semaphore_signal(barrier, inc=1, device_id=peer, device_id_type=MESH)

    used = [0]
    pending = []

    def remote(src, dst, device, guard=None):
        at = used[0]
        used[0] += 1
        copy = pltpu.make_async_remote_copy(
            src_ref=src,
            dst_ref=dst,
            send_sem=send_sem.at[at],
            recv_sem=recv_sem.at[at],
            device_id=device,
            device_id_type=MESH,
        )
        pending.append((copy, guard))
        return copy

    has_above = tile > 0
    has_below = tile < TILES - 1

    row = iota((TILES, ENTRIES), 0)
    listed = strip_listed[...]
    mine = jnp.where(listed == tile, 1.0, 0.0)
    upto = jnp.where(
        iota((ENTRIES, ENTRIES), 0) <= iota((ENTRIES, ENTRIES), 1), 1.0, 0.0
    ).astype(BF16)
    rank = jnp.dot(mine.astype(BF16), upto, preferred_element_type=F32) - 1.0
    count = jnp.broadcast_to(jnp.sum(mine, axis=1, keepdims=True), (TILES, ENTRIES))
    gap = chip_gap(row, tile)
    up_count, down_count = way_counts(gap, count)
    up_key, down_key = way_keys(gap, row)
    up_at = jnp.zeros((TILES, ENTRIES), F32)
    down_at = jnp.zeros((TILES, ENTRIES), F32)
    for other in range(TILES):
        up_at += jnp.where(up_key[other : other + 1] < up_key, up_count[other : other + 1], 0.0)
        down_at += jnp.where(
            down_key[other : other + 1] < down_key, down_count[other : other + 1], 0.0
        )
    half = jnp.floor(rank * 0.5)
    odd = rank - 2.0 * half
    goes_up = ((gap >= 1) & (gap <= 3)) | ((gap == 4) & (odd < 0.5))
    goes_down = (gap >= 5) | ((gap == 4) & (odd > 0.5))
    in_row = jnp.where(gap == 4, half, rank)
    slot = jnp.where(
        goes_up,
        up_at + in_row,
        jnp.where(
            goes_down,
            first + down_at + in_row,
            jnp.where((gap == 0) & (row != tile), 2 * first + rank, -1.0),
        ),
    )
    slot_of[...] = jnp.where(mine > 0.5, slot, -1.0)
    blocks = strip_block[...]
    block_of[...] = ((blocks & 7) * ROWS + (blocks >> 3) + 1).astype(F32)

    def gather_matrix(begin, size):
        wanted = (iota((size, ENTRIES), 0) + begin).astype(F32)

        total = jnp.zeros((size, ENTRIES), F32)
        for nest_tile in range(TILES):
            at = slice(nest_tile, nest_tile + 1)
            total = jnp.where(slot_of[at, :] == wanted, block_of[at, :], total)
        index = jnp.sum(total, axis=1, keepdims=True) - 1.0
        return jnp.where(index == iota((size, NBLK), 1).astype(F32), 1.0, 0.0).astype(BF16)

    gather = jnp.concatenate(
        [gather_matrix(0, first), gather_matrix(first, first), gather_matrix(2 * first, SLOTS)],
        axis=0,
    )

    def lines_of(part):
        return pl.ds(HALF * part, HALF)

    def pack(quad, _):
        for pair in (2 * quad, 2 * quad + 1):
            pack_pair(pair)
        return 0

    def pack_pair(pair):
        cells = jnp.concatenate([blocks_of(parent, 2 * pair), blocks_of(parent, 2 * pair + 1)], axis=1)
        taken = routed(gather, cells)
        for side in range(2):
            lanes = slice(LANES * side, LANES * (side + 1))
            outgoing[0, 2 * pair + side] = taken[:first, lanes]
            outgoing[1, 2 * pair + side] = taken[first : 2 * first, lanes]
            near_out[2 * pair + side] = taken[2 * first :, lanes]

    cuts = (0, cap[3], cap[2], cap[1], cap[0])
    hop_copy = {}
    side_copy = {}
    for part in range(PARTS):
        lines = pl.ds(LINES // PARTS * part, LINES // PARTS)
        for hop in range(1, 5):
            src = outgoing if hop == 1 else got[hop - 1]
            for way in range(2):
                for piece in range(5 - hop):
                    slots = pl.ds(cuts[piece], cuts[piece + 1] - cuts[piece])
                    hop_copy[hop, piece, way, part] = remote(
                        src.at[way, lines, slots, :],
                        got[hop].at[way, lines, slots, :],
                        {"tile": ring[way]},
                    )
                side_copy[hop, way, part] = remote(
                    got[hop].at[way, lines], got[hop].at[2 + way, lines], {"tile": sibling}
                )

    def send(part):
        for piece in range(4):
            for way in range(2):
                hop_copy[1, piece, way, part].start()

    loads[0].wait()
    for copy in loads[1:]:
        copy.start()
    for part in range(PARTS):
        for quad in range(HALF // 2 // PARTS * part, HALF // 2 // PARTS * (part + 1)):
            pack(quad, 0)
        if part == 0:
            pl.semaphore_wait(barrier, len(peers))
        send(part)

    def level(step):
        return step + down * (LEVELS - 1 - 2 * step)

    def field(which, at, rows):
        return parent[which * LEVELS + at, rows, :]

    def sweep(rows, pivot, value0, value1):
        for step in range(LEVELS - 1):
            at = level(step)
            edge = edges[at + 1 - down, rows, :]
            inverse = 1.0 / (pivot + edge)
            ratio = edge * inverse
            carry0 = value0 * inverse
            carry1 = value1 * inverse
            solved[at, rows, :] = carry0
            solved[LEVELS + at, rows, :] = carry1
            weight[at, rows, :] = ratio
            follow = level(step + 1)
            pivot = 1.0 + ratio * pivot
            value0 = field(0, follow, rows) + edge * carry0
            value1 = field(1, follow, rows) + edge * carry1
        message[0, rows, :] = pivot
        message[1, rows, :] = value0
        message[2, rows, :] = value1

    def back(rows, value0, value1):
        at = level(LEVELS - 1)
        solved[at, rows, :] = value0
        solved[LEVELS + at, rows, :] = value1
        for step in range(LEVELS - 2, -1, -1):
            at = level(step)
            ratio = weight[at, rows, :]
            value0 = solved[at, rows, :] + ratio * value0
            value1 = solved[LEVELS + at, rows, :] + ratio * value1
            solved[at, rows, :] = value0
            solved[LEVELS + at, rows, :] = value1

    halves = [pl.ds(0, 8), pl.ds(8, 8)]
    near_level = level(0)
    outer_copy = [
        remote(message.at[:, rows, :], from_outer.at[:, rows, :], {"lev": mate}, outer)
        for rows in halves
    ]
    center_copy = [
        remote(message.at[:, rows, :], from_center.at[:, rows, :], {"lev": across}, inner)
        for rows in halves
    ]
    inner_copy = [
        [
            remote(
                solved.at[which * LEVELS + near_level, rows, :],
                from_inner.at[which, rows, :],
                {"lev": mate},
                inner,
            )
            for which in range(2)
        ]
        for rows in halves
    ]

    for copy in loads[1:2]:
        copy.wait()
    edges[0:LEVELS] = mixing[...]

    @pl.when(lev == 3)
    def _():
        edges[LEVELS] = jnp.zeros((ROWS, COLS), F32)

    edge_copy = remote(edges.at[0], edges.at[LEVELS], {"lev": (lev + 3) % 4}, lev > 0)
    pl.when(lev > 0)(edge_copy.start)

    @pl.when(outer)
    def _():
        for part, rows in enumerate(halves):
            at = level(0)
            sweep(rows, 1.0 + edges[at + down, rows, :], field(0, at, rows), field(1, at, rows))
            outer_copy[part].start()

    for copy in loads[2:5]:
        copy.wait()

    pack_bottom[0:3] = nest_e[ROWS - 3 : ROWS]
    pack_bottom[3:6] = nest_n[ROWS - 3 : ROWS]
    pack_bottom[6:7] = parent_n[ROWS - 1 : ROWS]
    pack_bottom[7:8] = parent_n[ROWS - 1 : ROWS]
    pack_top[0:3] = nest_e[0:3]
    pack_top[3:6] = nest_n[0:3]
    pack_top[6:8] = parent_n[0:2]

    pack_down_copy = remote(pack_bottom, coef_top, {"tile": tile_up}, has_below)
    pl.when(has_below)(pack_down_copy.start)
    pack_up_copy = remote(pack_top, coef_bottom, {"tile": tile_down}, has_above)
    pl.when(has_above)(pack_up_copy.start)
    near_copy = remote(near_out, near_in, {"tile": sibling})
    near_copy.start()

    def relay(hop, *pieces):
        for part in range(PARTS):
            for piece in pieces:
                for way in range(2):
                    hop_copy[hop - 1, piece, way, part].wait_recv()
                    hop_copy[hop, piece, way, part].start()

    def share(hop):
        for part in range(PARTS):
            for way in range(2):
                hop_copy[hop, 4 - hop, way, part].wait_recv()
                side_copy[hop, way, part].start()

    for copy in loads[5:]:
        copy.wait()
    own_tiles = strip_listed[pl.ds(tile, 1), :]
    source_row = iota((TILES, ENTRIES), 0)
    from_source = jnp.where(own_tiles == source_row, 1.0, 0.0)
    own_rank = jnp.sum(
        from_source
        * (jnp.dot(from_source.astype(BF16), upto, preferred_element_type=F32) - 1.0),
        axis=0,
        keepdims=True,
    )
    nest_column = iota((TILES, 1), 0)

    def offsets(source, totals):
        up_total, down_total = totals
        count = jnp.sum(jnp.where(listed == source, 1.0, 0.0), axis=1, keepdims=True)
        gap = chip_gap(nest_column, source)
        up, down_ = way_counts(gap, count)
        up_key, down_key = way_keys(gap, nest_column)
        own_up, own_down = way_keys(chip_gap(tile, source), tile)
        up_here = jnp.sum(jnp.where(up_key < own_up, up, 0.0), axis=0, keepdims=True)
        down_here = jnp.sum(jnp.where(down_key < own_down, down_, 0.0), axis=0, keepdims=True)
        here = own_tiles == source
        return (
            up_total + jnp.where(here, up_here, 0.0),
            down_total + jnp.where(here, down_here, 0.0),
        )

    nothing = jnp.zeros((1, ENTRIES), F32)
    up_start, down_start = lax.fori_loop(0, TILES, offsets, (nothing, nothing))
    own_gap = jnp.where(own_tiles >= 0, chip_gap(tile, own_tiles), -1)
    own_half = jnp.floor(own_rank * 0.5)
    own_odd = own_rank - 2.0 * own_half
    comes_up = ((own_gap >= 1) & (own_gap <= 3)) | ((own_gap == 4) & (own_odd < 0.5))
    place = jnp.where(own_gap == 4, own_half, own_rank) + jnp.where(comes_up, up_start, down_start)
    hops = jnp.where(own_gap >= 1, jnp.where(comes_up, own_gap, CHIPS - own_gap), 0)
    group = jnp.where((own_tiles & 1) == (tile & 1), 0.0, 2.0) + jnp.where(comes_up, 0.0, 1.0)
    targets = strip_target[pl.ds(tile, 1), :]
    targets = jnp.where(own_tiles >= 0, (targets & 7) * ROWS + (targets >> 3), -1)
    lands = jnp.where(targets == iota((NBLK, ENTRIES), 0), 1.0, 0.0).astype(BF16)

    def picks(place, rows):
        return jnp.where(place == iota((rows, ENTRIES), 0).astype(F32), 1.0, 0.0).astype(BF16)

    for hop in range(1, 5):
        size = cap[hop - 1]
        at = jnp.where(hops == hop, group * size + place, -1.0)
        route[hop][...] = onehot_product(lands, picks(at, 4 * size)).astype(BF16)
    at = jnp.where((own_gap == 0) & (own_tiles != tile), own_rank, -1.0)
    route_near[...] = onehot_product(lands, picks(at, SLOTS)).astype(BF16)
    own_blocks = strip_block[pl.ds(tile, 1), :]
    own_blocks = jnp.where(own_tiles == tile, (own_blocks & 7) * ROWS + (own_blocks >> 3), -1)
    route_own[...] = onehot_product(lands, picks(own_blocks.astype(F32), NBLK)).astype(BF16)

    pl.when(lev < 3)(edge_copy.wait_recv)

    @pl.when(inner)
    def _():
        for part, rows in enumerate(halves):
            at = level(0)
            outer_copy[part].wait_recv()
            edge = edges[at + down, rows, :]
            pivot = from_outer[0, rows, :]
            ratio = edge / (pivot + edge)
            sweep(
                rows,
                1.0 + ratio * pivot,
                field(0, at, rows) + ratio * from_outer[1, rows, :],
                field(1, at, rows) + ratio * from_outer[2, rows, :],
            )
            center_copy[part].start()

    relay(2, 0, 1)

    @pl.when(inner)
    def _():
        for part, rows in enumerate(halves):
            center_copy[part].wait_recv()
            at = level(LEVELS - 1)
            edge = edges[at + 1 - down, rows, :]
            pivot = from_center[0, rows, :]
            ratio = edge / (pivot + edge)
            inverse = 1.0 / (message[0, rows, :] + ratio * pivot)
            value0 = (message[1, rows, :] + ratio * from_center[1, rows, :]) * inverse
            value1 = (message[2, rows, :] + ratio * from_center[2, rows, :]) * inverse
            back(rows, value0, value1)
            for copy in inner_copy[part]:
                copy.start()

    @pl.when(has_above)
    def _():
        pack_down_copy.wait_recv()

    @pl.when(has_below)
    def _():
        pack_up_copy.wait_recv()

    @pl.when(tile == 0)
    def _():
        coef_top[...] = jnp.zeros((8, COLS), F32)

    @pl.when(tile == TILES - 1)
    def _():
        coef_bottom[...] = jnp.zeros((8, COLS), F32)

    cell_row = iota((ROWS, COLS), 0)
    for target, e_ref, n_ref, above in (
        (parent_coef, parent_e, parent_n, coef_top[6:7]),
        (nest_coef, nest_e, nest_n, coef_top[5:6]),
    ):
        northward = n_ref[...]
        north_above = jnp.where(cell_row == 0, above, pltpu.roll(northward, 1, 0))
        for which, value in enumerate(coefficients(e_ref[...], northward, north_above)):
            target[which] = value

    near_copy.wait_recv()

    def add_blocks(line, taken):
        for c in range(COLS // LANES):
            start[line, :, LANES * c : LANES * (c + 1)] += taken[ROWS * c : ROWS * (c + 1)]

    def scatter_near(pair, _):
        cells = jnp.concatenate([blocks_of(parent, 2 * pair), blocks_of(parent, 2 * pair + 1)], axis=1)
        near = jnp.concatenate([near_in[2 * pair], near_in[2 * pair + 1]], axis=1)
        taken = routed(route_own[...], cells) + routed(route_near[...], near)
        for side in range(2):
            line = 2 * pair + side
            start[line] = nest[line]
            add_blocks(line, taken[:, LANES * side : LANES * (side + 1)])
        return 0

    lax.fori_loop(0, LINES // 2, scatter_near, 0)

    relay(2, 2)

    @pl.when(outer)
    def _():
        for part, rows in enumerate(halves):
            for copy in inner_copy[part]:
                copy.wait_recv()
            edge = edges[level(LEVELS - 1) + 1 - down, rows, :]
            inverse = 1.0 / (message[0, rows, :] + edge)
            back(
                rows,
                (message[1, rows, :] + edge * from_inner[0, rows, :]) * inverse,
                (message[2, rows, :] + edge * from_inner[1, rows, :]) * inverse,
            )

    for line in range(LINES):
        rim_out[0, line : line + 1] = solved[line, 0:1, :]
        rim_out[1, line : line + 1] = solved[line, ROWS - 1 : ROWS, :]
    rim_up = remote(rim_out.at[0], rim_in.at[1], {"tile": tile_down}, has_above)
    rim_down = remote(rim_out.at[1], rim_in.at[0], {"tile": tile_up}, has_below)
    pl.when(has_above)(rim_up.start)
    pl.when(has_below)(rim_down.start)

    relay(3, 0, 1)
    share(1)

    def scatter(hop, part):
        if part < PARTS:
            for way in range(2):
                side_copy[hop, way, part].wait_recv()

        def one(quad, _):
            for pair in (2 * quad, 2 * quad + 1):
                one_pair(pair)
            return 0

        def one_pair(pair):
            cells = jnp.concatenate(
                [
                    jnp.concatenate([got[hop][g, 2 * pair + side] for g in range(4)], axis=0)
                    for side in range(2)
                ],
                axis=1,
            )
            taken = routed(route[hop][...], cells)
            for side in range(2):
                add_blocks(2 * pair + side, taken[:, LANES * side : LANES * (side + 1)])

        lax.fori_loop(HALF // 4 * part, HALF // 4 * (part + 1), one, 0)

    share(2)
    scatter(1, 0)
    scatter(1, 1)
    relay(4, 0)
    share(3)
    pl.when(has_above)(rim_down.wait_recv)
    pl.when(has_below)(rim_up.wait_recv)

    @pl.when(tile == 0)
    def _():
        rim_in[0] = jnp.zeros((LINES, COLS), F32)

    @pl.when(tile == TILES - 1)
    def _():
        rim_in[1] = jnp.zeros((LINES, COLS), F32)

    def parent_level(at, _):
        results = []
        for which in range(2):
            line = which * LEVELS + at
            results.append(
                relax(
                    halves_of(solved, line),
                    rim_in[0, pl.ds(line, 1), :],
                    rim_in[1, pl.ds(line, 1), :],
                    parent_coef,
                )
            )
            for part in range(2):
                parent_out[line, 8 * part : 8 * part + 8] = results[which][part]
        for part in range(2):
            tag_sum[at, 8 * part : 8 * part + 8] = results[0][part] + results[1][part]
        return 0

    lax.fori_loop(0, LEVELS, parent_level, 0)

    quarter = COLS // 4

    def columns(which):
        return pl.ds(pl.multiple_of(which * quarter, quarter), quarter)

    tag_copy = []
    for d in (1, 2, 3):
        to = (tag + d) % 4
        copy = remote(tag_sum.at[:, :, columns(to)], tag_in.at[d - 1], {"tag": to})
        copy.start()
        tag_copy.append(copy)

    halo_up = []
    halo_down = []
    for part in range(2):
        lines = lines_of(part)
        halo_up.append(
            remote(
                halo_out.at[0, :, lines, :],
                halo_in.at[1, :, lines, :],
                {"tile": tile_down},
                has_above,
            )
        )
        halo_down.append(
            remote(
                halo_out.at[1, :, lines, :],
                halo_in.at[0, :, lines, :],
                {"tile": tile_up},
                has_below,
            )
        )

    def send_halo(part):
        for line in range(HALF * part, HALF * (part + 1)):
            for r in range(NSUB):
                halo_out[0, r, line : line + 1] = start[line, r : r + 1, :]
                at = ROWS - NSUB + r
                halo_out[1, r, line : line + 1] = start[line, at : at + 1, :]
        pl.when(has_above)(halo_up[part].start)
        pl.when(has_below)(halo_down[part].start)

    in_grid = jnp.where(has_below, 1.0, 0.0)

    def e_top(r):
        return coef_top[r : r + 1]

    def n_top(r):
        return coef_top[3 + r : 4 + r]

    def e_bottom(r):
        return coef_bottom[r : r + 1]

    def n_bottom(r):
        return coef_bottom[3 + r : 4 + r]

    def own(ref, r):
        return ref[r : r + 1]

    def receive_halo(part):
        lines = slice(HALF * part, HALF * (part + 1))
        pl.when(has_above)(halo_down[part].wait_recv)
        pl.when(has_below)(halo_up[part].wait_recv)

        @pl.when(tile == 0)
        def _():
            halo_in[0, :, lines] = jnp.zeros((NSUB, HALF, COLS), F32)

        @pl.when(tile == TILES - 1)
        def _():
            halo_in[1, :, lines] = jnp.zeros((NSUB, HALF, COLS), F32)

        far, mid, close = (halo_in[0, r, lines] for r in range(3))
        inner0, inner1 = (halo_out[0, r, lines] for r in range(2))
        second = relax_row(mid, far, close, e_top(1), n_top(1), n_top(0))
        third = relax_row(close, mid, inner0, e_top(2), n_top(2), n_top(1))
        edge_row = relax_row(inner0, close, inner1, own(nest_e, 0), own(nest_n, 0), n_top(2))
        halos[0, 0, lines] = close
        halos[0, 1, lines] = third
        halos[0, 2, lines] = relax_row(third, second, edge_row, e_top(2), n_top(2), n_top(1))
        last = ROWS - 1
        close, mid, far = (halo_in[1, r, lines] for r in range(3))
        inner1, inner0 = (halo_out[1, r, lines] for r in (1, 2))
        second = relax_row(mid, close, far, e_bottom(1), n_bottom(1), n_bottom(0))
        third = in_grid * relax_row(
            close, inner0, mid, e_bottom(0), n_bottom(0), own(nest_n, last)
        )
        edge_row = relax_row(
            inner0, inner1, close, own(nest_e, last), own(nest_n, last), own(nest_n, last - 1)
        )
        halos[1, 0, lines] = close
        halos[1, 1, lines] = third
        halos[1, 2, lines] = in_grid * relax_row(
            third, edge_row, second, e_bottom(0), n_bottom(0), own(nest_n, last)
        )

    scatter(2, 0)
    scatter(2, 1)
    share(4)
    scatter(3, 0)
    scatter(3, 1)
    scatter(4, 0)
    send_halo(0)
    scatter(4, 1)
    send_halo(1)
    receive_halo(0)

    def first_lines(at, _):
        sub_steps(start, [GROUP * at + k for k in range(GROUP)], start, halos, nest_coef)
        return 0

    lax.fori_loop(0, HALF // GROUP, first_lines, 0)
    for copy in tag_copy:
        copy.wait_recv()
    bulk_out[...] = tag_sum[:, :, columns(tag)] + tag_in[0] + tag_in[1] + tag_in[2]
    receive_halo(1)

    for copy, guard in pending:
        if guard is None:
            copy.wait_send()
        else:
            pl.when(guard)(copy.wait_send)


GROUP = 8


def sub_steps(start, lines, result, halos, coef):
    values = [halves_of(start, line) for line in lines]
    for step in range(NSUB):
        for k, line in enumerate(lines):
            values[k] = relax(
                values[k],
                halos[0, step, pl.ds(line, 1), :],
                halos[1, step, pl.ds(line, 1), :],
                coef,
            )
    for k, line in enumerate(lines):
        for part in range(2):
            result[line, 8 * part : 8 * part + 8] = values[k][part]


def finish_kernel(start, halos, coef, parent, bulk, parent_out, nest_out, bulk_out, held, sems):
    ready = pl.ds(0, HALF)
    copies = [
        pltpu.make_async_copy(parent, parent_out, sems.at[0]),
        pltpu.make_async_copy(start.at[ready], nest_out.at[ready], sems.at[1]),
        pltpu.make_async_copy(bulk, bulk_out, sems.at[2]),
    ]
    for copy in copies:
        copy.start()

    def part_copy(at):
        lines = pl.ds(GROUP * at, GROUP)
        return pltpu.make_async_copy(held.at[lines], nest_out.at[lines], sems.at[3 + at])

    def lines_at(at, _):
        sub_steps(start, [GROUP * at + k for k in range(GROUP)], held, halos, coef)
        part_copy(at).start()
        return 0

    lax.fori_loop(HALF // GROUP, LINES // GROUP, lines_at, 0)
    for copy in copies:
        copy.wait()
    for at in range(HALF // GROUP, LINES // GROUP):
        part_copy(at).wait()


VMEM = pl.BlockSpec(memory_space=pltpu.VMEM)
ANY = pl.BlockSpec(memory_space=pl.ANY)
HBM = pl.BlockSpec(memory_space=pltpu.HBM)
SMEM = pl.BlockSpec(memory_space=pltpu.SMEM)


def step_call(cap, collective, arrays):
    first = cap[0]
    grid = (LINES, ROWS, COLS)
    copies = 3 + 1 + 28 * PARTS + 2 + 2 + 4 + 2 + 3 + 4
    shapes = [
        pltpu.VMEM(grid, F32),
        pltpu.VMEM(grid, F32),
        pltpu.VMEM((LEVELS, ROWS, COLS), F32),
        pltpu.VMEM((ROWS, COLS), F32),
        pltpu.VMEM((ROWS, COLS), F32),
        pltpu.VMEM((ROWS, COLS), F32),
        pltpu.VMEM((ROWS, COLS), F32),
        pltpu.VMEM((LEVELS + 1, ROWS, COLS), F32),
        pltpu.VMEM((8, COLS), F32),
        pltpu.VMEM((8, COLS), F32),
        pltpu.VMEM((8, COLS), F32),
        pltpu.VMEM((8, COLS), F32),
        pltpu.VMEM((TILES, ENTRIES), F32),
        pltpu.VMEM((TILES, ENTRIES), F32),
        pltpu.VMEM((2, LINES, first, LANES), F32),
        pltpu.VMEM((LINES, SLOTS, LANES), F32),
        pltpu.VMEM((LINES, SLOTS, LANES), F32),
    ]
    shapes += [pltpu.VMEM((4, LINES, size, LANES), F32) for size in cap]
    shapes += [pltpu.VMEM((NBLK, 4 * size), BF16) for size in cap]
    shapes += [
        pltpu.VMEM((NBLK, SLOTS), BF16),
        pltpu.VMEM((NBLK, NBLK), BF16),
        pltpu.VMEM(grid, F32),
        pltpu.VMEM((LEVELS, ROWS, COLS), F32),
        pltpu.VMEM((3, ROWS, COLS), F32),
        pltpu.VMEM((3, ROWS, COLS), F32),
        pltpu.VMEM((3, ROWS, COLS), F32),
        pltpu.VMEM((2, ROWS, COLS), F32),
        pltpu.VMEM((2, LINES, COLS), F32),
        pltpu.VMEM((2, LINES, COLS), F32),
        pltpu.VMEM((5, ROWS, COLS), F32),
        pltpu.VMEM((LEVELS, ROWS, COLS), F32),
        pltpu.VMEM((3, LEVELS, ROWS, COLS // 4), F32),
        pltpu.VMEM((2, NSUB, LINES, COLS), F32),
        pltpu.VMEM((2, NSUB, LINES, COLS), F32),
        pltpu.SemaphoreType.DMA((copies,)),
        pltpu.SemaphoreType.DMA((copies,)),
        pltpu.SemaphoreType.DMA((7,)),
    ]
    return pl.pallas_call(
        functools.partial(step_kernel, cap),
        out_shape=[
            jax.ShapeDtypeStruct(grid, F32),
            jax.ShapeDtypeStruct((2, NSUB, LINES, COLS), F32),
            jax.ShapeDtypeStruct((5, ROWS, COLS), F32),
            jax.ShapeDtypeStruct(grid, F32),
            jax.ShapeDtypeStruct((LEVELS, ROWS, COLS // 4), F32),
        ],
        in_specs=[HBM] * 7 + [VMEM],
        out_specs=[VMEM] * 5,
        scratch_shapes=shapes,
        compiler_params=pltpu.CompilerParams(
            collective_id=collective, has_side_effects=True, vmem_limit_bytes=56 * 1024 * 1024
        ),
    )(*arrays)


def shards(
    parent_field,
    nest_field,
    parent_mixing,
    parent_eastward,
    parent_northward,
    nest_eastward,
    nest_northward,
    strip_tile,
    strip_block,
    strip_target,
    strip_count,
):
    full_shape = parent_field.shape
    grid = (LINES, ROWS, COLS)
    flag, lists = pl.pallas_call(
        plan_kernel,
        out_shape=[
            jax.ShapeDtypeStruct((1,), jnp.int32),
            jax.ShapeDtypeStruct((3, TILES, ENTRIES), jnp.int32),
        ],
        in_specs=[VMEM, VMEM, VMEM, SMEM],
        out_specs=[SMEM, VMEM],
    )(strip_tile, strip_block, strip_target, strip_count)
    arrays = (
        parent_field.reshape(grid),
        nest_field.reshape(grid),
        parent_mixing,
        parent_eastward,
        parent_northward,
        nest_eastward,
        nest_northward,
        lists,
    )

    def step(size, collective, *operands):
        return step_call(size, collective, operands)

    states = lax.switch(
        flag[0],
        [functools.partial(step, size, at) for at, size in enumerate(SIZES)],
        *arrays,
    )
    parent_adjoint, nest_adjoint, bulk_adjoint = pl.pallas_call(
        finish_kernel,
        out_shape=[
            jax.ShapeDtypeStruct(grid, F32),
            jax.ShapeDtypeStruct(grid, F32),
            jax.ShapeDtypeStruct((LEVELS, ROWS, COLS // 4), F32),
        ],
        in_specs=[VMEM] * 5,
        out_specs=[ANY] * 3,
        scratch_shapes=[
            pltpu.VMEM(grid, F32),
            pltpu.SemaphoreType.DMA((3 + LINES // GROUP,)),
        ],
        compiler_params=pltpu.CompilerParams(vmem_limit_bytes=32 * 1024 * 1024),
    )(*states)
    return parent_adjoint.reshape(full_shape), nest_adjoint.reshape(full_shape), bulk_adjoint


def solution(mesh):
    in_specs = (
        P("tag", "lev", "tile", None),
        P("tag", "lev", "tile", None),
        P("lev", "tile", None),
        P("tile", None),
        P("tile", None),
        P("tile", None),
        P("tile", None),
        P(),
        P(),
        P(),
        P(),
    )
    out_specs = (
        P("tag", "lev", "tile", None),
        P("tag", "lev", "tile", None),
        P("lev", "tile", "tag"),
    )
    return jax.shard_map(shards, mesh=mesh, in_specs=in_specs, out_specs=out_specs, check_vma=False)
```
